32 devices in a mesh: narrow: 4 (over x, core), wide: 8 (over z, y).
Axes of the slice: x: 2, y: 2, z: 4, core: 2. Of those that a mesh axis runs over, the one named last changes fastest.
Arguments:
- tokens: bfloat16 [16384, 1024], P(('narrow', 'wide')), may hold values from -6 to 6
- lengths: int32 [32], P(('narrow', 'wide')), may hold values from 64 to 512, as said below
- buckets: int32 [512], replicated, may hold values from 0 to 31, as said below
- ln1_gain: bfloat16 [1024], P('wide'), may hold values from 0.099609375 to 1.8984375
- ln1_bias: bfloat16 [1024], P('wide'), may hold values from -3 to 3
- w_qkv: bfloat16 [1024, 3072], P('wide'), may hold values from -0.1875 to 0.1875
- rel_table: bfloat16 [512], P('wide'), may hold values from -4 to 4
- w_out: bfloat16 [1024, 1024], P('wide'), may hold values from -2 to 2
- ln2_gain: bfloat16 [1024], P('wide'), may hold values from 0.099609375 to 1.8984375
- ln2_bias: bfloat16 [1024], P('wide'), may hold values from -3 to 3
- w_up: bfloat16 [1024, 4096], P('wide'), may hold values from -0.1875 to 0.1875
- w_down: bfloat16 [4096, 1024], P('wide'), may hold values from -0.09375 to 0.09375
- cotangent: bfloat16 [16384, 1024], P(('narrow', 'wide')), may hold values from -6 to 6
Outputs:
- output: bfloat16 [16384, 1024], P(('narrow', 'wide'))
- grad_tokens: float32 [16384, 1024], P(('narrow', 'wide'))
- grad_ln1_gain: float32 [1024], P('wide')
- grad_ln1_bias: float32 [1024], P('wide')
- grad_w_qkv: float32 [1024, 3072], P('wide')
- grad_rel_table: float32 [512], P('wide')
- grad_w_out: float32 [1024, 1024], P('wide')
- grad_ln2_gain: float32 [1024], P('wide')
- grad_ln2_bias: float32 [1024], P('wide')
- grad_w_up: float32 [1024, 4096], P('wide')
- grad_w_down: float32 [4096, 1024], P('wide')
The draws below stay inside these ranges and needn't reach their ends.
Inputs may be any that keep to these rules, and one draw needn't show every extreme that they name: `lengths`: in each aligned group of eight sequences exactly one has length 512. `buckets`: never falls as the distance grows; 0 at distance 0; every bucket occurs.
All inputs are finite; a program needn't handle non-finite values.
Results may differ from the reference program's by a relative error of at most 0.015.
Values may be sent and summed in bfloat16 or wider, within the bound.
No kernel may reach another device: no remote copies, remote signals or barrier semaphores. Data moves between devices by JAX's collectives and lax.ppermute only.
A program may use at most 320 MiB of HBM per device.

```python
import jax
import jax.numpy as jnp
from jax import lax

D = 1024
HEADS = 16
HEAD_DIM = 64
FF = 4096
BUCKETS = 32
SLOT = 512
SEQS = 32
TOKENS = 16384


def draw_lengths(key, part):
    key = jax.random.fold_in(key, 11)
    first_key, second_key = jax.random.split(key)
    base = jax.random.randint(first_key, (SEQS,), SLOT // 8, SLOT * 13 // 16, dtype=jnp.int32)
    offset = jax.random.randint(second_key, (), 0, 8, dtype=jnp.int32)
    longest = jnp.arange(SEQS, dtype=jnp.int32) % 8 == offset
    return jnp.where(longest, SLOT, base).astype(jnp.int32)


def draw_buckets(key, part):
    key = jax.random.fold_in(key, 23)
    order = jax.random.permutation(key, SLOT - 1).astype(jnp.int32) + 1
    bounds = order[:BUCKETS - 1]
    distance = jnp.arange(SLOT, dtype=jnp.int32)
    return jnp.sum((bounds[None, :] <= distance[:, None]).astype(jnp.int32), axis=1).astype(jnp.int32)


def raised(entries, own_key, source, target, shards_of, factor):
    def block_of(axis_at):
        return (jnp.arange(entries.shape[axis_at]) // (entries.shape[axis_at] // shards_of)).reshape((-1,) + (1,) * (entries.ndim - 1 - axis_at))

    near = jax.random.permutation(own_key, shards_of)[block_of(target)]
    second = (block_of(target) + shards_of // 2) % shards_of
    return jnp.where((block_of(source) == near) | (block_of(source) == second), factor * entries, entries)


def level_of(own_key, extent, shards, smallest, high):
    def one(axis_at, shards_of):
        draws = jax.random.uniform(jax.random.fold_in(jax.random.fold_in(own_key, 6), axis_at), (shards_of,), jnp.float32, smallest / len(shards), high / len(shards))
        return jnp.repeat(jnp.exp(draws), extent[axis_at] // shards_of).reshape((-1,) + (1,) * (len(extent) - axis_at - 1))

    factor_of = one(*shards[0])
    for cut in shards[1:]:
        factor_of = factor_of * one(*cut)
    return factor_of


def gaussian(rng, extent, width, limit, pieces=(), held_as=jnp.bfloat16):
    factor_of = level_of(rng, extent, pieces, -0.22, 0.18) if pieces else 1.0
    values = jax.random.normal(rng, extent, jnp.float32) * width * factor_of
    return jnp.minimum(jnp.maximum(values, -limit), limit).astype(held_as)


def noise_with(key, shape, width, limit, cuts, heavy, kind=jnp.bfloat16):
    array = width * jax.random.normal(key, shape, jnp.float32)
    if cuts:
        array = array * level_of(key, shape, cuts, -0.22, 0.18)
    return jnp.clip(raised(array, jax.random.fold_in(key, 3), *heavy), -limit, limit).astype(kind)


def setup_inputs(seed: int = 0) -> dict:
    keys = jax.random.split(jax.random.key(seed), 14)
    return {
        "tokens": noise_with(keys[0], (TOKENS, D), 1.0, 6.0, ((0, 32),), (0, 1, 32, 2.75)),
        "lengths": draw_lengths(jax.random.fold_in(keys[13], 71), 0),
        "buckets": draw_buckets(jax.random.fold_in(keys[13], 71), 0),
        "ln1_gain": jnp.clip(1.0 + 0.18 * jax.random.normal(keys[3], (D,), jnp.float32), 0.099609375, 1.8984375).astype(jnp.bfloat16),
        "ln1_bias": gaussian(keys[4], (D,), 0.5, 3.0, ((0, 8),)),
        "w_qkv": gaussian(keys[5], (D, 3 * D), D ** -0.5, 0.1875, ((0, 8),)),
        "rel_table": gaussian(keys[6], (HEADS * BUCKETS,), 1.0, 4.0, ((0, 8),)),
        "w_out": gaussian(keys[7], (D, D), (D // 128) ** -0.5, 2.0, ((0, 8),)),
        "ln2_gain": jnp.clip(1.0 + 0.18 * jax.random.normal(keys[8], (D,), jnp.float32), 0.099609375, 1.8984375).astype(jnp.bfloat16),
        "ln2_bias": gaussian(keys[9], (D,), 0.5, 3.0, ((0, 8),)),
        "w_up": gaussian(keys[10], (D, FF), D ** -0.5, 0.1875, ((0, 8),)),
        "w_down": gaussian(keys[11], (FF, D), FF ** -0.5, 0.09375, ((0, 8),)),
        "cotangent": gaussian(keys[12], (TOKENS, D), 1.0, 6.0, ((0, 32),)),
    }


norm_eps = 1e-05
highest = lax.Precision.HIGHEST

@jax.custom_vjp
def low(v):
    return lax.optimization_barrier(v.astype(jnp.bfloat16)).astype(jnp.float32)

@jax.custom_vjp
def low_back(v):
    return v

def low_keep(v):
    return (low(v), None)

def low_pass(kept, grad):
    return (grad,)

def back_keep(v):
    return (v, None)

def back_low(kept, grad):
    return (low(grad),)
low.defvjp(low_keep, low_pass)
low_back.defvjp(back_keep, back_low)

def layer_norm(values, gain, shift):
    center = values - lax.optimization_barrier(jnp.mean(values, axis=-1, keepdims=True))
    spread = lax.optimization_barrier(jnp.mean(center * center, axis=-1, keepdims=True))
    return center * lax.rsqrt(spread + norm_eps) * gain + shift

def matmul(left, right):
    return jnp.dot(left, right, precision=highest)

def forward(inputs, valid_rows, allowed, bias_index, params):
    gain_one, shift_one, weight_qkv, table_flat, weight_out, gain_two, shift_two, weight_up, weight_down = params
    normed_one = low(layer_norm(inputs, gain_one, shift_one))
    packed = low(low_back(matmul(normed_one, weight_qkv)))
    queries = packed[:, :D].reshape(SLOT, HEADS, HEAD_DIM)
    keys_all = packed[:, D:2 * D].reshape(SLOT, HEADS, HEAD_DIM)
    values_all = packed[:, 2 * D:].reshape(SLOT, HEADS, HEAD_DIM)
    bias_full = table_flat.reshape(HEADS, BUCKETS)[:, bias_index]
    scores = jnp.einsum('ihd,jhd->hij', queries, keys_all, precision=highest) * HEAD_DIM ** (-0.5) + bias_full
    scores = low_back(scores)
    masked = jnp.where(allowed[None], scores, -1e+30)
    row_max = lax.optimization_barrier(jnp.max(masked, axis=-1, keepdims=True))
    weights_exp = jnp.exp(masked - row_max)
    probs = weights_exp / lax.optimization_barrier(jnp.sum(weights_exp, axis=-1, keepdims=True))
    mixed = jnp.einsum('hij,jhd->ihd', low(probs), values_all, precision=highest).reshape(SLOT, D)
    attended = low(low_back(mixed))
    attn_out = low_back(matmul(attended, weight_out))
    middle = inputs + valid_rows * attn_out
    normed_two = low(layer_norm(middle, gain_two, shift_two))
    up_proj = low_back(matmul(normed_two, weight_up))
    hidden = low(jax.nn.gelu(up_proj))
    ffn_out = low_back(matmul(hidden, weight_down))
    return middle + valid_rows * ffn_out

def reference(tokens, lengths, buckets, ln1_gain, ln1_bias, w_qkv, rel_table, w_out, ln2_gain, ln2_bias, w_up, w_down, cotangent):
    params = tuple((member.astype(jnp.float32) for member in (ln1_gain, ln1_bias, w_qkv, rel_table, w_out, ln2_gain, ln2_bias, w_up, w_down)))
    position = jnp.arange(SLOT, dtype=jnp.int32)
    distance = jnp.maximum(position[:, None] - position[None, :], 0).astype(jnp.int32)
    bias_index = buckets[distance]
    inputs_all = tokens.astype(jnp.float32).reshape(SEQS, SLOT, D)
    cotan_all = cotangent.astype(jnp.float32).reshape(SEQS, SLOT, D)

    def per_sequence(totals, member):
        inputs, cotan, seq_length = member
        valid_rows = (position < seq_length).astype(jnp.float32)[:, None]
        allowed = (position[None, :] <= position[:, None]) & (position[None, :] < seq_length)

        def apply_layer(inputs_in, params_in):
            return forward(inputs_in, valid_rows, allowed, bias_index, params_in)
        result, pullback = jax.vjp(apply_layer, inputs, params)
        grad_inputs, grad_params = pullback(cotan)
        totals = jax.tree.map(jnp.add, totals, grad_params)
        return (totals, (result.astype(jnp.bfloat16), grad_inputs))
    zeros_init = tuple((jnp.zeros_like(member) for member in params))
    totals, (results, grad_inputs) = lax.scan(per_sequence, zeros_init, (inputs_all, cotan_all, lengths))
    return (results.reshape(TOKENS, D), grad_inputs.reshape(TOKENS, D), totals[0], totals[1], totals[2], totals[3], totals[4], totals[5], totals[6], totals[7], totals[8])
```

```python
import functools

import jax
import jax.numpy as jnp
from jax import lax
from jax.experimental import pallas as pl
from jax.experimental.layout import Layout, with_layout_constraint
from jax.experimental.pallas import tpu as pltpu
from jax.sharding import PartitionSpec as P

HEADS = 16
HEAD_DIM = 64
BUCKETS = 32
TILE = 128
PAIR = 2 * HEAD_DIM

norm_eps = 1e-05
neg_large = -1e30
f32 = jnp.float32
bf16 = jnp.bfloat16
VMEM_LIMIT = 56 * 1024 * 1024


PEAK = 1.15e15


def cost(us, share=1.0):
    return pl.CostEstimate(flops=int(us * share * 1e-6 * PEAK), bytes_accessed=0, transcendentals=0)


def dot(a, b, dims=((1,), (0,))):
    return lax.dot_general(a, b, (dims, ((), ())), preferred_element_type=f32)


NT = ((1,), (1,))
TN = ((0,), (0,))


def block_of(x):
    zeros = (0,) * x.ndim
    return pl.BlockSpec(x.shape, lambda i: zeros)


def cut_attn_kernel(n_ref, qkv_ref, out_ref, small_ref, o_ref):
    n = n_ref[0]
    model = out_ref.shape[1]
    mine = model // 4
    at = 0
    for p in range(mine // PAIR):
        for part in range(3):
            start = pl.multiple_of(part * model + n * mine + p * PAIR, PAIR)
            o_ref[:, at : at + PAIR] = qkv_ref[:, pl.ds(start, PAIR)]
            at += PAIR
    o_ref[:, at : at + mine] = out_ref[:, pl.ds(pl.multiple_of(n * mine, mine), mine)]
    at += mine
    o_ref[:, at:] = jnp.zeros((o_ref.shape[0], TILE), bf16)
    o_ref[:16, at:] = small_ref[...]


def cut_attn(n, w_qkv, w_out, small):
    rows, model = w_out.shape
    return pl.pallas_call(
        cut_attn_kernel,
        grid=(1,),
        in_specs=[pl.BlockSpec(memory_space=pltpu.SMEM)]
        + [block_of(x) for x in (w_qkv, w_out, small)],
        out_specs=pl.BlockSpec((rows, model + TILE), lambda i: (0, 0)),
        out_shape=jax.ShapeDtypeStruct((rows, model + TILE), bf16),
        cost_estimate=cost(2),
        name="cut_attn",
    )(n, w_qkv, w_out, small)


def cut_ffn_kernel(n_ref, up_ref, down_ref, o_ref):
    n = n_ref[0]
    size = down_ref.shape[0]
    model = down_ref.shape[1]
    for d in range(model // size):
        start = pl.multiple_of(d * 4 * size + n * size, size)
        o_ref[0, :, d * size : (d + 1) * size] = up_ref[:, pl.ds(start, size)]
    o_ref[1] = down_ref[...]


def cut_ffn(n, w_up, w_down):
    rows = w_up.shape[0]
    quarter, model = w_down.shape[0] // 4, w_down.shape[1]
    return pl.pallas_call(
        cut_ffn_kernel,
        grid_spec=pltpu.PrefetchScalarGridSpec(
            num_scalar_prefetch=1,
            grid=(1,),
            in_specs=[
                pl.BlockSpec(w_up.shape, lambda i, n: (0, 0)),
                pl.BlockSpec((quarter, model), lambda i, n: (n[0], 0)),
            ],
            out_specs=pl.BlockSpec((2, rows, model), lambda i, n: (0, 0, 0)),
        ),
        out_shape=jax.ShapeDtypeStruct((2, rows, model), bf16),
        cost_estimate=cost(2, 0.05),
        name="cut_ffn",
    )(n, w_up, w_down)


def small_kernel(where_ref, *refs):
    out_ref = refs[-1]
    out_ref[...] = jnp.zeros_like(out_ref)
    lane = lax.broadcasted_iota(jnp.int32, (1, TILE), 1)
    for i, ref in enumerate(refs[:-1]):
        d = where_ref[i]
        got = ref[...].astype(f32)
        start = pl.multiple_of(d * TILE, TILE)
        for v in range(4):
            out_ref[v : v + 1, pl.ds(start, TILE)] = got[v : v + 1]
        rel = got[4:5]
        odd = lax.rem(d, 2) == 1
        rel = jnp.where(odd, pltpu.roll(rel, TILE // 2, 1), rel)
        rel = jnp.where((lane >= TILE // 2) == odd, rel, 0.0)
        start = pl.multiple_of((d // 2) * TILE, TILE)
        out_ref[4:5, pl.ds(start, TILE)] += rel


def small_rows(where, pieces, at):
    model = len(pieces) * TILE
    return pl.pallas_call(
        small_kernel,
        grid=(1,),
        in_specs=[pl.BlockSpec(memory_space=pltpu.SMEM)]
        + [pl.BlockSpec((16, TILE), lambda i: (0, at // TILE))] * len(pieces),
        out_specs=pl.BlockSpec((8, model), lambda i: (0, 0)),
        out_shape=jax.ShapeDtypeStruct((8, model), f32),
        cost_estimate=cost(2),
        name="small_rows",
    )(where, *pieces)


def tiles_kernel(n_ref, small_ref, buckets_ref, out_ref):
    heads, count = out_ref.shape[:2]
    lanes = heads * BUCKETS
    slot = buckets_ref.shape[1]
    rel = small_ref[4:5, pl.ds(pl.multiple_of(n_ref[0] * lanes, lanes), lanes)]
    head = lax.broadcasted_iota(jnp.int32, (8, lanes), 0)
    lane = lax.broadcasted_iota(jnp.int32, (8, lanes), 1)
    table = jnp.where(lane // BUCKETS == head, rel, 0.0).astype(bf16)
    bucket = lax.broadcasted_iota(jnp.int32, (lanes, slot), 0) % BUCKETS
    onehot = (buckets_ref[...] == bucket).astype(f32).astype(bf16)
    by_distance = dot(table, onehot)
    row = lax.broadcasted_iota(jnp.int32, (TILE, TILE), 0)
    col = lax.broadcasted_iota(jnp.int32, (TILE, TILE), 1)
    for h in range(heads):
        for delta in range(count):
            here = by_distance[h : h + 1, delta * TILE : (delta + 1) * TILE]
            below = by_distance[h : h + 1, max(delta - 1, 0) * TILE : max(delta, 1) * TILE]
            wide = jnp.broadcast_to(jnp.concatenate([here, below], axis=1), (TILE, 2 * TILE))
            tile = pltpu.roll(wide, 0, 1, stride=1, stride_axis=0)[:, :TILE].T
            if delta == 0:
                tile = jnp.where(col <= row, tile, neg_large)
            out_ref[h, delta] = tile


def bias_tiles(n, small, buckets, heads):
    slot = buckets.shape[0]
    buckets = buckets.reshape(1, slot)
    shape = (heads, slot // TILE, TILE, TILE)
    return pl.pallas_call(
        tiles_kernel,
        grid=(1,),
        in_specs=[pl.BlockSpec(memory_space=pltpu.SMEM), block_of(small), block_of(buckets)],
        out_specs=pl.BlockSpec(shape, lambda i: (0, 0, 0, 0)),
        out_shape=jax.ShapeDtypeStruct(shape, f32),
        cost_estimate=cost(4),
        name="bias_tiles",
    )(n, small, buckets)


def normalized(v):
    center = v - jnp.mean(v, axis=-1, keepdims=True)
    factor = lax.rsqrt(jnp.mean(center * center, axis=-1, keepdims=True) + norm_eps)
    return center * factor, factor


def xhat_kernel(*refs):
    out_ref = refs[-1]
    at = 0
    for ref in refs[:-1]:
        rows = ref.shape[0]
        out_ref[at : at + rows] = normalized(ref[...].astype(f32))[0]
        at += rows


def xhat_of(pieces):
    slot, model = sum(p.shape[0] for p in pieces), pieces[0].shape[1]
    return pl.pallas_call(
        xhat_kernel,
        grid=(1,),
        in_specs=[block_of(p) for p in pieces],
        out_specs=pl.BlockSpec((slot, model), lambda i: (0, 0)),
        out_shape=jax.ShapeDtypeStruct((slot, model), f32),
        compiler_params=pltpu.CompilerParams(vmem_limit_bytes=VMEM_LIMIT),
        cost_estimate=cost(2.5, 0.05),
        name="xhat",
    )(*pieces)


def qkv_kernel(count, where_ref, small_ref, *refs):
    xhats, pieces = refs[:4], refs[4 : 4 + count]
    norm_ref, packed_ref, wq_ref, wo_ref, w_ref, x_ref, sems, x_sems = refs[4 + count :]
    step = pl.program_id(0)
    width = wq_ref.shape[1]

    def fetch(r):
        return pltpu.make_async_copy(xhats[r], x_ref.at[r % 2], x_sems.at[r % 2])

    @pl.when(step == 0)
    def _():
        fetch(0).start()
        copies = []
        for i, piece in enumerate(pieces):
            size = piece.shape[0]
            start = pl.multiple_of(where_ref[i] * size, size)
            copies.append(pltpu.make_async_copy(piece, w_ref.at[pl.ds(start, size)], sems.at[i]))
            copies[-1].start()
        for copy in copies:
            copy.wait()
        wq_ref[...] = w_ref[:, :width]
        wo_ref[...] = w_ref[:, width : width + wo_ref.shape[1]]

    for r in range(4):

        @pl.when(step == r)
        def _(r=r):
            if r < 3:
                fetch(r + 1).start()
            fetch(r).wait()

    norm = (x_ref[lax.rem(step, 2)] * small_ref[0:1] + small_ref[1:2]).astype(bf16)
    norm_ref[...] = norm
    packed_ref[...] = dot(norm, wq_ref[...]).astype(bf16)


def qkv_of(where, small, xhats, pieces, width):
    slot, model = xhats[0].shape
    total = pieces[0].shape[1]
    out = model // 4
    whole = lambda shape: pl.BlockSpec(shape, lambda i: (0, 0))
    rows = lambda cols: pl.BlockSpec((slot, cols), lambda i: (i, 0))
    return pl.pallas_call(
        functools.partial(qkv_kernel, len(pieces)),
        grid=(4,),
        in_specs=[pl.BlockSpec(memory_space=pltpu.SMEM), whole(small.shape)]
        + [pl.BlockSpec(memory_space=pl.ANY)] * (4 + len(pieces)),
        out_specs=[rows(model), rows(width), whole((model, width)), whole((model, out))],
        out_shape=[
            jax.ShapeDtypeStruct((4 * slot, model), bf16),
            jax.ShapeDtypeStruct((4 * slot, width), bf16),
            jax.ShapeDtypeStruct((model, width), bf16),
            jax.ShapeDtypeStruct((model, out), bf16),
        ],
        scratch_shapes=[
            pltpu.VMEM((model, total), bf16),
            pltpu.VMEM((2, slot, model), f32),
            pltpu.SemaphoreType.DMA((len(pieces),)),
            pltpu.SemaphoreType.DMA((2,)),
        ],
        compiler_params=pltpu.CompilerParams(vmem_limit_bytes=VMEM_LIMIT),
        cost_estimate=cost(7),
        name="qkv",
    )(where, small, *xhats, *pieces)


def ln1_back_kernel(gp_ref, wq_ref, x0_ref, x1_ref, p0_ref, p1_ref, vec_ref):
    step = pl.program_id(0)
    grad = dot(gp_ref[...], wq_ref[...], NT)

    @pl.when(step == 0)
    def _():
        vec_ref[0:1] = jnp.sum(grad * x0_ref[...], axis=0, keepdims=True)
        vec_ref[1:2] = jnp.sum(grad, axis=0, keepdims=True)
        p0_ref[...] = grad.astype(p0_ref.dtype)

    @pl.when(step == 1)
    def _():
        vec_ref[0:1] += jnp.sum(grad * x1_ref[...], axis=0, keepdims=True)
        vec_ref[1:2] += jnp.sum(grad, axis=0, keepdims=True)
        p1_ref[...] = grad.astype(p1_ref.dtype)


def ln1_back(grad_packed, wqkv, xhats, first):
    slot, model = xhats[0].shape
    width = wqkv.shape[1]
    whole = lambda shape: pl.BlockSpec(shape, lambda i: (0, 0))
    return pl.pallas_call(
        ln1_back_kernel,
        grid=(2,),
        in_specs=[
            pl.BlockSpec((slot, width), lambda i: (first + i, 0)),
            whole((model, width)),
            whole((slot, model)),
            whole((slot, model)),
        ],
        out_specs=[whole((slot, model)), whole((slot, model)), whole((2, model))],
        out_shape=[
            jax.ShapeDtypeStruct((slot, model), bf16 if first else f32),
            jax.ShapeDtypeStruct((slot, model), bf16),
            jax.ShapeDtypeStruct((2, model), f32),
        ],
        compiler_params=pltpu.CompilerParams(vmem_limit_bytes=VMEM_LIMIT),
        cost_estimate=cost(5, 0.1 if first else 1.0),
        name="ln1_back",
    )(grad_packed, wqkv, *xhats)


def attn_fwd_kernel(len_ref, qkv_ref, tiles_ref, att_ref, p_ref):
    slot = qkv_ref.shape[0]
    blocks = range(slot // TILE)
    heads = range(2)
    length = len_ref[0]
    lane = lax.broadcasted_iota(jnp.int32, (1, PAIR), 1)
    col = lax.broadcasted_iota(jnp.int32, (1, slot), 1)
    hidden = jnp.where(col < length, 0.0, neg_large)
    q = qkv_ref[:, :PAIR] * HEAD_DIM ** (-0.5)
    k = qkv_ref[:, PAIR : 2 * PAIR]
    v = qkv_ref[:, 2 * PAIR :]
    own = [(lane // HEAD_DIM) == hh for hh in heads]
    qm = [jnp.where(own[hh], q, jnp.zeros_like(q)) for hh in heads]
    span = [(i + 1) * TILE for i in blocks]
    items = [(hh, i) for hh in heads for i in blocks]
    s = [dot(qm[hh][i * TILE : span[i]], k[: span[i]], NT) for hh, i in items]
    s = [
        x + jnp.concatenate([tiles_ref[hh, i - j] for j in range(i + 1)], axis=1) + hidden[:, : span[i]]
        for x, (hh, i) in zip(s, items)
    ]
    top = [jnp.max(x, axis=1, keepdims=True) for x in s]
    e = [jnp.exp(x - m) for x, m in zip(s, top)]
    scale = [1.0 / jnp.sum(x, axis=1, keepdims=True) for x in e]
    probs = [(x * r).astype(bf16) for x, r in zip(e, scale)]
    for x, (hh, i) in zip(probs, items):
        p_ref[hh, i * TILE : span[i], : span[i]] = x
    o = {item: dot(x, v[: span[item[1]]]) for x, item in zip(probs, items)}
    for i in blocks:
        att_ref[i * TILE : span[i], :] = jnp.where(own[0], o[0, i], o[1, i]).astype(bf16)


def attn_fwd(lengths, packed, tiles, seq):
    heads, count = tiles.shape[:2]
    slot = count * TILE
    return pl.pallas_call(
        attn_fwd_kernel,
        grid=(heads // 2,),
        in_specs=[
            pl.BlockSpec(memory_space=pltpu.SMEM),
            pl.BlockSpec((slot, 3 * PAIR), lambda p: (seq, p)),
            pl.BlockSpec((2, count, TILE, TILE), lambda p: (p, 0, 0, 0)),
        ],
        out_specs=[
            pl.BlockSpec((slot, PAIR), lambda p: (0, p)),
            pl.BlockSpec((2, slot, slot), lambda p: (p, 0, 0)),
        ],
        out_shape=[
            jax.ShapeDtypeStruct((slot, heads * HEAD_DIM), bf16),
            jax.ShapeDtypeStruct((heads, slot, slot), bf16),
        ],
        compiler_params=pltpu.CompilerParams(vmem_limit_bytes=VMEM_LIMIT),
        cost_estimate=cost(7.5),
        name="attn_fwd",
    )(lengths, packed, tiles)


def attn_bwd_kernel(qkv_ref, ga_ref, att_ref, p_ref, *refs):
    g_ref, sum_ref, ds_ref = refs[-3:]
    slot = qkv_ref.shape[0]
    blocks = range(slot // TILE)
    heads = range(2)
    lane = lax.broadcasted_iota(jnp.int32, (1, PAIR), 1)
    scale = HEAD_DIM ** (-0.5)
    q = qkv_ref[:, :PAIR] * scale
    k = qkv_ref[:, PAIR : 2 * PAIR]
    v = qkv_ref[:, 2 * PAIR :]
    ga = ga_ref[...]
    prod = ga.astype(f32) * att_ref[...].astype(f32)
    own = [(lane // HEAD_DIM) == hh for hh in heads]
    gam = [jnp.where(own[hh], ga, jnp.zeros_like(ga)) for hh in heads]
    inner = [jnp.sum(jnp.where(own[hh], prod, 0.0), axis=1, keepdims=True) for hh in heads]
    span = [(i + 1) * TILE for i in blocks]
    rows = [slice(i * TILE, span[i]) for i in blocks]
    items = [(hh, i) for hh in heads for i in blocks]
    dp = [dot(gam[hh][rows[i]], v[: span[i]], NT) for hh, i in items]
    ds = {
        (hh, i): (p_ref[hh, rows[i], : span[i]].astype(f32) * (x - inner[hh][rows[i]])).astype(bf16)
        for x, (hh, i) in zip(dp, items)
    }
    for hh, i in items:
        ds_ref[hh, rows[i], : span[i]] = ds[hh, i]
    dq = {(hh, i): dot(ds[hh, i], k[: span[i]]) for hh, i in items}
    dv = {(hh, j): dot(p_ref[hh, j * TILE :, rows[j]], ga[j * TILE :], TN) for hh, j in items}
    dk = {(hh, j): dot(ds_ref[hh, j * TILE :, rows[j]], q[j * TILE :], TN) for hh, j in items}
    for i in blocks:
        for at, got, factor in ((0, dq, scale), (PAIR, dk, 1.0), (2 * PAIR, dv, 1.0)):
            both = jnp.where(own[0], got[0, i], got[1, i]) * factor
            g_ref[rows[i], at : at + PAIR] = both.astype(bf16)
    row = lax.broadcasted_iota(jnp.int32, (TILE, TILE), 0)
    col = lax.broadcasted_iota(jnp.int32, (TILE, TILE), 1)
    flip = jnp.where(row + col == TILE - 1, 1.0, 0.0).astype(bf16)
    diag = {}
    for hh in heads:
        for delta in blocks:
            parts = [
                ds[hh, i][:, (i - delta) * TILE : (i - delta + 1) * TILE].astype(f32)
                for i in blocks
                if i >= delta
            ]
            diag[hh, delta] = functools.reduce(jnp.add, parts)
    high = {key: x.astype(bf16) for key, x in diag.items()}
    low = {key: (x - high[key].astype(f32)).astype(bf16) for key, x in diag.items()}
    turned = {key: dot(flip, high[key]) + dot(flip, low[key]) for key in diag}
    sums = {}
    for key, x in turned.items():
        wide = jnp.concatenate([x, jnp.zeros_like(x)], axis=1)
        wide = pltpu.roll(wide, 0, 1, stride=1, stride_axis=0)
        sums[key] = jnp.sum(wide, axis=0, keepdims=True)
    for hh in heads:
        for delta in blocks:
            here = sums[hh, delta][:, :TILE]
            if delta + 1 in blocks:
                here = here + sums[hh, delta + 1][:, TILE:]
            sum_ref[0, hh : hh + 1, rows[delta]] = here


def attn_bwd(packed, ga, att, probs, seq, into):
    heads, slot = probs.shape[:2]
    steps = heads // 2
    return pl.pallas_call(
        attn_bwd_kernel,
        grid=(steps,),
        in_specs=[
            pl.BlockSpec((slot, 3 * PAIR), lambda p: (seq, p)),
            pl.BlockSpec((slot, PAIR), lambda p: (0, p)),
            pl.BlockSpec((slot, PAIR), lambda p: (0, p)),
            pl.BlockSpec((2, slot, slot), lambda p: (p, 0, 0)),
        ]
        + ([] if into is None else [pl.BlockSpec(memory_space=pl.ANY)]),
        out_specs=[
            pl.BlockSpec((slot, 3 * PAIR), lambda p: (seq, p)),
            pl.BlockSpec((1, 2, slot), lambda p: (p, 0, 0)),
        ],
        out_shape=[
            jax.ShapeDtypeStruct(packed.shape, bf16),
            jax.ShapeDtypeStruct((steps, 2, slot), f32),
        ],
        scratch_shapes=[pltpu.VMEM((2, slot, slot), bf16)],
        input_output_aliases={} if into is None else {4: 0},
        compiler_params=pltpu.CompilerParams(vmem_limit_bytes=VMEM_LIMIT),
        cost_estimate=cost(5, 0.2),
        name="attn_bwd",
    )(packed, ga, att, probs, *(() if into is None else (into,)))


def ln1_last_kernel(tok_ref, xhat_ref, gmid_ref, small_ref, p0_ref, p1_ref, p2_ref, p3_ref, out_ref):
    _, factor = normalized(tok_ref[...].astype(f32))
    xhat = xhat_ref[...]
    low = pl.program_id(0) == 0
    e = p0_ref[...] + p1_ref[...].astype(f32) + jnp.where(low, p2_ref[...], p3_ref[...]).astype(f32)
    e = e * small_ref[0:1]
    out_ref[...] = gmid_ref[...] + factor * (
        e - jnp.mean(e, axis=-1, keepdims=True) - xhat * jnp.mean(e * xhat, axis=-1, keepdims=True)
    )


def ln1_last(tokens, xhat, grad_middle, small, p0, p1, p2, p3):
    slot, model = tokens.shape
    row = pl.BlockSpec((slot // 2, model), lambda i: (i, 0))
    part = pl.BlockSpec((slot // 2, model), lambda i: (0, 0))
    return pl.pallas_call(
        ln1_last_kernel,
        grid=(2,),
        in_specs=[row] * 3 + [block_of(small), row, row, part, part],
        out_specs=row,
        out_shape=jax.ShapeDtypeStruct((slot, model), f32),
        compiler_params=pltpu.CompilerParams(vmem_limit_bytes=VMEM_LIMIT),
        cost_estimate=cost(5, 0.05),
        name="ln1_last",
    )(tokens, xhat, grad_middle, small, p0, p1, p2, p3)


def quarters(n, r, size):
    return pl.ds(pl.multiple_of(lax.bitwise_xor(n, r) * size, size), size)


def out_ln2_kernel(part, n_ref, len_ref, tok_ref, small_ref, *refs):
    atts, wouts = refs[:4], refs[4:8]
    mid_ref, all_ref, norm_ref = refs[-3:]
    n = n_ref[0]
    rows, model = tok_ref.shape
    size = model // 4
    for r in range(4):
        all_ref[:, quarters(n, r, size)] = atts[r][...]
    valid = part * rows + lax.broadcasted_iota(jnp.int32, (rows, 1), 0) < len_ref[0]
    for r in range(4):
        cols = quarters(n, r, size)
        out = dot(all_ref[...], wouts[r][...])
        mid_ref[:, cols] = tok_ref[:, cols].astype(f32) + jnp.where(valid, out, 0.0)
    xhat, _ = normalized(mid_ref[...])
    norm_ref[...] = (xhat * small_ref[2:3] + small_ref[3:4]).astype(bf16)


def out_ln2(n, length, tokens, small, atts, wouts, part, into):
    slot, model = tokens.shape
    smem = pl.BlockSpec(memory_space=pltpu.SMEM)
    whole = lambda x: pl.BlockSpec(x.shape, lambda i: (0, 0))
    rows = lambda cols: pl.BlockSpec((slot // 2, cols), lambda i: (part, 0))
    return pl.pallas_call(
        functools.partial(out_ln2_kernel, part),
        grid=(1,),
        in_specs=[smem, smem, rows(model), whole(small)]
        + [rows(model // 4)] * 4
        + [whole(w) for w in wouts]
        + [pl.BlockSpec(memory_space=pl.ANY)] * len(into),
        out_specs=[rows(model), rows(model), pl.BlockSpec((slot // 2, model), lambda i: (0, 0))],
        out_shape=[
            jax.ShapeDtypeStruct((slot, model), f32),
            jax.ShapeDtypeStruct((slot, model), bf16),
            jax.ShapeDtypeStruct((slot // 2, model), bf16),
        ],
        input_output_aliases={12 + i: i for i in range(len(into))},
        compiler_params=pltpu.CompilerParams(vmem_limit_bytes=VMEM_LIMIT),
        cost_estimate=cost(4, 1 / 64),
        name="out_ln2",
    )(n, length, tokens, small, *atts, *wouts, *into)


def ln2_back_kernel(part, n_ref, len_ref, mid_ref, cot_ref, small_ref, p0_ref, p2_ref, *refs):
    near, wouts = refs[:2], refs[2:6]
    gmid_ref, keep_ref, send_ref = refs[-9:-6]
    gatts = refs[-6:-2]
    vec_ref, branch_ref = refs[-2:]
    n = n_ref[0]
    rows, model = mid_ref.shape
    size = model // 4
    xhat, factor = normalized(mid_ref[...])
    grad = p0_ref[...] + p2_ref[...].astype(f32)
    grad = grad + jnp.concatenate([x[...] for x in near], axis=0).astype(f32)
    vec_ref[0:1] = jnp.sum(grad * xhat, axis=0, keepdims=True)
    vec_ref[1:2] = jnp.sum(grad, axis=0, keepdims=True)
    e = grad * small_ref[2:3]
    back = factor * (
        e - jnp.mean(e, axis=-1, keepdims=True) - xhat * jnp.mean(e * xhat, axis=-1, keepdims=True)
    )
    gmid = cot_ref[...].astype(f32) + back
    gmid_ref[...] = gmid
    valid = part * rows + lax.broadcasted_iota(jnp.int32, (rows, 1), 0) < len_ref[0]
    branch_ref[...] = jnp.where(valid, gmid, 0.0).astype(bf16)
    cuts = [branch_ref[:, quarters(n, r, size)] for r in range(4)]
    keep_ref[:, :size] = cuts[0]
    keep_ref[:, size:] = cuts[2]
    send_ref[:, :size] = cuts[1]
    send_ref[:, size:] = cuts[3]
    for r in range(4):
        feats = quarters(n, r, size)
        total = dot(cuts[0], wouts[0][feats, :], NT)
        for k in range(1, 4):
            total = total + dot(cuts[k], wouts[k][feats, :], NT)
        gatts[r][...] = total.astype(bf16)


def ln2_back(n, length, middle, cot, small, p0, near, p2, wouts, part, into):
    slot, model = middle.shape
    smem = pl.BlockSpec(memory_space=pltpu.SMEM)
    whole = lambda x: pl.BlockSpec(x.shape, lambda i: (0, 0))
    rows = lambda cols: pl.BlockSpec((slot // 2, cols), lambda i: (part, 0))
    return pl.pallas_call(
        functools.partial(ln2_back_kernel, part),
        grid=(1,),
        in_specs=[smem, smem, rows(model), rows(model), whole(small), rows(model), whole(p2)]
        + [whole(w) for w in (*near, *wouts)]
        + [pl.BlockSpec(memory_space=pl.ANY)] * len(into),
        out_specs=[rows(model), rows(model // 2), rows(model // 2)]
        + [rows(model // 4)] * 4
        + [pl.BlockSpec((2, model), lambda i: (0, 0))],
        out_shape=[
            jax.ShapeDtypeStruct((slot, model), f32),
            jax.ShapeDtypeStruct((slot, model // 2), bf16),
            jax.ShapeDtypeStruct((slot, model // 2), bf16),
        ]
        + [jax.ShapeDtypeStruct((slot, model // 4), bf16)] * 4
        + [jax.ShapeDtypeStruct((2, model), f32)],
        scratch_shapes=[pltpu.VMEM((slot // 2, model), bf16)],
        input_output_aliases={13 + i: i for i in range(len(into))},
        compiler_params=pltpu.CompilerParams(vmem_limit_bytes=VMEM_LIMIT),
        cost_estimate=cost(5),
        name="ln2_back",
    )(n, length, middle, cot, small, p0, p2, *near, *wouts, *into)


def gelu_both(u):
    c0 = 0.7978845608028654
    c1 = 0.044715
    sq = u * u
    t = jnp.tanh(u * (c0 + (c0 * c1) * sq))
    half = 0.5 + 0.5 * t
    slope = half + (1.0 - t * t) * (u * (0.5 * c0 + (1.5 * c0 * c1) * sq))
    return u * half, slope


def ffn_kernel(count, places, start, cuts, w_any, *refs):
    norms, grads = refs[:count], refs[count : count + len(places)]
    n4_any, g4_any, hid4_any, gua4_any = refs[-13:-9]
    sums = refs[-16 - cuts : -13]
    o0_ref, gn0_ref = sums[:2]
    n_ref, g_ref, wu_ref, wd_ref, hid_ref, gua_ref, sems, w_sems, out_sems = refs[-9:]
    step = pl.program_id(0)
    steps = pl.num_programs(0) // 2
    rows = n_ref.shape[0]
    block = o0_ref.shape[1]
    mine = pl.ds(start, rows)
    outs = [
        pltpu.make_async_copy(src, dst.at[mine], out_sems.at[i])
        for i, (src, dst) in enumerate(
            ((n_ref, n4_any), (g_ref, g4_any), (hid_ref, hid4_any), (gua_ref, gua4_any))
        )
    ]
    shards, _, size, _ = w_any.shape
    weights = [
        [
            pltpu.make_async_copy(
                w_any.at[d, i], whole.at[pl.ds(d * size, size)], w_sems.at[d, i]
            )
            for d in range(shards)
        ]
        for i, whole in enumerate((wu_ref, wd_ref))
    ]
    acts = []
    grads = [g.at[pl.ds(first, size)] for g, (first, size) in zip(grads, places)]
    for j, (pieces, whole) in enumerate(((norms, n_ref), (grads, g_ref))):
        acts.append([])
        at = 0
        for i, piece in enumerate(pieces):
            here = piece.shape[0]
            acts[j].append(
                pltpu.make_async_copy(piece, whole.at[pl.ds(at, here)], sems.at[j, i])
            )
            at += here

    @pl.when(step == 0)
    def _():
        for copy in acts[0] + weights[0] + acts[1] + weights[1]:
            copy.start()
        for copy in acts[0] + weights[0]:
            copy.wait()

    @pl.when(step < steps)
    def _():
        cols = pl.ds(pl.multiple_of(step * block, block), block)
        u = dot(n_ref[...], wu_ref[:, cols])
        hid, slope = gelu_both(u)

        @pl.when(step == 0)
        def _():
            for copy in acts[1] + weights[1]:
                copy.wait()

        gh = dot(g_ref[...], wd_ref[cols, :], NT)
        hid_ref[:, cols] = hid.astype(bf16)
        gua_ref[:, cols] = (slope * gh).astype(bf16)

    @pl.when(step == steps)
    def _():
        for copy in outs:
            copy.start()

    @pl.when(step >= steps)
    def _():
        cols = pl.ds(pl.multiple_of((step - steps) * block, block), block)
        half = rows // 2
        gn = dot(gua_ref[...], wu_ref[cols, :], NT)
        o = dot(hid_ref[...], wd_ref[:, cols])
        for first, pieces, total in ((o0_ref, sums[2:3], o), (gn0_ref, sums[3:], gn)):
            first[...] = total[:half]
            size = half // len(pieces)
            for i, piece in enumerate(pieces):
                piece[...] = total[half + i * size : half + (i + 1) * size].astype(bf16)

    @pl.when(step == 2 * steps - 1)
    def _():
        for copy in outs:
            copy.wait()


def ffn(norms, grads, places, weights, start, into, cuts):
    width = norms[0].shape[1]
    rows = sum(x.shape[0] for x in norms)
    total = into[0].shape[0] if into else 2 * rows
    units = weights.shape[0] * weights.shape[2]
    block = min(512, units)
    steps = units // block
    half = rows // 2
    anywhere = pl.BlockSpec(memory_space=pl.ANY)
    late = lambda size: pl.BlockSpec((size, block), lambda i: (0, jnp.maximum(i - steps, 0)))
    acts = pltpu.VMEM((rows, width), bf16)
    hidden = pltpu.VMEM((rows, units), bf16)
    ins = 1 + len(norms) + len(grads)
    outs = 3 + cuts
    got = pl.pallas_call(
        functools.partial(ffn_kernel, len(norms), places, start, cuts),
        grid=(2 * steps,),
        in_specs=[anywhere] * (ins + len(into)),
        out_specs=[late(half)] * 2 + [late(half)] + [late(half // cuts)] * cuts + [anywhere] * 4,
        out_shape=[jax.ShapeDtypeStruct((half, width), f32)] * 2
        + [jax.ShapeDtypeStruct((half, width), bf16)]
        + [jax.ShapeDtypeStruct((half // cuts, width), bf16)] * cuts
        + [jax.ShapeDtypeStruct((total, width), bf16)] * 2
        + [jax.ShapeDtypeStruct((total, units), bf16)] * 2,
        scratch_shapes=[
            acts,
            acts,
            pltpu.VMEM((width, units), bf16),
            pltpu.VMEM((units, width), bf16),
            hidden,
            hidden,
            pltpu.SemaphoreType.DMA((2, max(len(norms), len(grads)))),
            pltpu.SemaphoreType.DMA((weights.shape[0], 2)),
            pltpu.SemaphoreType.DMA((4,)),
        ],
        input_output_aliases={ins + i: outs + i for i in range(len(into))},
        compiler_params=pltpu.CompilerParams(vmem_limit_bytes=VMEM_LIMIT),
        cost_estimate=cost(8 if into else 12, 1 / 64),
        name="ffn",
    )(weights, *norms, *grads, *into)
    return got[0], got[2], got[1], got[3:outs], got[outs:]


def pack_small_kernel(heads, n_ref, y_ref, one_ref, also_ref, two_ref, more_ref, buckets_ref, *refs):
    dists, (keep_ref, send_ref) = refs[:-2], refs[-2:]
    n = n_ref[0]
    odd = y_ref[0] == 1
    slot = buckets_ref.shape[1]
    total = dists[0][...]
    for ref in dists[1:]:
        total = total + ref[...]
    lanes = heads * BUCKETS
    bucket = lax.broadcasted_iota(jnp.int32, (lanes, slot), 0) % BUCKETS
    onehot = (buckets_ref[...] == bucket).astype(f32).astype(bf16)
    lane = lax.broadcasted_iota(jnp.int32, (1, lanes), 1)
    table = jnp.zeros((1, lanes), f32)
    for h in range(heads):
        row = jnp.broadcast_to(total[h // 2, h % 2 : h % 2 + 1], (8, slot))
        parts = []
        for _ in range(3):
            low = row.astype(bf16)
            parts.append(dot(low, onehot, NT))
            row = row - low.astype(f32)
        got = (parts[0] + parts[1] + parts[2])[0:1]
        table = jnp.where(lane // BUCKETS == h, got, table)
    zeros = jnp.zeros((1, TILE), f32)
    half = lanes // 2
    low = jnp.where(lane < half, table, 0.0)
    high = jnp.where(lane < half, pltpu.roll(table, half, 1), 0.0)
    for z in range(keep_ref.shape[0]):
        both = []
        for b, share in ((0, low), (1, high)):
            d = 2 * z + b
            cols = slice(d * TILE, (d + 1) * TILE)
            rel = jnp.where(d == 2 * n + b, share, zeros)
            both.append(
                jnp.concatenate(
                    [
                        one_ref[:, cols] + also_ref[:, cols],
                        two_ref[:, cols] + more_ref[:, cols],
                        rel,
                        zeros,
                        zeros,
                        zeros,
                    ],
                    axis=0,
                )
            )
        keep_ref[z] = jnp.where(odd, both[1], both[0])
        send_ref[z] = jnp.where(odd, both[0], both[1])


def pack_small(n, y, grad_one, grad_two, buckets, dists, heads):
    slot = buckets.shape[0]
    model = grad_one[0].shape[1]
    smem = pl.BlockSpec(memory_space=pltpu.SMEM)
    operands = [*grad_one, *grad_two, buckets.reshape(1, slot), *dists]
    shape = jax.ShapeDtypeStruct((model // TILE // 2, 8, TILE), f32)
    return pl.pallas_call(
        functools.partial(pack_small_kernel, heads),
        grid=(1,),
        in_specs=[smem, smem] + [block_of(x) for x in operands],
        out_specs=[pl.BlockSpec(shape.shape, lambda i: (0, 0, 0))] * 2,
        out_shape=[shape, shape],
        cost_estimate=cost(3),
        name="pack_small",
    )(n, y, *operands)


def join_ffn_kernel(quarter, n_ref, *refs):
    ins, (up_ref, down_ref) = refs[:4], refs[4:]
    model = down_ref.shape[1]
    rows = up_ref.shape[0]
    for r in range(4):
        j = lax.bitwise_xor(n_ref[0], r)
        for d in range(model // quarter):
            start = pl.multiple_of((d * 4 + j) * quarter, quarter)
            up_ref[:, pl.ds(start, quarter)] = ins[r][:, d * quarter : (d + 1) * quarter].astype(f32)
        down_ref[pl.ds(pl.multiple_of(j * quarter, quarter), quarter), :] = ins[r][:, model:].astype(f32)


def join_ffn(n, parts, quarter):
    rows, both = parts[0].shape
    model = both // 2
    shapes = [(rows, 4 * model), (4 * quarter, model)]
    if quarter % TILE:
        wide = model // quarter
        rel = jnp.stack(parts)
        rel = jnp.stack(
            [lax.dynamic_index_in_dim(rel, n[0] ^ j, 0, keepdims=False) for j in range(4)]
        ).astype(f32)
        up = rel[:, :, :model].reshape(4, rows, wide, quarter).transpose(1, 2, 0, 3)
        return up.reshape(shapes[0]), rel[:, :, model:].reshape(shapes[1])
    return pl.pallas_call(
        functools.partial(join_ffn_kernel, quarter),
        grid=(1,),
        in_specs=[pl.BlockSpec(memory_space=pltpu.SMEM)] + [block_of(x) for x in parts],
        out_specs=[pl.BlockSpec(x, lambda i: (0, 0)) for x in shapes],
        out_shape=[jax.ShapeDtypeStruct(x, f32) for x in shapes],
        compiler_params=pltpu.CompilerParams(vmem_limit_bytes=VMEM_LIMIT),
        cost_estimate=cost(4, 0.05),
        name="join_ffn",
    )(n, *parts)


def join_attn_kernel(n_ref, *refs):
    ins, (qkv_ref, out_ref) = refs[:4], refs[4:]
    model = out_ref.shape[1]
    mine = model // 4
    for r in range(4):
        j = lax.bitwise_xor(n_ref[0], r)
        at = 0
        for p in range(mine // PAIR):
            for part in range(3):
                start = pl.multiple_of(part * model + j * mine + p * PAIR, PAIR)
                qkv_ref[:, pl.ds(start, PAIR)] = ins[r][:, at : at + PAIR].astype(f32)
                at += PAIR
        out_ref[:, pl.ds(pl.multiple_of(j * mine, mine), mine)] = ins[r][
            :, at : at + mine
        ].astype(f32) + ins[r ^ 2][:, at + mine :].astype(f32)


def join_attn(n, parts, model):
    rows = parts[0].shape[0]
    shapes = [(rows, 3 * model), (rows, model)]
    return pl.pallas_call(
        join_attn_kernel,
        grid=(1,),
        in_specs=[pl.BlockSpec(memory_space=pltpu.SMEM)] + [block_of(x) for x in parts],
        out_specs=[pl.BlockSpec(x, lambda i: (0, 0)) for x in shapes],
        out_shape=[jax.ShapeDtypeStruct(x, f32) for x in shapes],
        cost_estimate=cost(3),
        name="join_attn",
    )(n, *parts)


def ring_order(size):
    return list(range(0, size, 2)) + list(range(size - 1, 0, -2))


def ring_member(pos, size):
    pos = lax.rem(pos + 2 * size, size)
    return jnp.where(pos < size // 2, 2 * pos, 2 * (size - 1 - pos) + 1)


def ring_pairs(narrow, size):
    order = ring_order(size)
    pairs = []
    for n in range(narrow):
        turn = 1 if n % 2 == 0 else -1
        for p in range(size):
            pairs.append((n * size + order[p], n * size + order[(p + turn) % size]))
    return pairs


class Places:
    def __init__(self):
        self.narrow = lax.axis_size("narrow")
        self.wide = lax.axis_size("wide")
        self.n = lax.axis_index("narrow")
        self.w = lax.axis_index("wide")
        self.core = lax.rem(self.n, 2)
        self.turn = 1 - 2 * self.core
        self.y = lax.rem(self.w, 2)
        self.z = self.w // 2
        self.pos = jnp.where(self.y == 0, self.z, self.wide - 1 - self.z)
        self.pairs = ring_pairs(self.narrow, self.wide)
        self.rings = self.wide <= 16

    def ring(self, x, way):
        pairs = self.pairs if way == 0 else [(b, a) for a, b in self.pairs]
        return lax.ppermute(x, ("narrow", "wide"), pairs)

    def member(self, steps):
        return ring_member(self.pos + self.turn * steps, self.wide)

    def swap(self, x, bit):
        return lax.ppermute(x, "narrow", [(i, i ^ bit) for i in range(self.narrow)])

    def all_narrow(self, x):
        far = self.swap(x, 2)
        return [x, self.swap(x, 1), far, self.swap(far, 1)]

    def swap_y(self, x):
        return lax.ppermute(x, "wide", [(i, i ^ 1) for i in range(self.wide)])

    def along_z(self, x, steps):
        return lax.ppermute(
            x, "wide", [(i, (i + 2 * steps) % self.wide) for i in range(self.wide)]
        )


def row_major(x):
    return with_layout_constraint(x, Layout(major_to_minor=tuple(range(x.ndim))))


def after(x, *deps):
    return lax.optimization_barrier((x, *deps))[0]


def add_low(*terms):
    return sum(t.astype(f32) for t in terms).astype(bf16)


def gather_ring(at, piece, holds):
    pieces, steps = [piece], [0]
    ahead = behind = piece
    far = at.wide // 2
    for k in range(1, far + 1):
        ahead = at.ring(ahead, 0)
        came = [ahead]
        if k < far:
            behind = at.ring(behind, 1)
            came.append(behind)
        held = holds[k](*came) if k in holds else ()
        came = lax.optimization_barrier((*came, *held))
        ahead = came[0]
        if k < far:
            behind = came[1]
            pieces.append(behind)
            steps.append(k)
        pieces.append(ahead)
        steps.append(-k)
    return pieces, steps


def reduce_ring(at, parts):
    size = at.wide

    def chunk(k):
        member = at.member(k)
        cut = [lax.dynamic_index_in_dim(p, member, 0, keepdims=False) for p in parts]
        return row_major(jnp.concatenate(cut, axis=1) if len(cut) > 1 else cut[0])

    far = size // 2
    ahead, behind = chunk(far), chunk(1 - far)
    yield ahead, behind
    for k in range(far - 1, 0, -1):
        ahead, behind = at.ring(ahead, 0), at.ring(behind, 1)
        held = yield ahead, behind
        ahead, behind, *_ = lax.optimization_barrier((ahead, behind, *(held or ())))
        ahead = row_major(add_low(ahead, chunk(k)))
        if k > 1:
            behind = row_major(add_low(behind, chunk(1 - k)))
        yield ahead, behind
    ahead = at.ring(ahead, 0)
    held = yield (ahead,)
    ahead, *_ = lax.optimization_barrier((ahead, *(held or ())))
    yield row_major(add_low(chunk(0), ahead, behind))


def scatter(at, parts):
    return jnp.concatenate(
        [lax.psum_scatter(p, "wide", scatter_dimension=0, tiled=True)[0] for p in parts], axis=1
    )


def local(
    tokens,
    lengths,
    buckets,
    ln1_gain,
    ln1_bias,
    w_qkv,
    rel_table,
    w_out,
    ln2_gain,
    ln2_bias,
    w_up,
    w_down,
    cotangent,
):
    at = Places()
    wide = at.wide
    slot, model = tokens.shape
    backwards = buckets.reshape(-1, TILE)[:, ::-1].reshape(slot)
    rows = w_qkv.shape[0]
    ff = w_up.shape[1]
    ff_rows = w_down.shape[0]
    quarter = ff_rows // 4
    heads = HEADS // 4
    width = 3 * model // 4
    rel_rows = rel_table.shape[0]
    n = at.n.reshape(1)
    far = wide // 2

    cut = slot // 16 * 7
    tokens_far = [at.swap(tokens[:cut], 2), at.swap(tokens[cut:], 2)]
    tokens_all = [[tokens], [at.swap(tokens, 1)], tokens_far, [at.swap(t, 1) for t in tokens_far]]

    lengths_far = at.swap(after(lengths, tokens_far[0]), 2)
    lengths_all = [lengths, at.swap(lengths, 1), lengths_far, at.swap(lengths_far, 1)]

    vectors = [ln1_gain, ln1_bias, ln2_gain, ln2_bias, rel_table]
    vectors = jnp.stack([jnp.pad(s, (0, TILE - s.shape[0])) for s in vectors])
    vectors = jnp.pad(vectors, ((0, 16 - vectors.shape[0]), (0, 0)))
    if at.rings:
        attn_piece = cut_attn(n, w_qkv, w_out, vectors)
        ffn_piece = cut_ffn(n, after(w_up, attn_piece), w_down)
        came, xhats = [], []

        def hold(x, *deps):
            xhats.append(xhat_of([after(t, *deps) for t in x]))
            return xhats[-1]

        pieces, steps = gather_ring(
            at,
            attn_piece,
            {
                1: lambda *x: [ffn_piece, tokens_far[0]],
                2: lambda *x: [
                    lengths_far,
                    tokens_far[1],
                    hold(tokens_all[0], *x),
                    hold(tokens_all[1], *x),
                ],
                3: lambda *x: came.extend(x) or lengths_all[1::2],
            },
        )
        hold(tokens_all[2], *came)
        hold(tokens_all[3], *came)
        ffn_piece = after(ffn_piece, *came)
        where = jnp.stack([at.member(k) for k in steps])
        small = small_rows(where, pieces, model)
    else:
        pick = lambda x, axis: lax.dynamic_index_in_dim(x, at.n, axis, keepdims=False)
        cut = pick(w_qkv.reshape(rows, 3, 4, heads // 2, PAIR), 2)
        cut = cut.transpose(0, 2, 1, 3).reshape(rows, width)
        cut = [cut, pick(w_out.reshape(rows, 4, model // 4), 1), jnp.zeros((rows, TILE), bf16)]
        attn_piece = jnp.concatenate(cut, axis=1)
        ffn_piece = jnp.stack(
            [
                pick(w_up.reshape(rows, wide, 4, quarter), 2).reshape(rows, wide * quarter),
                pick(w_down.reshape(4, quarter, model), 0),
            ]
        )
        pieces = [lax.all_gather(attn_piece, "wide", axis=0, tiled=True)]
        where = jnp.zeros((1,), jnp.int32)
        small = lax.all_gather(vectors, "wide", axis=0).astype(f32)
        small = [small[:, i, :rows].reshape(1, model) for i in range(4)] + [
            jnp.pad(small[:, 4, :rel_rows].reshape(1, -1), ((0, 0), (0, model - HEADS * BUCKETS)))
        ]
        small = jnp.pad(jnp.concatenate(small, axis=0), ((0, 3), (0, 0)))
    w_ffn = lax.all_gather(ffn_piece, "wide", axis=0)

    if not at.rings:
        xhats = [xhat_of(t) for t in tokens_all]
    valid = (jnp.arange(slot, dtype=jnp.int32) < lengths[0]).astype(f32)[:, None]
    cotan = cotangent.astype(f32)
    grad_ffn = at.all_narrow(after((valid * cotan).astype(bf16), xhats[2]))
    half = slot // 2
    norm_one, packed, wqkv, wout = qkv_of(where, small, xhats, pieces, width)
    wouts = at.all_narrow(wout)
    tiles = bias_tiles(n, small, buckets, heads)
    atts, probs = [None] * 4, [None] * 4
    for r in (3, 2, 1, 0):
        length = after(lengths_all[r], *grad_ffn[1:]) if r == 0 else lengths_all[r]
        atts[r], probs[r] = attn_fwd(length, packed, tiles, r)
    attended = [atts[0]] + [at.swap(atts[r], r) for r in (1, 2, 3)]
    whole, norm_two, norm_far = [], [], []
    for i in range(2):
        *whole, norm = out_ln2(n, lengths, tokens, small, attended, wouts, i, whole)
        norm_two.append(norm)
        norm_far.append(at.swap(norm, 2))
    middle, attended = whole

    norm_near = norm_two + [at.swap(x, 1) for x in norm_two]
    o0, o1, gn0, gn1, rows_all = ffn(
        norm_near, grad_ffn[:2], [(0, slot)] * 2, w_ffn, 0, [], 4
    )
    gn_near = [at.swap(x, 1) for x in gn1]

    def chip_sum(p2, p3):
        return add_low(p2, jnp.concatenate([at.swap(x, 1) for x in p3], axis=0))

    cuts = 4
    gn_far, o_far, gn_back = [], [], []
    for i in range(2):
        norms = after(norm_far[i], gn2 if i else gn0)
        cut = half // cuts
        norms = [norms] + [at.swap(norms[j : j + cut], 1) for j in range(0, half, cut)]
        norms[0] = after(norms[0], *gn_far)
        o2, o3, gn2, gn3, rows_all = ffn(
            norms, grad_ffn[2:], [(i * half, half)] * 2, w_ffn, 2 * slot + i * slot, rows_all, cuts
        )
        gn_far.append(chip_sum(gn2, gn3))
        o_far.append((o2, o3))
        gn_back.append(at.swap(gn_far[i], 2))
    norms, grads, hid, gua = rows_all
    gu = dot(norms, after(gua, gn_back[0], *gn_far), TN).astype(bf16)
    gd = dot(hid, after(grads, gn_back[0], *gn_far), TN).astype(bf16)
    shape = (wide, rows, model)
    if at.rings:
        turns = reduce_ring(at, [gu.reshape(shape), gd.reshape(shape)])
        next(turns)

    whole, grad_two = [], []
    for i in range(2):
        near = gn_near[2 * i : 2 * i + 2]
        *whole, vec = ln2_back(
            n, lengths, middle, cotangent, small, gn0, near, gn_back[i], wouts, i, whole
        )
        grad_two.append(vec)
    grad_middle, branch_keep, branch_send, *grad_att = whole
    if at.rings:
        next(turns)
        grad_att[0] = after(grad_att[0], *next(turns))
    grad_att = [grad_att[0]] + [at.swap(grad_att[r], r) for r in (1, 2, 3)]
    grad_packed, dists = None, []

    def backward(r, *deps):
        ga = after(grad_att[r], *deps) if deps else grad_att[r]
        return attn_bwd(packed, ga, atts[r], probs[r], r, grad_packed)

    def turned():
        return list(next(turns)) if at.rings else []

    def turn_after(*deps):
        if at.rings:
            turns.send(list(deps))

    grad_packed, dist = backward(0)
    dists.append(dist)
    attended = after(attended, dist, *grad_att[2:])
    out_send = dot(attended, branch_send, TN).astype(bf16)
    out_keep = dot(attended, branch_keep, TN).astype(bf16)
    o_far = [chip_sum(after(x, dist), [after(y, dist)]) for x, y in o_far]
    out_back = [at.swap(o_far[0], 2)]
    grad_packed, dist = backward(2, out_send, out_keep, *turned())
    turn_after(grad_att[2])
    dists.append(dist)
    out_sum = add_low(out_keep, at.swap(out_send, 1))
    grad_packed, dist = backward(3, out_sum)
    dists.append(dist)
    p2, p3, more_one = ln1_back(after(grad_packed, out_back[0], *turned()), wqkv, xhats[2:], 2)
    turn_after(p3)
    p_far = chip_sum(p2, [p3])
    p_back = [at.swap(p_far[:half], 2)]
    grad_packed, dist = backward(1, p_far)
    dists.append(dist)
    grad_qkv = dot(norm_one, after(grad_packed, p_back[0]), TN).astype(bf16)
    parts = [grad_qkv.reshape(wide, rows, width), out_sum.reshape(wide, rows, model // 2)]
    if at.rings:
        next(turns)
        ffn_own = turns.send([dist])
        turns = reduce_ring(at, parts)
        grad_packed = after(grad_packed, *next(turns))
    else:
        ffn_own = scatter(at, [gu.reshape(shape), gd.reshape(shape)])
        attn_own = scatter(at, parts)
    ffn_all = at.all_narrow(after(ffn_own, p_back[0]))
    p_back.append(at.swap(after(p_far[half:], ffn_all[2]), 2))
    out_back.append(at.swap(after(o_far[1], p_back[1]), 2))

    p0, p1, grad_one = ln1_back(grad_packed, wqkv, xhats[:2], 0)
    grad_one = [grad_one, more_one]
    p_near = at.swap(p1, 1)
    up_full, down_full = join_ffn(n, ffn_all, quarter)
    if at.rings:
        keep, send = pack_small(n, at.y.reshape(1), grad_one, grad_two, backwards, dists, heads)
        next(turns)
        sent = turns.send([p1, keep, ffn_all[2]])
        smalls = keep + at.swap_y(after(send, *sent))
        next(turns)
        sent = turns.send([p_back[1], up_full])
        p0 = after(p0, *sent)
    grad_tokens = ln1_last(tokens, xhats[0], grad_middle, small, p0, p_near, *p_back)

    outs = [o0, at.swap(o1, 1), jnp.concatenate(out_back, axis=0)]
    if at.rings:
        next(turns)
        sent = turns.send([grad_tokens, out_back[1], smalls])
        smalls, outs[0] = after(smalls, *sent), after(o0, *sent)
        pick = lambda i: lax.dynamic_index_in_dim(smalls, i, 0, keepdims=False)
        z_parts = [pick(at.z)] + [
            at.along_z(pick(lax.rem(at.z + k, far)), k) for k in range(1, far)
        ]
    output = (middle + valid * sum(p.astype(f32) for p in outs)).astype(bf16)
    if at.rings:
        next(turns)
        attn_own = turns.send([output])
        smalls = after(z_parts[0], attn_own) + sum(z_parts[1:])

    if not at.rings:
        onehot = (backwards[:, None] == jnp.arange(BUCKETS, dtype=jnp.int32)[None, :]).astype(f32)
        table = jnp.dot(sum(dists).reshape(heads, slot), onehot, precision=lax.Precision.HIGHEST)
        table = lax.dynamic_update_slice(
            jnp.zeros((4, heads * BUCKETS), f32), table.reshape(1, -1), (at.n, 0)
        )
        two = grad_two[0] + grad_two[1]
        one = grad_one[0] + grad_one[1]
        smalls = [one[0], one[1], two[0], two[1], table]
        smalls = [g.reshape(wide, 1, -1) for g in smalls]
        smalls = [jnp.pad(g, ((0, 0), (0, 0), (0, TILE - g.shape[2]))) for g in smalls]
        smalls = jnp.concatenate(smalls + [jnp.zeros((wide, 3, TILE), f32)], axis=1)
        smalls = lax.psum_scatter(smalls, "wide", scatter_dimension=0, tiled=True)[0]
    smalls = smalls + at.swap(smalls, 2)
    smalls = smalls + at.swap(smalls, 1)

    qkv_full, out_full = join_attn(n, at.all_narrow(attn_own), model)

    return (
        output,
        grad_tokens,
        smalls[0, :rows],
        smalls[1, :rows],
        qkv_full,
        smalls[4, :rel_rows],
        out_full,
        smalls[2, :rows],
        smalls[3, :rows],
        up_full,
        down_full,
    )


def solution(mesh):
    return jax.shard_map(
        local,
        mesh=mesh,
        in_specs=(
            P(("narrow", "wide"), None),
            P(("narrow", "wide")),
            P(),
            P("wide"),
            P("wide"),
            P("wide", None),
            P("wide"),
            P("wide", None),
            P("wide"),
            P("wide"),
            P("wide", None),
            P("wide", None),
            P(("narrow", "wide"), None),
        ),
        out_specs=(
            P(("narrow", "wide"), None),
            P(("narrow", "wide"), None),
            P("wide"),
            P("wide"),
            P("wide", None),
            P("wide"),
            P("wide", None),
            P("wide"),
            P("wide"),
            P("wide", None),
            P("wide", None),
        ),
        check_vma=False,
    )
```

```python
import functools

import jax
import jax.numpy as jnp
from jax import lax
from jax.experimental import pallas as pl
from jax.experimental.layout import Layout, with_layout_constraint
from jax.experimental.pallas import tpu as pltpu
from jax.sharding import PartitionSpec as P

HEADS = 16
HEAD_DIM = 64
BUCKETS = 32
TILE = 128
PAIR = 2 * HEAD_DIM

norm_eps = 1e-05
neg_large = -1e30
f32 = jnp.float32
bf16 = jnp.bfloat16
VMEM_LIMIT = 56 * 1024 * 1024


PEAK = 1.15e15


def cost(us, share=1.0):
    return pl.CostEstimate(flops=int(us * share * 1e-6 * PEAK), bytes_accessed=0, transcendentals=0)


def dot(a, b, dims=((1,), (0,))):
    return lax.dot_general(a, b, (dims, ((), ())), preferred_element_type=f32)


NT = ((1,), (1,))
TN = ((0,), (0,))


def block_of(x):
    zeros = (0,) * x.ndim
    return pl.BlockSpec(x.shape, lambda i: zeros)


def cut_attn_kernel(n_ref, qkv_ref, out_ref, small_ref, o_ref):
    n = n_ref[0]
    model = out_ref.shape[1]
    mine = model // 4
    at = 0
    for p in range(mine // PAIR):
        for part in range(3):
            start = pl.multiple_of(part * model + n * mine + p * PAIR, PAIR)
            o_ref[:, at : at + PAIR] = qkv_ref[:, pl.ds(start, PAIR)]
            at += PAIR
    o_ref[:, at : at + mine] = out_ref[:, pl.ds(pl.multiple_of(n * mine, mine), mine)]
    at += mine
    o_ref[:, at:] = jnp.zeros((o_ref.shape[0], TILE), bf16)
    o_ref[:16, at:] = small_ref[...]


def cut_attn(n, w_qkv, w_out, small):
    rows, model = w_out.shape
    return pl.pallas_call(
        cut_attn_kernel,
        grid=(1,),
        in_specs=[pl.BlockSpec(memory_space=pltpu.SMEM)]
        + [block_of(x) for x in (w_qkv, w_out, small)],
        out_specs=pl.BlockSpec((rows, model + TILE), lambda i: (0, 0)),
        out_shape=jax.ShapeDtypeStruct((rows, model + TILE), bf16),
        cost_estimate=cost(2),
        name="cut_attn",
    )(n, w_qkv, w_out, small)


def cut_ffn_kernel(n_ref, up_ref, down_ref, o_ref):
    n = n_ref[0]
    size = down_ref.shape[0]
    model = down_ref.shape[1]
    for d in range(model // size):
        start = pl.multiple_of(d * 4 * size + n * size, size)
        o_ref[0, :, d * size : (d + 1) * size] = up_ref[:, pl.ds(start, size)]
    o_ref[1] = down_ref[...]


def cut_ffn(n, w_up, w_down):
    rows = w_up.shape[0]
    quarter, model = w_down.shape[0] // 4, w_down.shape[1]
    return pl.pallas_call(
        cut_ffn_kernel,
        grid_spec=pltpu.PrefetchScalarGridSpec(
            num_scalar_prefetch=1,
            grid=(1,),
            in_specs=[
                pl.BlockSpec(w_up.shape, lambda i, n: (0, 0)),
                pl.BlockSpec((quarter, model), lambda i, n: (n[0], 0)),
            ],
            out_specs=pl.BlockSpec((2, rows, model), lambda i, n: (0, 0, 0)),
        ),
        out_shape=jax.ShapeDtypeStruct((2, rows, model), bf16),
        cost_estimate=cost(2, 0.05),
        name="cut_ffn",
    )(n, w_up, w_down)


def small_kernel(where_ref, *refs):
    out_ref = refs[-1]
    out_ref[...] = jnp.zeros_like(out_ref)
    lane = lax.broadcasted_iota(jnp.int32, (1, TILE), 1)
    for i, ref in enumerate(refs[:-1]):
        d = where_ref[i]
        got = ref[...].astype(f32)
        start = pl.multiple_of(d * TILE, TILE)
        for v in range(4):
            out_ref[v : v + 1, pl.ds(start, TILE)] = got[v : v + 1]
        rel = got[4:5]
        odd = lax.rem(d, 2) == 1
        rel = jnp.where(odd, pltpu.roll(rel, TILE // 2, 1), rel)
        rel = jnp.where((lane >= TILE // 2) == odd, rel, 0.0)
        start = pl.multiple_of((d // 2) * TILE, TILE)
        out_ref[4:5, pl.ds(start, TILE)] += rel


def small_rows(where, pieces, at):
    model = len(pieces) * TILE
    return pl.pallas_call(
        small_kernel,
        grid=(1,),
        in_specs=[pl.BlockSpec(memory_space=pltpu.SMEM)]
        + [pl.BlockSpec((16, TILE), lambda i: (0, at // TILE))] * len(pieces),
        out_specs=pl.BlockSpec((8, model), lambda i: (0, 0)),
        out_shape=jax.ShapeDtypeStruct((8, model), f32),
        cost_estimate=cost(2),
        name="small_rows",
    )(where, *pieces)


def tiles_kernel(n_ref, small_ref, buckets_ref, out_ref):
    heads, count = out_ref.shape[:2]
    lanes = heads * BUCKETS
    slot = buckets_ref.shape[1]
    rel = small_ref[4:5, pl.ds(pl.multiple_of(n_ref[0] * lanes, lanes), lanes)]
    head = lax.broadcasted_iota(jnp.int32, (8, lanes), 0)
    lane = lax.broadcasted_iota(jnp.int32, (8, lanes), 1)
    table = jnp.where(lane // BUCKETS == head, rel, 0.0).astype(bf16)
    bucket = lax.broadcasted_iota(jnp.int32, (lanes, slot), 0) % BUCKETS
    onehot = (buckets_ref[...] == bucket).astype(f32).astype(bf16)
    by_distance = dot(table, onehot)
    row = lax.broadcasted_iota(jnp.int32, (TILE, TILE), 0)
    col = lax.broadcasted_iota(jnp.int32, (TILE, TILE), 1)
    for h in range(heads):
        for delta in range(count):
            here = by_distance[h : h + 1, delta * TILE : (delta + 1) * TILE]
            below = by_distance[h : h + 1, max(delta - 1, 0) * TILE : max(delta, 1) * TILE]
            wide = jnp.broadcast_to(jnp.concatenate([here, below], axis=1), (TILE, 2 * TILE))
            tile = pltpu.roll(wide, 0, 1, stride=1, stride_axis=0)[:, :TILE].T
            if delta == 0:
                tile = jnp.where(col <= row, tile, neg_large)
            out_ref[h, delta] = tile


def bias_tiles(n, small, buckets, heads):
    slot = buckets.shape[0]
    buckets = buckets.reshape(1, slot)
    shape = (heads, slot // TILE, TILE, TILE)
    return pl.pallas_call(
        tiles_kernel,
        grid=(1,),
        in_specs=[pl.BlockSpec(memory_space=pltpu.SMEM), block_of(small), block_of(buckets)],
        out_specs=pl.BlockSpec(shape, lambda i: (0, 0, 0, 0)),
        out_shape=jax.ShapeDtypeStruct(shape, f32),
        cost_estimate=cost(4),
        name="bias_tiles",
    )(n, small, buckets)


def normalized(v):
    center = v - jnp.mean(v, axis=-1, keepdims=True)
    factor = lax.rsqrt(jnp.mean(center * center, axis=-1, keepdims=True) + norm_eps)
    return center * factor, factor


def xhat_kernel(*refs):
    out_ref = refs[-1]
    at = 0
    for ref in refs[:-1]:
        rows = ref.shape[0]
        out_ref[at : at + rows] = normalized(ref[...].astype(f32))[0]
        at += rows


def xhat_of(pieces):
    slot, model = sum(p.shape[0] for p in pieces), pieces[0].shape[1]
    return pl.pallas_call(
        xhat_kernel,
        grid=(1,),
        in_specs=[block_of(p) for p in pieces],
        out_specs=pl.BlockSpec((slot, model), lambda i: (0, 0)),
        out_shape=jax.ShapeDtypeStruct((slot, model), f32),
        compiler_params=pltpu.CompilerParams(vmem_limit_bytes=VMEM_LIMIT),
        cost_estimate=cost(2.5, 0.05),
        name="xhat",
    )(*pieces)


def qkv_kernel(count, where_ref, small_ref, *refs):
    xhats, pieces = refs[:4], refs[4 : 4 + count]
    norm_ref, packed_ref, wq_ref, wo_ref, w_ref, x_ref, sems, x_sems = refs[4 + count :]
    step = pl.program_id(0)
    width = wq_ref.shape[1]

    def fetch(r):
        return pltpu.make_async_copy(xhats[r], x_ref.at[r % 2], x_sems.at[r % 2])

    @pl.when(step == 0)
    def _():
        fetch(0).start()
        copies = []
        for i, piece in enumerate(pieces):
            size = piece.shape[0]
            start = pl.multiple_of(where_ref[i] * size, size)
            copies.append(pltpu.make_async_copy(piece, w_ref.at[pl.ds(start, size)], sems.at[i]))
            copies[-1].start()
        for copy in copies:
            copy.wait()
        wq_ref[...] = w_ref[:, :width]
        wo_ref[...] = w_ref[:, width : width + wo_ref.shape[1]]

    for r in range(4):

        @pl.when(step == r)
        def _(r=r):
            if r < 3:
                fetch(r + 1).start()
            fetch(r).wait()

    norm = (x_ref[lax.rem(step, 2)] * small_ref[0:1] + small_ref[1:2]).astype(bf16)
    norm_ref[...] = norm
    packed_ref[...] = dot(norm, wq_ref[...]).astype(bf16)


def qkv_of(where, small, xhats, pieces, width):
    slot, model = xhats[0].shape
    total = pieces[0].shape[1]
    out = model // 4
    whole = lambda shape: pl.BlockSpec(shape, lambda i: (0, 0))
    rows = lambda cols: pl.BlockSpec((slot, cols), lambda i: (i, 0))
    return pl.pallas_call(
        functools.partial(qkv_kernel, len(pieces)),
        grid=(4,),
        in_specs=[pl.BlockSpec(memory_space=pltpu.SMEM), whole(small.shape)]
        + [pl.BlockSpec(memory_space=pl.ANY)] * (4 + len(pieces)),
        out_specs=[rows(model), rows(width), whole((model, width)), whole((model, out))],
        out_shape=[
            jax.ShapeDtypeStruct((4 * slot, model), bf16),
            jax.ShapeDtypeStruct((4 * slot, width), bf16),
            jax.ShapeDtypeStruct((model, width), bf16),
            jax.ShapeDtypeStruct((model, out), bf16),
        ],
        scratch_shapes=[
            pltpu.VMEM((model, total), bf16),
            pltpu.VMEM((2, slot, model), f32),
            pltpu.SemaphoreType.DMA((len(pieces),)),
            pltpu.SemaphoreType.DMA((2,)),
        ],
        compiler_params=pltpu.CompilerParams(vmem_limit_bytes=VMEM_LIMIT),
        cost_estimate=cost(7, 0.05),
        name="qkv",
    )(where, small, *xhats, *pieces)


def ln1_back_kernel(gp_ref, wq_ref, x0_ref, x1_ref, p0_ref, p1_ref, vec_ref):
    step = pl.program_id(0)
    grad = dot(gp_ref[...], wq_ref[...], NT)

    @pl.when(step == 0)
    def _():
        vec_ref[0:1] = jnp.sum(grad * x0_ref[...], axis=0, keepdims=True)
        vec_ref[1:2] = jnp.sum(grad, axis=0, keepdims=True)
        p0_ref[...] = grad.astype(p0_ref.dtype)

    @pl.when(step == 1)
    def _():
        vec_ref[0:1] += jnp.sum(grad * x1_ref[...], axis=0, keepdims=True)
        vec_ref[1:2] += jnp.sum(grad, axis=0, keepdims=True)
        p1_ref[...] = grad.astype(p1_ref.dtype)


def ln1_back(grad_packed, wqkv, xhats, first):
    slot, model = xhats[0].shape
    width = wqkv.shape[1]
    whole = lambda shape: pl.BlockSpec(shape, lambda i: (0, 0))
    return pl.pallas_call(
        ln1_back_kernel,
        grid=(2,),
        in_specs=[
            pl.BlockSpec((slot, width), lambda i: (first + i, 0)),
            whole((model, width)),
            whole((slot, model)),
            whole((slot, model)),
        ],
        out_specs=[whole((slot, model)), whole((slot, model)), whole((2, model))],
        out_shape=[
            jax.ShapeDtypeStruct((slot, model), bf16 if first else f32),
            jax.ShapeDtypeStruct((slot, model), bf16),
            jax.ShapeDtypeStruct((2, model), f32),
        ],
        compiler_params=pltpu.CompilerParams(vmem_limit_bytes=VMEM_LIMIT),
        cost_estimate=cost(5, 0.1 if first else 1.0),
        name="ln1_back",
    )(grad_packed, wqkv, *xhats)


def attn_fwd_kernel(len_ref, qkv_ref, tiles_ref, att_ref, p_ref):
    slot = qkv_ref.shape[0]
    blocks = range(slot // TILE)
    heads = range(2)
    length = len_ref[0]
    lane = lax.broadcasted_iota(jnp.int32, (1, PAIR), 1)
    col = lax.broadcasted_iota(jnp.int32, (1, slot), 1)
    hidden = jnp.where(col < length, 0.0, neg_large)
    q = qkv_ref[:, :PAIR] * HEAD_DIM ** (-0.5)
    k = qkv_ref[:, PAIR : 2 * PAIR]
    v = qkv_ref[:, 2 * PAIR :]
    own = [(lane // HEAD_DIM) == hh for hh in heads]
    qm = [jnp.where(own[hh], q, jnp.zeros_like(q)) for hh in heads]
    span = [(i + 1) * TILE for i in blocks]
    items = [(hh, i) for hh in heads for i in blocks]
    s = [dot(qm[hh][i * TILE : span[i]], k[: span[i]], NT) for hh, i in items]
    s = [
        x + jnp.concatenate([tiles_ref[hh, i - j] for j in range(i + 1)], axis=1) + hidden[:, : span[i]]
        for x, (hh, i) in zip(s, items)
    ]
    top = [jnp.max(x, axis=1, keepdims=True) for x in s]
    e = [jnp.exp(x - m) for x, m in zip(s, top)]
    scale = [1.0 / jnp.sum(x, axis=1, keepdims=True) for x in e]
    probs = [(x * r).astype(bf16) for x, r in zip(e, scale)]
    for x, (hh, i) in zip(probs, items):
        p_ref[hh, i * TILE : span[i], : span[i]] = x
    o = {item: dot(x, v[: span[item[1]]]) for x, item in zip(probs, items)}
    for i in blocks:
        att_ref[i * TILE : span[i], :] = jnp.where(own[0], o[0, i], o[1, i]).astype(bf16)


def attn_fwd(lengths, packed, tiles, seq):
    heads, count = tiles.shape[:2]
    slot = count * TILE
    return pl.pallas_call(
        attn_fwd_kernel,
        grid=(heads // 2,),
        in_specs=[
            pl.BlockSpec(memory_space=pltpu.SMEM),
            pl.BlockSpec((slot, 3 * PAIR), lambda p: (seq, p)),
            pl.BlockSpec((2, count, TILE, TILE), lambda p: (p, 0, 0, 0)),
        ],
        out_specs=[
            pl.BlockSpec((slot, PAIR), lambda p: (0, p)),
            pl.BlockSpec((2, slot, slot), lambda p: (p, 0, 0)),
        ],
        out_shape=[
            jax.ShapeDtypeStruct((slot, heads * HEAD_DIM), bf16),
            jax.ShapeDtypeStruct((heads, slot, slot), bf16),
        ],
        compiler_params=pltpu.CompilerParams(vmem_limit_bytes=VMEM_LIMIT),
        cost_estimate=cost(4.5, 0.1),
        name="attn_fwd",
    )(lengths, packed, tiles)


def attn_bwd_kernel(qkv_ref, ga_ref, att_ref, p_ref, *refs):
    g_ref, sum_ref, ds_ref = refs[-3:]
    slot = qkv_ref.shape[0]
    blocks = range(slot // TILE)
    heads = range(2)
    lane = lax.broadcasted_iota(jnp.int32, (1, PAIR), 1)
    scale = HEAD_DIM ** (-0.5)
    q = qkv_ref[:, :PAIR] * scale
    k = qkv_ref[:, PAIR : 2 * PAIR]
    v = qkv_ref[:, 2 * PAIR :]
    ga = ga_ref[...]
    prod = ga.astype(f32) * att_ref[...].astype(f32)
    own = [(lane // HEAD_DIM) == hh for hh in heads]
    gam = [jnp.where(own[hh], ga, jnp.zeros_like(ga)) for hh in heads]
    inner = [jnp.sum(jnp.where(own[hh], prod, 0.0), axis=1, keepdims=True) for hh in heads]
    span = [(i + 1) * TILE for i in blocks]
    rows = [slice(i * TILE, span[i]) for i in blocks]
    items = [(hh, i) for hh in heads for i in blocks]
    dp = [dot(gam[hh][rows[i]], v[: span[i]], NT) for hh, i in items]
    ds = {
        (hh, i): (p_ref[hh, rows[i], : span[i]].astype(f32) * (x - inner[hh][rows[i]])).astype(bf16)
        for x, (hh, i) in zip(dp, items)
    }
    for hh, i in items:
        ds_ref[hh, rows[i], : span[i]] = ds[hh, i]
    dq = {(hh, i): dot(ds[hh, i], k[: span[i]]) for hh, i in items}
    dv = {(hh, j): dot(p_ref[hh, j * TILE :, rows[j]], ga[j * TILE :], TN) for hh, j in items}
    dk = {(hh, j): dot(ds_ref[hh, j * TILE :, rows[j]], q[j * TILE :], TN) for hh, j in items}
    for i in blocks:
        for at, got, factor in ((0, dq, scale), (PAIR, dk, 1.0), (2 * PAIR, dv, 1.0)):
            both = jnp.where(own[0], got[0, i], got[1, i]) * factor
            g_ref[rows[i], at : at + PAIR] = both.astype(bf16)
    row = lax.broadcasted_iota(jnp.int32, (TILE, TILE), 0)
    col = lax.broadcasted_iota(jnp.int32, (TILE, TILE), 1)
    flip = jnp.where(row + col == TILE - 1, 1.0, 0.0).astype(bf16)
    diag = {}
    for hh in heads:
        for delta in blocks:
            parts = [
                ds[hh, i][:, (i - delta) * TILE : (i - delta + 1) * TILE].astype(f32)
                for i in blocks
                if i >= delta
            ]
            diag[hh, delta] = functools.reduce(jnp.add, parts)
    high = {key: x.astype(bf16) for key, x in diag.items()}
    low = {key: (x - high[key].astype(f32)).astype(bf16) for key, x in diag.items()}
    turned = {key: dot(flip, high[key]) + dot(flip, low[key]) for key in diag}
    sums = {}
    for key, x in turned.items():
        wide = jnp.concatenate([x, jnp.zeros_like(x)], axis=1)
        wide = pltpu.roll(wide, 0, 1, stride=1, stride_axis=0)
        sums[key] = jnp.sum(wide, axis=0, keepdims=True)
    for hh in heads:
        for delta in blocks:
            here = sums[hh, delta][:, :TILE]
            if delta + 1 in blocks:
                here = here + sums[hh, delta + 1][:, TILE:]
            sum_ref[0, hh : hh + 1, rows[delta]] = here


def attn_bwd(packed, ga, att, probs, seq, into):
    heads, slot = probs.shape[:2]
    steps = heads // 2
    return pl.pallas_call(
        attn_bwd_kernel,
        grid=(steps,),
        in_specs=[
            pl.BlockSpec((slot, 3 * PAIR), lambda p: (seq, p)),
            pl.BlockSpec((slot, PAIR), lambda p: (0, p)),
            pl.BlockSpec((slot, PAIR), lambda p: (0, p)),
            pl.BlockSpec((2, slot, slot), lambda p: (p, 0, 0)),
        ]
        + ([] if into is None else [pl.BlockSpec(memory_space=pl.ANY)]),
        out_specs=[
            pl.BlockSpec((slot, 3 * PAIR), lambda p: (seq, p)),
            pl.BlockSpec((1, 2, slot), lambda p: (p, 0, 0)),
        ],
        out_shape=[
            jax.ShapeDtypeStruct(packed.shape, bf16),
            jax.ShapeDtypeStruct((steps, 2, slot), f32),
        ],
        scratch_shapes=[pltpu.VMEM((2, slot, slot), bf16)],
        input_output_aliases={} if into is None else {4: 0},
        compiler_params=pltpu.CompilerParams(vmem_limit_bytes=VMEM_LIMIT),
        cost_estimate=cost(5, 0.2),
        name="attn_bwd",
    )(packed, ga, att, probs, *(() if into is None else (into,)))


def ln1_last_kernel(tok_ref, xhat_ref, gmid_ref, small_ref, p0_ref, p1_ref, p2_ref, p3_ref, out_ref):
    _, factor = normalized(tok_ref[...].astype(f32))
    xhat = xhat_ref[...]
    low = pl.program_id(0) == 0
    e = p0_ref[...] + p1_ref[...].astype(f32) + jnp.where(low, p2_ref[...], p3_ref[...]).astype(f32)
    e = e * small_ref[0:1]
    out_ref[...] = gmid_ref[...] + factor * (
        e - jnp.mean(e, axis=-1, keepdims=True) - xhat * jnp.mean(e * xhat, axis=-1, keepdims=True)
    )


def ln1_last(tokens, xhat, grad_middle, small, p0, p1, p2, p3):
    slot, model = tokens.shape
    row = pl.BlockSpec((slot // 2, model), lambda i: (i, 0))
    part = pl.BlockSpec((slot // 2, model), lambda i: (0, 0))
    return pl.pallas_call(
        ln1_last_kernel,
        grid=(2,),
        in_specs=[row] * 3 + [block_of(small), row, row, part, part],
        out_specs=row,
        out_shape=jax.ShapeDtypeStruct((slot, model), f32),
        compiler_params=pltpu.CompilerParams(vmem_limit_bytes=VMEM_LIMIT),
        cost_estimate=cost(5, 0.05),
        name="ln1_last",
    )(tokens, xhat, grad_middle, small, p0, p1, p2, p3)


def quarters(n, r, size):
    return pl.ds(pl.multiple_of(lax.bitwise_xor(n, r) * size, size), size)


def out_ln2_kernel(part, n_ref, len_ref, tok_ref, small_ref, *refs):
    atts, wouts = refs[:4], refs[4:8]
    mid_ref, all_ref, norm_ref = refs[-3:]
    n = n_ref[0]
    rows, model = tok_ref.shape
    size = model // 4
    for r in range(4):
        all_ref[:, quarters(n, r, size)] = atts[r][...]
    valid = part * rows + lax.broadcasted_iota(jnp.int32, (rows, 1), 0) < len_ref[0]
    for r in range(4):
        cols = quarters(n, r, size)
        out = dot(all_ref[...], wouts[r][...])
        mid_ref[:, cols] = tok_ref[:, cols].astype(f32) + jnp.where(valid, out, 0.0)
    xhat, _ = normalized(mid_ref[...])
    norm_ref[...] = (xhat * small_ref[2:3] + small_ref[3:4]).astype(bf16)


def out_ln2(n, length, tokens, small, atts, wouts, part, into):
    slot, model = tokens.shape
    smem = pl.BlockSpec(memory_space=pltpu.SMEM)
    whole = lambda x: pl.BlockSpec(x.shape, lambda i: (0, 0))
    rows = lambda cols: pl.BlockSpec((slot // 2, cols), lambda i: (part, 0))
    return pl.pallas_call(
        functools.partial(out_ln2_kernel, part),
        grid=(1,),
        in_specs=[smem, smem, rows(model), whole(small)]
        + [rows(model // 4)] * 4
        + [whole(w) for w in wouts]
        + [pl.BlockSpec(memory_space=pl.ANY)] * len(into),
        out_specs=[rows(model), rows(model), pl.BlockSpec((slot // 2, model), lambda i: (0, 0))],
        out_shape=[
            jax.ShapeDtypeStruct((slot, model), f32),
            jax.ShapeDtypeStruct((slot, model), bf16),
            jax.ShapeDtypeStruct((slot // 2, model), bf16),
        ],
        input_output_aliases={12 + i: i for i in range(len(into))},
        compiler_params=pltpu.CompilerParams(vmem_limit_bytes=VMEM_LIMIT),
        cost_estimate=cost(4, 1 / 64),
        name="out_ln2",
    )(n, length, tokens, small, *atts, *wouts, *into)


def ln2_back_kernel(part, n_ref, len_ref, mid_ref, cot_ref, small_ref, p0_ref, p2_ref, *refs):
    near, wouts = refs[:2], refs[2:6]
    gmid_ref, keep_ref, send_ref = refs[-9:-6]
    gatts = refs[-6:-2]
    vec_ref, branch_ref = refs[-2:]
    n = n_ref[0]
    rows, model = mid_ref.shape
    size = model // 4
    xhat, factor = normalized(mid_ref[...])
    grad = p0_ref[...] + p2_ref[...].astype(f32)
    grad = grad + jnp.concatenate([x[...] for x in near], axis=0).astype(f32)
    vec_ref[0:1] = jnp.sum(grad * xhat, axis=0, keepdims=True)
    vec_ref[1:2] = jnp.sum(grad, axis=0, keepdims=True)
    e = grad * small_ref[2:3]
    back = factor * (
        e - jnp.mean(e, axis=-1, keepdims=True) - xhat * jnp.mean(e * xhat, axis=-1, keepdims=True)
    )
    gmid = cot_ref[...].astype(f32) + back
    gmid_ref[...] = gmid
    valid = part * rows + lax.broadcasted_iota(jnp.int32, (rows, 1), 0) < len_ref[0]
    branch_ref[...] = jnp.where(valid, gmid, 0.0).astype(bf16)
    cuts = [branch_ref[:, quarters(n, r, size)] for r in range(4)]
    keep_ref[:, :size] = cuts[0]
    keep_ref[:, size:] = cuts[2]
    send_ref[:, :size] = cuts[1]
    send_ref[:, size:] = cuts[3]
    for r in range(4):
        feats = quarters(n, r, size)
        total = dot(cuts[0], wouts[0][feats, :], NT)
        for k in range(1, 4):
            total = total + dot(cuts[k], wouts[k][feats, :], NT)
        gatts[r][...] = total.astype(bf16)


def ln2_back(n, length, middle, cot, small, p0, near, p2, wouts, part, into):
    slot, model = middle.shape
    smem = pl.BlockSpec(memory_space=pltpu.SMEM)
    whole = lambda x: pl.BlockSpec(x.shape, lambda i: (0, 0))
    rows = lambda cols: pl.BlockSpec((slot // 2, cols), lambda i: (part, 0))
    return pl.pallas_call(
        functools.partial(ln2_back_kernel, part),
        grid=(1,),
        in_specs=[smem, smem, rows(model), rows(model), whole(small), rows(model), whole(p2)]
        + [whole(w) for w in (*near, *wouts)]
        + [pl.BlockSpec(memory_space=pl.ANY)] * len(into),
        out_specs=[rows(model), rows(model // 2), rows(model // 2)]
        + [rows(model // 4)] * 4
        + [pl.BlockSpec((2, model), lambda i: (0, 0))],
        out_shape=[
            jax.ShapeDtypeStruct((slot, model), f32),
            jax.ShapeDtypeStruct((slot, model // 2), bf16),
            jax.ShapeDtypeStruct((slot, model // 2), bf16),
        ]
        + [jax.ShapeDtypeStruct((slot, model // 4), bf16)] * 4
        + [jax.ShapeDtypeStruct((2, model), f32)],
        scratch_shapes=[pltpu.VMEM((slot // 2, model), bf16)],
        input_output_aliases={13 + i: i for i in range(len(into))},
        compiler_params=pltpu.CompilerParams(vmem_limit_bytes=VMEM_LIMIT),
        cost_estimate=cost(5),
        name="ln2_back",
    )(n, length, middle, cot, small, p0, p2, *near, *wouts, *into)


def gelu_both(u):
    c0 = 0.7978845608028654
    c1 = 0.044715
    sq = u * u
    t = jnp.tanh(u * (c0 + (c0 * c1) * sq))
    half = 0.5 + 0.5 * t
    slope = half + (1.0 - t * t) * (u * (0.5 * c0 + (1.5 * c0 * c1) * sq))
    return u * half, slope


def ffn_kernel(count, places, start, cuts, w_any, *refs):
    norms, grads = refs[:count], refs[count : count + len(places)]
    n4_any, g4_any, hid4_any, gua4_any = refs[-13:-9]
    sums = refs[-16 - cuts : -13]
    o0_ref, gn0_ref = sums[:2]
    n_ref, g_ref, wu_ref, wd_ref, hid_ref, gua_ref, sems, w_sems, out_sems = refs[-9:]
    step = pl.program_id(0)
    steps = pl.num_programs(0) // 2
    rows = n_ref.shape[0]
    block = o0_ref.shape[1]
    mine = pl.ds(start, rows)
    outs = [
        pltpu.make_async_copy(src, dst.at[mine], out_sems.at[i])
        for i, (src, dst) in enumerate(
            ((n_ref, n4_any), (g_ref, g4_any), (hid_ref, hid4_any), (gua_ref, gua4_any))
        )
    ]
    shards, _, size, _ = w_any.shape
    weights = [
        [
            pltpu.make_async_copy(
                w_any.at[d, i], whole.at[pl.ds(d * size, size)], w_sems.at[d, i]
            )
            for d in range(shards)
        ]
        for i, whole in enumerate((wu_ref, wd_ref))
    ]
    acts = []
    grads = [g.at[pl.ds(first, size)] for g, (first, size) in zip(grads, places)]
    for j, (pieces, whole) in enumerate(((norms, n_ref), (grads, g_ref))):
        acts.append([])
        at = 0
        for i, piece in enumerate(pieces):
            here = piece.shape[0]
            acts[j].append(
                pltpu.make_async_copy(piece, whole.at[pl.ds(at, here)], sems.at[j, i])
            )
            at += here

    @pl.when(step == 0)
    def _():
        for copy in acts[0] + weights[0] + acts[1] + weights[1]:
            copy.start()
        for copy in acts[0] + weights[0]:
            copy.wait()

    @pl.when(step < steps)
    def _():
        cols = pl.ds(pl.multiple_of(step * block, block), block)
        u = dot(n_ref[...], wu_ref[:, cols])
        hid, slope = gelu_both(u)

        @pl.when(step == 0)
        def _():
            for copy in acts[1] + weights[1]:
                copy.wait()

        gh = dot(g_ref[...], wd_ref[cols, :], NT)
        hid_ref[:, cols] = hid.astype(bf16)
        gua_ref[:, cols] = (slope * gh).astype(bf16)

    @pl.when(step == steps)
    def _():
        for copy in outs:
            copy.start()

    @pl.when(step >= steps)
    def _():
        cols = pl.ds(pl.multiple_of((step - steps) * block, block), block)
        half = rows // 2
        gn = dot(gua_ref[...], wu_ref[cols, :], NT)
        o = dot(hid_ref[...], wd_ref[:, cols])
        for first, pieces, total in ((o0_ref, sums[2:3], o), (gn0_ref, sums[3:], gn)):
            first[...] = total[:half]
            size = half // len(pieces)
            for i, piece in enumerate(pieces):
                piece[...] = total[half + i * size : half + (i + 1) * size].astype(bf16)

    @pl.when(step == 2 * steps - 1)
    def _():
        for copy in outs:
            copy.wait()


def ffn(norms, grads, places, weights, start, into, cuts):
    width = norms[0].shape[1]
    rows = sum(x.shape[0] for x in norms)
    total = into[0].shape[0] if into else 2 * rows
    units = weights.shape[0] * weights.shape[2]
    block = min(512, units)
    steps = units // block
    half = rows // 2
    anywhere = pl.BlockSpec(memory_space=pl.ANY)
    late = lambda size: pl.BlockSpec((size, block), lambda i: (0, jnp.maximum(i - steps, 0)))
    acts = pltpu.VMEM((rows, width), bf16)
    hidden = pltpu.VMEM((rows, units), bf16)
    ins = 1 + len(norms) + len(grads)
    outs = 3 + cuts
    got = pl.pallas_call(
        functools.partial(ffn_kernel, len(norms), places, start, cuts),
        grid=(2 * steps,),
        in_specs=[anywhere] * (ins + len(into)),
        out_specs=[late(half)] * 2 + [late(half)] + [late(half // cuts)] * cuts + [anywhere] * 4,
        out_shape=[jax.ShapeDtypeStruct((half, width), f32)] * 2
        + [jax.ShapeDtypeStruct((half, width), bf16)]
        + [jax.ShapeDtypeStruct((half // cuts, width), bf16)] * cuts
        + [jax.ShapeDtypeStruct((total, width), bf16)] * 2
        + [jax.ShapeDtypeStruct((total, units), bf16)] * 2,
        scratch_shapes=[
            acts,
            acts,
            pltpu.VMEM((width, units), bf16),
            pltpu.VMEM((units, width), bf16),
            hidden,
            hidden,
            pltpu.SemaphoreType.DMA((2, max(len(norms), len(grads)))),
            pltpu.SemaphoreType.DMA((weights.shape[0], 2)),
            pltpu.SemaphoreType.DMA((4,)),
        ],
        input_output_aliases={ins + i: outs + i for i in range(len(into))},
        compiler_params=pltpu.CompilerParams(vmem_limit_bytes=VMEM_LIMIT),
        cost_estimate=cost(8 if into else 12, 1 / 64),
        name="ffn",
    )(weights, *norms, *grads, *into)
    return got[0], got[2], got[1], got[3:outs], got[outs:]


def pack_small_kernel(heads, n_ref, y_ref, one_ref, also_ref, two_ref, more_ref, buckets_ref, *refs):
    dists, (keep_ref, send_ref) = refs[:-2], refs[-2:]
    n = n_ref[0]
    odd = y_ref[0] == 1
    slot = buckets_ref.shape[1]
    total = dists[0][...]
    for ref in dists[1:]:
        total = total + ref[...]
    lanes = heads * BUCKETS
    bucket = lax.broadcasted_iota(jnp.int32, (lanes, slot), 0) % BUCKETS
    onehot = (buckets_ref[...] == bucket).astype(f32).astype(bf16)
    lane = lax.broadcasted_iota(jnp.int32, (1, lanes), 1)
    table = jnp.zeros((1, lanes), f32)
    for h in range(heads):
        row = jnp.broadcast_to(total[h // 2, h % 2 : h % 2 + 1], (8, slot))
        parts = []
        for _ in range(3):
            low = row.astype(bf16)
            parts.append(dot(low, onehot, NT))
            row = row - low.astype(f32)
        got = (parts[0] + parts[1] + parts[2])[0:1]
        table = jnp.where(lane // BUCKETS == h, got, table)
    zeros = jnp.zeros((1, TILE), f32)
    half = lanes // 2
    low = jnp.where(lane < half, table, 0.0)
    high = jnp.where(lane < half, pltpu.roll(table, half, 1), 0.0)
    for z in range(keep_ref.shape[0]):
        both = []
        for b, share in ((0, low), (1, high)):
            d = 2 * z + b
            cols = slice(d * TILE, (d + 1) * TILE)
            rel = jnp.where(d == 2 * n + b, share, zeros)
            both.append(
                jnp.concatenate(
                    [
                        one_ref[:, cols] + also_ref[:, cols],
                        two_ref[:, cols] + more_ref[:, cols],
                        rel,
                        zeros,
                        zeros,
                        zeros,
                    ],
                    axis=0,
                )
            )
        keep_ref[z] = jnp.where(odd, both[1], both[0])
        send_ref[z] = jnp.where(odd, both[0], both[1])


def pack_small(n, y, grad_one, grad_two, buckets, dists, heads):
    slot = buckets.shape[0]
    model = grad_one[0].shape[1]
    smem = pl.BlockSpec(memory_space=pltpu.SMEM)
    operands = [*grad_one, *grad_two, buckets.reshape(1, slot), *dists]
    shape = jax.ShapeDtypeStruct((model // TILE // 2, 8, TILE), f32)
    return pl.pallas_call(
        functools.partial(pack_small_kernel, heads),
        grid=(1,),
        in_specs=[smem, smem] + [block_of(x) for x in operands],
        out_specs=[pl.BlockSpec(shape.shape, lambda i: (0, 0, 0))] * 2,
        out_shape=[shape, shape],
        cost_estimate=cost(3),
        name="pack_small",
    )(n, y, *operands)


def join_ffn_kernel(quarter, n_ref, *refs):
    ins, (up_ref, down_ref) = refs[:4], refs[4:]
    model = down_ref.shape[1]
    rows = up_ref.shape[0]
    for r in range(4):
        j = lax.bitwise_xor(n_ref[0], r)
        for d in range(model // quarter):
            start = pl.multiple_of((d * 4 + j) * quarter, quarter)
            up_ref[:, pl.ds(start, quarter)] = ins[r][:, d * quarter : (d + 1) * quarter].astype(f32)
        down_ref[pl.ds(pl.multiple_of(j * quarter, quarter), quarter), :] = ins[r][:, model:].astype(f32)


def join_ffn(n, parts, quarter):
    rows, both = parts[0].shape
    model = both // 2
    shapes = [(rows, 4 * model), (4 * quarter, model)]
    if quarter % TILE:
        wide = model // quarter
        rel = jnp.stack(parts)
        rel = jnp.stack(
            [lax.dynamic_index_in_dim(rel, n[0] ^ j, 0, keepdims=False) for j in range(4)]
        ).astype(f32)
        up = rel[:, :, :model].reshape(4, rows, wide, quarter).transpose(1, 2, 0, 3)
        return up.reshape(shapes[0]), rel[:, :, model:].reshape(shapes[1])
    return pl.pallas_call(
        functools.partial(join_ffn_kernel, quarter),
        grid=(1,),
        in_specs=[pl.BlockSpec(memory_space=pltpu.SMEM)] + [block_of(x) for x in parts],
        out_specs=[pl.BlockSpec(x, lambda i: (0, 0)) for x in shapes],
        out_shape=[jax.ShapeDtypeStruct(x, f32) for x in shapes],
        compiler_params=pltpu.CompilerParams(vmem_limit_bytes=VMEM_LIMIT),
        cost_estimate=cost(4, 0.05),
        name="join_ffn",
    )(n, *parts)


def join_attn_kernel(n_ref, *refs):
    ins, (qkv_ref, out_ref) = refs[:4], refs[4:]
    model = out_ref.shape[1]
    mine = model // 4
    for r in range(4):
        j = lax.bitwise_xor(n_ref[0], r)
        at = 0
        for p in range(mine // PAIR):
            for part in range(3):
                start = pl.multiple_of(part * model + j * mine + p * PAIR, PAIR)
                qkv_ref[:, pl.ds(start, PAIR)] = ins[r][:, at : at + PAIR].astype(f32)
                at += PAIR
        out_ref[:, pl.ds(pl.multiple_of(j * mine, mine), mine)] = ins[r][
            :, at : at + mine
        ].astype(f32) + ins[r ^ 2][:, at + mine :].astype(f32)


def join_attn(n, parts, model):
    rows = parts[0].shape[0]
    shapes = [(rows, 3 * model), (rows, model)]
    return pl.pallas_call(
        join_attn_kernel,
        grid=(1,),
        in_specs=[pl.BlockSpec(memory_space=pltpu.SMEM)] + [block_of(x) for x in parts],
        out_specs=[pl.BlockSpec(x, lambda i: (0, 0)) for x in shapes],
        out_shape=[jax.ShapeDtypeStruct(x, f32) for x in shapes],
        cost_estimate=cost(3),
        name="join_attn",
    )(n, *parts)


def ring_order(size):
    return list(range(0, size, 2)) + list(range(size - 1, 0, -2))


def ring_member(pos, size):
    pos = lax.rem(pos + 2 * size, size)
    return jnp.where(pos < size // 2, 2 * pos, 2 * (size - 1 - pos) + 1)


def ring_pairs(narrow, size):
    order = ring_order(size)
    pairs = []
    for n in range(narrow):
        turn = 1 if n % 2 == 0 else -1
        for p in range(size):
            pairs.append((n * size + order[p], n * size + order[(p + turn) % size]))
    return pairs


class Places:
    def __init__(self):
        self.narrow = lax.axis_size("narrow")
        self.wide = lax.axis_size("wide")
        self.n = lax.axis_index("narrow")
        self.w = lax.axis_index("wide")
        self.core = lax.rem(self.n, 2)
        self.turn = 1 - 2 * self.core
        self.y = lax.rem(self.w, 2)
        self.z = self.w // 2
        self.pos = jnp.where(self.y == 0, self.z, self.wide - 1 - self.z)
        self.pairs = ring_pairs(self.narrow, self.wide)
        self.rings = self.wide <= 16

    def ring(self, x, way):
        pairs = self.pairs if way == 0 else [(b, a) for a, b in self.pairs]
        return lax.ppermute(x, ("narrow", "wide"), pairs)

    def member(self, steps):
        return ring_member(self.pos + self.turn * steps, self.wide)

    def swap(self, x, bit):
        return lax.ppermute(x, "narrow", [(i, i ^ bit) for i in range(self.narrow)])

    def all_narrow(self, x):
        far = self.swap(x, 2)
        return [x, self.swap(x, 1), far, self.swap(far, 1)]

    def swap_y(self, x):
        return lax.ppermute(x, "wide", [(i, i ^ 1) for i in range(self.wide)])

    def along_z(self, x, steps):
        return lax.ppermute(
            x, "wide", [(i, (i + 2 * steps) % self.wide) for i in range(self.wide)]
        )


def row_major(x):
    return with_layout_constraint(x, Layout(major_to_minor=tuple(range(x.ndim))))


def after(x, *deps):
    return lax.optimization_barrier((x, *deps))[0]


def add_low(*terms):
    return sum(t.astype(f32) for t in terms).astype(bf16)


def gather_ring(at, piece, holds):
    pieces, steps = [piece], [0]
    ahead = behind = piece
    far = at.wide // 2
    for k in range(1, far + 1):
        ahead = at.ring(ahead, 0)
        came = [ahead]
        if k < far:
            behind = at.ring(behind, 1)
            came.append(behind)
        held = holds[k](*came) if k in holds else ()
        came = lax.optimization_barrier((*came, *held))
        ahead = came[0]
        if k < far:
            behind = came[1]
            pieces.append(behind)
            steps.append(k)
        pieces.append(ahead)
        steps.append(-k)
    return pieces, steps


def reduce_ring(at, parts):
    size = at.wide

    def chunk(k):
        member = at.member(k)
        cut = [lax.dynamic_index_in_dim(p, member, 0, keepdims=False) for p in parts]
        return row_major(jnp.concatenate(cut, axis=1) if len(cut) > 1 else cut[0])

    far = size // 2
    ahead, behind = chunk(far), chunk(1 - far)
    yield ahead, behind
    for k in range(far - 1, 0, -1):
        ahead, behind = at.ring(ahead, 0), at.ring(behind, 1)
        held = yield ahead, behind
        ahead, behind, *_ = lax.optimization_barrier((ahead, behind, *(held or ())))
        ahead = row_major(add_low(ahead, chunk(k)))
        if k > 1:
            behind = row_major(add_low(behind, chunk(1 - k)))
        yield ahead, behind
    ahead = at.ring(ahead, 0)
    held = yield (ahead,)
    ahead, *_ = lax.optimization_barrier((ahead, *(held or ())))
    yield row_major(add_low(chunk(0), ahead, behind))


def scatter(at, parts):
    return jnp.concatenate(
        [lax.psum_scatter(p, "wide", scatter_dimension=0, tiled=True)[0] for p in parts], axis=1
    )


def local(
    tokens,
    lengths,
    buckets,
    ln1_gain,
    ln1_bias,
    w_qkv,
    rel_table,
    w_out,
    ln2_gain,
    ln2_bias,
    w_up,
    w_down,
    cotangent,
):
    at = Places()
    wide = at.wide
    slot, model = tokens.shape
    backwards = buckets.reshape(-1, TILE)[:, ::-1].reshape(slot)
    rows = w_qkv.shape[0]
    ff = w_up.shape[1]
    ff_rows = w_down.shape[0]
    quarter = ff_rows // 4
    heads = HEADS // 4
    width = 3 * model // 4
    rel_rows = rel_table.shape[0]
    n = at.n.reshape(1)
    far = wide // 2

    cut = slot // 16 * 7
    tokens_far = [at.swap(tokens[:cut], 2), at.swap(tokens[cut:], 2)]
    tokens_all = [[tokens], [at.swap(tokens, 1)], tokens_far, [at.swap(t, 1) for t in tokens_far]]

    lengths_far = at.swap(after(lengths, tokens_far[0]), 2)
    lengths_all = [lengths, at.swap(lengths, 1), lengths_far, at.swap(lengths_far, 1)]

    vectors = [ln1_gain, ln1_bias, ln2_gain, ln2_bias, rel_table]
    vectors = jnp.stack([jnp.pad(s, (0, TILE - s.shape[0])) for s in vectors])
    vectors = jnp.pad(vectors, ((0, 16 - vectors.shape[0]), (0, 0)))
    if at.rings:
        attn_piece = cut_attn(n, w_qkv, w_out, vectors)
        ffn_piece = cut_ffn(n, after(w_up, attn_piece), w_down)
        came, xhats = [], []

        def hold(x, *deps):
            xhats.append(xhat_of([after(t, *deps) for t in x]))
            return xhats[-1]

        pieces, steps = gather_ring(
            at,
            attn_piece,
            {
                1: lambda *x: [ffn_piece, tokens_far[0]],
                2: lambda *x: [
                    lengths_far,
                    tokens_far[1],
                    hold(tokens_all[0], *x),
                    hold(tokens_all[1], *x),
                ],
                3: lambda *x: came.extend(x) or lengths_all[1::2],
            },
        )
        hold(tokens_all[2], *came)
        hold(tokens_all[3], *came)
        ffn_piece = after(ffn_piece, *came)
        where = jnp.stack([at.member(k) for k in steps])
        small = small_rows(where, pieces, model)
    else:
        pick = lambda x, axis: lax.dynamic_index_in_dim(x, at.n, axis, keepdims=False)
        cut = pick(w_qkv.reshape(rows, 3, 4, heads // 2, PAIR), 2)
        cut = cut.transpose(0, 2, 1, 3).reshape(rows, width)
        cut = [cut, pick(w_out.reshape(rows, 4, model // 4), 1), jnp.zeros((rows, TILE), bf16)]
        attn_piece = jnp.concatenate(cut, axis=1)
        ffn_piece = jnp.stack(
            [
                pick(w_up.reshape(rows, wide, 4, quarter), 2).reshape(rows, wide * quarter),
                pick(w_down.reshape(4, quarter, model), 0),
            ]
        )
        pieces = [lax.all_gather(attn_piece, "wide", axis=0, tiled=True)]
        where = jnp.zeros((1,), jnp.int32)
        small = lax.all_gather(vectors, "wide", axis=0).astype(f32)
        small = [small[:, i, :rows].reshape(1, model) for i in range(4)] + [
            jnp.pad(small[:, 4, :rel_rows].reshape(1, -1), ((0, 0), (0, model - HEADS * BUCKETS)))
        ]
        small = jnp.pad(jnp.concatenate(small, axis=0), ((0, 3), (0, 0)))
    w_ffn = lax.all_gather(ffn_piece, "wide", axis=0)

    if not at.rings:
        xhats = [xhat_of(t) for t in tokens_all]
    valid = (jnp.arange(slot, dtype=jnp.int32) < lengths[0]).astype(f32)[:, None]
    cotan = cotangent.astype(f32)
    grad_ffn = at.all_narrow(after((valid * cotan).astype(bf16), *tokens_far))
    half = slot // 2
    norm_one, packed, wqkv, wout = qkv_of(where, small, xhats, pieces, width)
    wout_far = at.swap(wout, 2)
    tiles = bias_tiles(n, small, buckets, heads)
    atts, probs = [None] * 4, [None] * 4
    for r in (3, 2, 1, 0):
        length = {2: [grad_ffn[2]], 0: grad_ffn[1:]}.get(r, [])
        length = after(lengths_all[r], *length) if length else lengths_all[r]
        atts[r], probs[r] = attn_fwd(length, packed, tiles, r)
    wouts = [wout, at.swap(wout, 1), wout_far, at.swap(after(wout_far, atts[1]), 1)]
    attended = [atts[0]] + [at.swap(atts[r], r) for r in (1, 2, 3)]
    whole, norm_two, norm_far = [], [], []
    for i in range(2):
        *whole, norm = out_ln2(n, lengths, tokens, small, attended, wouts, i, whole)
        norm_two.append(norm)
        norm_far.append(at.swap(norm, 2))
    middle, attended = whole

    norm_near = norm_two + [at.swap(x, 1) for x in norm_two]
    o0, o1, gn0, gn1, rows_all = ffn(
        norm_near, grad_ffn[:2], [(0, slot)] * 2, w_ffn, 0, [], 4
    )
    gn_near = [at.swap(x, 1) for x in gn1]

    def chip_sum(p2, p3):
        return add_low(p2, jnp.concatenate([at.swap(x, 1) for x in p3], axis=0))

    cuts = 4
    gn_far, o_far, gn_back = [], [], []
    for i in range(2):
        norms = after(norm_far[i], gn2 if i else gn0)
        cut = half // cuts
        norms = [norms] + [at.swap(norms[j : j + cut], 1) for j in range(0, half, cut)]
        norms[0] = after(norms[0], *gn_far)
        o2, o3, gn2, gn3, rows_all = ffn(
            norms, grad_ffn[2:], [(i * half, half)] * 2, w_ffn, 2 * slot + i * slot, rows_all, cuts
        )
        gn_far.append(chip_sum(gn2, gn3))
        o_far.append((o2, o3))
        gn_back.append(at.swap(gn_far[i], 2))
    norms, grads, hid, gua = rows_all
    gu = dot(norms, after(gua, gn_back[0], *gn_far), TN).astype(bf16)
    gd = dot(hid, after(grads, gn_back[0], *gn_far), TN).astype(bf16)
    shape = (wide, rows, model)
    if at.rings:
        turns = reduce_ring(at, [gu.reshape(shape), gd.reshape(shape)])
        next(turns)

    whole, grad_two = [], []
    for i in range(2):
        near = gn_near[2 * i : 2 * i + 2]
        *whole, vec = ln2_back(
            n, lengths, middle, cotangent, small, gn0, near, gn_back[i], wouts, i, whole
        )
        grad_two.append(vec)
    grad_middle, branch_keep, branch_send, *grad_att = whole
    if at.rings:
        next(turns)
        grad_att[0] = after(grad_att[0], *next(turns))
    grad_att = [grad_att[0]] + [at.swap(grad_att[r], r) for r in (1, 2, 3)]
    grad_packed, dists = None, []

    def backward(r, *deps):
        ga = after(grad_att[r], *deps) if deps else grad_att[r]
        return attn_bwd(packed, ga, atts[r], probs[r], r, grad_packed)

    def turned():
        return list(next(turns)) if at.rings else []

    def turn_after(*deps):
        if at.rings:
            turns.send(list(deps))

    grad_packed, dist = backward(0)
    dists.append(dist)
    attended = after(attended, dist, *grad_att[2:])
    out_send = dot(attended, branch_send, TN).astype(bf16)
    out_keep = dot(attended, branch_keep, TN).astype(bf16)
    o_far = [chip_sum(after(x, dist), [after(y, dist)]) for x, y in o_far]
    out_back = [at.swap(o_far[0], 2)]
    grad_packed, dist = backward(2, out_send, out_keep, *turned())
    turn_after(grad_att[2])
    dists.append(dist)
    out_sum = add_low(out_keep, at.swap(out_send, 1))
    grad_packed, dist = backward(3, out_sum)
    dists.append(dist)
    p2, p3, more_one = ln1_back(after(grad_packed, out_back[0], *turned()), wqkv, xhats[2:], 2)
    turn_after(p3)
    p_far = chip_sum(p2, [p3])
    p_back = [at.swap(p_far[:half], 2)]
    grad_packed, dist = backward(1, p_far)
    dists.append(dist)
    grad_qkv = dot(norm_one, grad_packed, TN).astype(bf16)
    parts = [grad_qkv.reshape(wide, rows, width), out_sum.reshape(wide, rows, model // 2)]
    if at.rings:
        next(turns)
        ffn_own = turns.send([dist])
        turns = reduce_ring(at, parts)
        grad_packed = after(grad_packed, p_back[0], *next(turns))
    else:
        ffn_own = scatter(at, [gu.reshape(shape), gd.reshape(shape)])
        attn_own = scatter(at, parts)
    ffn_all = at.all_narrow(after(ffn_own, p_back[0]))
    p_back.append(at.swap(after(p_far[half:], ffn_all[2]), 2))
    out_back.append(at.swap(after(o_far[1], p_back[1]), 2))

    p0, p1, grad_one = ln1_back(grad_packed, wqkv, xhats[:2], 0)
    grad_one = [grad_one, more_one]
    p_near = at.swap(p1, 1)
    if at.rings:
        keep, send = pack_small(n, at.y.reshape(1), grad_one, grad_two, backwards, dists, heads)
        next(turns)
        sent = turns.send([p1, keep, ffn_all[2]])
        smalls = keep + at.swap_y(after(send, *sent))
        next(turns)
        sent = turns.send([p_back[1]])
        p0 = after(p0, *sent)
    grad_tokens = ln1_last(tokens, xhats[0], grad_middle, small, p0, p_near, *p_back)

    outs = [o0, at.swap(o1, 1), jnp.concatenate(out_back, axis=0)]
    if at.rings:
        next(turns)
        sent = turns.send([grad_tokens, smalls])
        smalls, outs[0] = after(smalls, *sent), after(o0, *sent)
        pick = lambda i: lax.dynamic_index_in_dim(smalls, i, 0, keepdims=False)
        z_parts = [pick(at.z)] + [
            at.along_z(pick(lax.rem(at.z + k, far)), k) for k in range(1, far)
        ]
    output = (middle + valid * sum(p.astype(f32) for p in outs)).astype(bf16)
    if at.rings:
        next(turns)
        attn_own = turns.send([output])
        smalls = after(z_parts[0], attn_own) + sum(z_parts[1:])

    if not at.rings:
        onehot = (backwards[:, None] == jnp.arange(BUCKETS, dtype=jnp.int32)[None, :]).astype(f32)
        table = jnp.dot(sum(dists).reshape(heads, slot), onehot, precision=lax.Precision.HIGHEST)
        table = lax.dynamic_update_slice(
            jnp.zeros((4, heads * BUCKETS), f32), table.reshape(1, -1), (at.n, 0)
        )
        two = grad_two[0] + grad_two[1]
        one = grad_one[0] + grad_one[1]
        smalls = [one[0], one[1], two[0], two[1], table]
        smalls = [g.reshape(wide, 1, -1) for g in smalls]
        smalls = [jnp.pad(g, ((0, 0), (0, 0), (0, TILE - g.shape[2]))) for g in smalls]
        smalls = jnp.concatenate(smalls + [jnp.zeros((wide, 3, TILE), f32)], axis=1)
        smalls = lax.psum_scatter(smalls, "wide", scatter_dimension=0, tiled=True)[0]
    smalls = smalls + at.swap(smalls, 2)
    smalls = smalls + at.swap(smalls, 1)

    ffn_all[0] = after(ffn_all[0], attn_own)
    up_full, down_full = join_ffn(n, ffn_all, quarter)
    qkv_full, out_full = join_attn(n, at.all_narrow(attn_own), model)

    return (
        output,
        grad_tokens,
        smalls[0, :rows],
        smalls[1, :rows],
        qkv_full,
        smalls[4, :rel_rows],
        out_full,
        smalls[2, :rows],
        smalls[3, :rows],
        up_full,
        down_full,
    )


def solution(mesh):
    return jax.shard_map(
        local,
        mesh=mesh,
        in_specs=(
            P(("narrow", "wide"), None),
            P(("narrow", "wide")),
            P(),
            P("wide"),
            P("wide"),
            P("wide", None),
            P("wide"),
            P("wide", None),
            P("wide"),
            P("wide"),
            P("wide", None),
            P("wide", None),
            P(("narrow", "wide"), None),
        ),
        out_specs=(
            P(("narrow", "wide"), None),
            P(("narrow", "wide"), None),
            P("wide"),
            P("wide"),
            P("wide", None),
            P("wide"),
            P("wide", None),
            P("wide"),
            P("wide"),
            P("wide", None),
            P("wide", None),
        ),
        check_vma=False,
    )
```

```python
import functools

import jax
import jax.numpy as jnp
from jax import lax
from jax.experimental import pallas as pl
from jax.experimental.layout import Layout, with_layout_constraint
from jax.experimental.pallas import tpu as pltpu
from jax.sharding import PartitionSpec as P

HEADS = 16
HEAD_DIM = 64
BUCKETS = 32
TILE = 128
PAIR = 2 * HEAD_DIM

norm_eps = 1e-05
neg_large = -1e30
f32 = jnp.float32
bf16 = jnp.bfloat16
VMEM_LIMIT = 56 * 1024 * 1024


PEAK = 1.15e15


def cost(us, share=1.0):
    return pl.CostEstimate(flops=int(us * share * 1e-6 * PEAK), bytes_accessed=0, transcendentals=0)


def dot(a, b, dims=((1,), (0,))):
    return lax.dot_general(a, b, (dims, ((), ())), preferred_element_type=f32)


NT = ((1,), (1,))
TN = ((0,), (0,))


def block_of(x):
    zeros = (0,) * x.ndim
    return pl.BlockSpec(x.shape, lambda i: zeros)


def cut_attn_kernel(n_ref, qkv_ref, out_ref, small_ref, o_ref):
    n = n_ref[0]
    model = out_ref.shape[1]
    mine = model // 4
    at = 0
    for p in range(mine // PAIR):
        for part in range(3):
            start = pl.multiple_of(part * model + n * mine + p * PAIR, PAIR)
            o_ref[:, at : at + PAIR] = qkv_ref[:, pl.ds(start, PAIR)]
            at += PAIR
    o_ref[:, at : at + mine] = out_ref[:, pl.ds(pl.multiple_of(n * mine, mine), mine)]
    at += mine
    o_ref[:, at:] = jnp.zeros((o_ref.shape[0], TILE), bf16)
    o_ref[:16, at:] = small_ref[...]


def cut_attn(n, w_qkv, w_out, small):
    rows, model = w_out.shape
    return pl.pallas_call(
        cut_attn_kernel,
        grid=(1,),
        in_specs=[pl.BlockSpec(memory_space=pltpu.SMEM)]
        + [block_of(x) for x in (w_qkv, w_out, small)],
        out_specs=pl.BlockSpec((rows, model + TILE), lambda i: (0, 0)),
        out_shape=jax.ShapeDtypeStruct((rows, model + TILE), bf16),
        cost_estimate=cost(2),
        name="cut_attn",
    )(n, w_qkv, w_out, small)


def cut_ffn_kernel(n_ref, up_ref, down_ref, o_ref):
    n = n_ref[0]
    size = down_ref.shape[0]
    model = down_ref.shape[1]
    for d in range(model // size):
        start = pl.multiple_of(d * 4 * size + n * size, size)
        o_ref[0, :, d * size : (d + 1) * size] = up_ref[:, pl.ds(start, size)]
    o_ref[1] = down_ref[...]


def cut_ffn(n, w_up, w_down):
    rows = w_up.shape[0]
    quarter, model = w_down.shape[0] // 4, w_down.shape[1]
    return pl.pallas_call(
        cut_ffn_kernel,
        grid_spec=pltpu.PrefetchScalarGridSpec(
            num_scalar_prefetch=1,
            grid=(1,),
            in_specs=[
                pl.BlockSpec(w_up.shape, lambda i, n: (0, 0)),
                pl.BlockSpec((quarter, model), lambda i, n: (n[0], 0)),
            ],
            out_specs=pl.BlockSpec((2, rows, model), lambda i, n: (0, 0, 0)),
        ),
        out_shape=jax.ShapeDtypeStruct((2, rows, model), bf16),
        cost_estimate=cost(2, 0.05),
        name="cut_ffn",
    )(n, w_up, w_down)


def small_kernel(where_ref, *refs):
    out_ref = refs[-1]
    out_ref[...] = jnp.zeros_like(out_ref)
    lane = lax.broadcasted_iota(jnp.int32, (1, TILE), 1)
    for i, ref in enumerate(refs[:-1]):
        d = where_ref[i]
        got = ref[...].astype(f32)
        start = pl.multiple_of(d * TILE, TILE)
        for v in range(4):
            out_ref[v : v + 1, pl.ds(start, TILE)] = got[v : v + 1]
        rel = got[4:5]
        odd = lax.rem(d, 2) == 1
        rel = jnp.where(odd, pltpu.roll(rel, TILE // 2, 1), rel)
        rel = jnp.where((lane >= TILE // 2) == odd, rel, 0.0)
        start = pl.multiple_of((d // 2) * TILE, TILE)
        out_ref[4:5, pl.ds(start, TILE)] += rel


def small_rows(where, pieces, at):
    model = len(pieces) * TILE
    return pl.pallas_call(
        small_kernel,
        grid=(1,),
        in_specs=[pl.BlockSpec(memory_space=pltpu.SMEM)]
        + [pl.BlockSpec((16, TILE), lambda i: (0, at // TILE))] * len(pieces),
        out_specs=pl.BlockSpec((8, model), lambda i: (0, 0)),
        out_shape=jax.ShapeDtypeStruct((8, model), f32),
        cost_estimate=cost(2),
        name="small_rows",
    )(where, *pieces)


def tiles_kernel(n_ref, small_ref, buckets_ref, out_ref):
    heads, count = out_ref.shape[:2]
    lanes = heads * BUCKETS
    slot = buckets_ref.shape[1]
    rel = small_ref[4:5, pl.ds(pl.multiple_of(n_ref[0] * lanes, lanes), lanes)]
    head = lax.broadcasted_iota(jnp.int32, (8, lanes), 0)
    lane = lax.broadcasted_iota(jnp.int32, (8, lanes), 1)
    table = jnp.where(lane // BUCKETS == head, rel, 0.0).astype(bf16)
    bucket = lax.broadcasted_iota(jnp.int32, (lanes, slot), 0) % BUCKETS
    onehot = (buckets_ref[...] == bucket).astype(f32).astype(bf16)
    by_distance = dot(table, onehot)
    row = lax.broadcasted_iota(jnp.int32, (TILE, TILE), 0)
    col = lax.broadcasted_iota(jnp.int32, (TILE, TILE), 1)
    for h in range(heads):
        for delta in range(count):
            here = by_distance[h : h + 1, delta * TILE : (delta + 1) * TILE]
            below = by_distance[h : h + 1, max(delta - 1, 0) * TILE : max(delta, 1) * TILE]
            wide = jnp.broadcast_to(jnp.concatenate([here, below], axis=1), (TILE, 2 * TILE))
            tile = pltpu.roll(wide, 0, 1, stride=1, stride_axis=0)[:, :TILE].T
            if delta == 0:
                tile = jnp.where(col <= row, tile, neg_large)
            out_ref[h, delta] = tile


def bias_tiles(n, small, buckets, heads):
    slot = buckets.shape[0]
    buckets = buckets.reshape(1, slot)
    shape = (heads, slot // TILE, TILE, TILE)
    return pl.pallas_call(
        tiles_kernel,
        grid=(1,),
        in_specs=[pl.BlockSpec(memory_space=pltpu.SMEM), block_of(small), block_of(buckets)],
        out_specs=pl.BlockSpec(shape, lambda i: (0, 0, 0, 0)),
        out_shape=jax.ShapeDtypeStruct(shape, f32),
        cost_estimate=cost(4),
        name="bias_tiles",
    )(n, small, buckets)


def normalized(v):
    center = v - jnp.mean(v, axis=-1, keepdims=True)
    factor = lax.rsqrt(jnp.mean(center * center, axis=-1, keepdims=True) + norm_eps)
    return center * factor, factor


def xhat_kernel(*refs):
    out_ref = refs[-1]
    at = 0
    for ref in refs[:-1]:
        rows = ref.shape[0]
        out_ref[at : at + rows] = normalized(ref[...].astype(f32))[0]
        at += rows


def xhat_of(pieces):
    slot, model = sum(p.shape[0] for p in pieces), pieces[0].shape[1]
    return pl.pallas_call(
        xhat_kernel,
        grid=(1,),
        in_specs=[block_of(p) for p in pieces],
        out_specs=pl.BlockSpec((slot, model), lambda i: (0, 0)),
        out_shape=jax.ShapeDtypeStruct((slot, model), f32),
        compiler_params=pltpu.CompilerParams(vmem_limit_bytes=VMEM_LIMIT),
        cost_estimate=cost(2.5, 0.05),
        name="xhat",
    )(*pieces)


def qkv_kernel(count, where_ref, small_ref, *refs):
    xhats, pieces = refs[:4], refs[4 : 4 + count]
    norm_ref, packed_ref, wq_ref, wo_ref, w_ref, x_ref, sems, x_sems = refs[4 + count :]
    step = pl.program_id(0)
    width = wq_ref.shape[1]

    def fetch(r):
        return pltpu.make_async_copy(xhats[r], x_ref.at[r % 2], x_sems.at[r % 2])

    @pl.when(step == 0)
    def _():
        fetch(0).start()
        copies = []
        for i, piece in enumerate(pieces):
            size = piece.shape[0]
            start = pl.multiple_of(where_ref[i] * size, size)
            copies.append(pltpu.make_async_copy(piece, w_ref.at[pl.ds(start, size)], sems.at[i]))
            copies[-1].start()
        for copy in copies:
            copy.wait()
        wq_ref[...] = w_ref[:, :width]
        wo_ref[...] = w_ref[:, width : width + wo_ref.shape[1]]

    for r in range(4):

        @pl.when(step == r)
        def _(r=r):
            if r < 3:
                fetch(r + 1).start()
            fetch(r).wait()

    norm = (x_ref[lax.rem(step, 2)] * small_ref[0:1] + small_ref[1:2]).astype(bf16)
    norm_ref[...] = norm
    packed_ref[...] = dot(norm, wq_ref[...]).astype(bf16)


def qkv_of(where, small, xhats, pieces, width):
    slot, model = xhats[0].shape
    total = pieces[0].shape[1]
    out = model // 4
    whole = lambda shape: pl.BlockSpec(shape, lambda i: (0, 0))
    rows = lambda cols: pl.BlockSpec((slot, cols), lambda i: (i, 0))
    return pl.pallas_call(
        functools.partial(qkv_kernel, len(pieces)),
        grid=(4,),
        in_specs=[pl.BlockSpec(memory_space=pltpu.SMEM), whole(small.shape)]
        + [pl.BlockSpec(memory_space=pl.ANY)] * (4 + len(pieces)),
        out_specs=[rows(model), rows(width), whole((model, width)), whole((model, out))],
        out_shape=[
            jax.ShapeDtypeStruct((4 * slot, model), bf16),
            jax.ShapeDtypeStruct((4 * slot, width), bf16),
            jax.ShapeDtypeStruct((model, width), bf16),
            jax.ShapeDtypeStruct((model, out), bf16),
        ],
        scratch_shapes=[
            pltpu.VMEM((model, total), bf16),
            pltpu.VMEM((2, slot, model), f32),
            pltpu.SemaphoreType.DMA((len(pieces),)),
            pltpu.SemaphoreType.DMA((2,)),
        ],
        compiler_params=pltpu.CompilerParams(vmem_limit_bytes=VMEM_LIMIT),
        cost_estimate=cost(7, 0.05),
        name="qkv",
    )(where, small, *xhats, *pieces)


def ln1_back_kernel(gp_ref, wq_ref, x0_ref, x1_ref, p0_ref, p1_ref, vec_ref):
    step = pl.program_id(0)
    grad = dot(gp_ref[...], wq_ref[...], NT)

    @pl.when(step == 0)
    def _():
        vec_ref[0:1] = jnp.sum(grad * x0_ref[...], axis=0, keepdims=True)
        vec_ref[1:2] = jnp.sum(grad, axis=0, keepdims=True)
        p0_ref[...] = grad.astype(p0_ref.dtype)

    @pl.when(step == 1)
    def _():
        vec_ref[0:1] += jnp.sum(grad * x1_ref[...], axis=0, keepdims=True)
        vec_ref[1:2] += jnp.sum(grad, axis=0, keepdims=True)
        p1_ref[...] = grad.astype(p1_ref.dtype)


def ln1_back(grad_packed, wqkv, xhats, first):
    slot, model = xhats[0].shape
    width = wqkv.shape[1]
    whole = lambda shape: pl.BlockSpec(shape, lambda i: (0, 0))
    return pl.pallas_call(
        ln1_back_kernel,
        grid=(2,),
        in_specs=[
            pl.BlockSpec((slot, width), lambda i: (first + i, 0)),
            whole((model, width)),
            whole((slot, model)),
            whole((slot, model)),
        ],
        out_specs=[whole((slot, model)), whole((slot, model)), whole((2, model))],
        out_shape=[
            jax.ShapeDtypeStruct((slot, model), bf16 if first else f32),
            jax.ShapeDtypeStruct((slot, model), bf16),
            jax.ShapeDtypeStruct((2, model), f32),
        ],
        compiler_params=pltpu.CompilerParams(vmem_limit_bytes=VMEM_LIMIT),
        cost_estimate=cost(5, 0.1 if first else 1.0),
        name="ln1_back",
    )(grad_packed, wqkv, *xhats)


def attn_fwd_kernel(len_ref, qkv_ref, tiles_ref, att_ref, p_ref):
    slot = qkv_ref.shape[0]
    blocks = range(slot // TILE)
    heads = range(2)
    length = len_ref[0]
    lane = lax.broadcasted_iota(jnp.int32, (1, PAIR), 1)
    col = lax.broadcasted_iota(jnp.int32, (1, slot), 1)
    hidden = jnp.where(col < length, 0.0, neg_large)
    q = qkv_ref[:, :PAIR] * HEAD_DIM ** (-0.5)
    k = qkv_ref[:, PAIR : 2 * PAIR]
    v = qkv_ref[:, 2 * PAIR :]
    own = [(lane // HEAD_DIM) == hh for hh in heads]
    qm = [jnp.where(own[hh], q, jnp.zeros_like(q)) for hh in heads]
    span = [(i + 1) * TILE for i in blocks]
    items = [(hh, i) for hh in heads for i in blocks]
    s = [dot(qm[hh][i * TILE : span[i]], k[: span[i]], NT) for hh, i in items]
    s = [
        x + jnp.concatenate([tiles_ref[hh, i - j] for j in range(i + 1)], axis=1) + hidden[:, : span[i]]
        for x, (hh, i) in zip(s, items)
    ]
    top = [jnp.max(x, axis=1, keepdims=True) for x in s]
    e = [jnp.exp(x - m) for x, m in zip(s, top)]
    scale = [1.0 / jnp.sum(x, axis=1, keepdims=True) for x in e]
    probs = [(x * r).astype(bf16) for x, r in zip(e, scale)]
    for x, (hh, i) in zip(probs, items):
        p_ref[hh, i * TILE : span[i], : span[i]] = x
    o = {item: dot(x, v[: span[item[1]]]) for x, item in zip(probs, items)}
    for i in blocks:
        att_ref[i * TILE : span[i], :] = jnp.where(own[0], o[0, i], o[1, i]).astype(bf16)


def attn_fwd(lengths, packed, tiles, seq):
    heads, count = tiles.shape[:2]
    slot = count * TILE
    return pl.pallas_call(
        attn_fwd_kernel,
        grid=(heads // 2,),
        in_specs=[
            pl.BlockSpec(memory_space=pltpu.SMEM),
            pl.BlockSpec((slot, 3 * PAIR), lambda p: (seq, p)),
            pl.BlockSpec((2, count, TILE, TILE), lambda p: (p, 0, 0, 0)),
        ],
        out_specs=[
            pl.BlockSpec((slot, PAIR), lambda p: (0, p)),
            pl.BlockSpec((2, slot, slot), lambda p: (p, 0, 0)),
        ],
        out_shape=[
            jax.ShapeDtypeStruct((slot, heads * HEAD_DIM), bf16),
            jax.ShapeDtypeStruct((heads, slot, slot), bf16),
        ],
        compiler_params=pltpu.CompilerParams(vmem_limit_bytes=VMEM_LIMIT),
        cost_estimate=cost(4.5, 0.1),
        name="attn_fwd",
    )(lengths, packed, tiles)


def attn_bwd_kernel(qkv_ref, ga_ref, att_ref, p_ref, *refs):
    g_ref, sum_ref, ds_ref = refs[-3:]
    slot = qkv_ref.shape[0]
    blocks = range(slot // TILE)
    heads = range(2)
    lane = lax.broadcasted_iota(jnp.int32, (1, PAIR), 1)
    scale = HEAD_DIM ** (-0.5)
    q = qkv_ref[:, :PAIR] * scale
    k = qkv_ref[:, PAIR : 2 * PAIR]
    v = qkv_ref[:, 2 * PAIR :]
    ga = ga_ref[...]
    prod = ga.astype(f32) * att_ref[...].astype(f32)
    own = [(lane // HEAD_DIM) == hh for hh in heads]
    gam = [jnp.where(own[hh], ga, jnp.zeros_like(ga)) for hh in heads]
    inner = [jnp.sum(jnp.where(own[hh], prod, 0.0), axis=1, keepdims=True) for hh in heads]
    span = [(i + 1) * TILE for i in blocks]
    rows = [slice(i * TILE, span[i]) for i in blocks]
    items = [(hh, i) for hh in heads for i in blocks]
    dp = [dot(gam[hh][rows[i]], v[: span[i]], NT) for hh, i in items]
    ds = {
        (hh, i): (p_ref[hh, rows[i], : span[i]].astype(f32) * (x - inner[hh][rows[i]])).astype(bf16)
        for x, (hh, i) in zip(dp, items)
    }
    for hh, i in items:
        ds_ref[hh, rows[i], : span[i]] = ds[hh, i]
    dq = {(hh, i): dot(ds[hh, i], k[: span[i]]) for hh, i in items}
    dv = {(hh, j): dot(p_ref[hh, j * TILE :, rows[j]], ga[j * TILE :], TN) for hh, j in items}
    dk = {(hh, j): dot(ds_ref[hh, j * TILE :, rows[j]], q[j * TILE :], TN) for hh, j in items}
    for i in blocks:
        for at, got, factor in ((0, dq, scale), (PAIR, dk, 1.0), (2 * PAIR, dv, 1.0)):
            both = jnp.where(own[0], got[0, i], got[1, i]) * factor
            g_ref[rows[i], at : at + PAIR] = both.astype(bf16)
    row = lax.broadcasted_iota(jnp.int32, (TILE, TILE), 0)
    col = lax.broadcasted_iota(jnp.int32, (TILE, TILE), 1)
    flip = jnp.where(row + col == TILE - 1, 1.0, 0.0).astype(bf16)
    diag = {}
    for hh in heads:
        for delta in blocks:
            parts = [
                ds[hh, i][:, (i - delta) * TILE : (i - delta + 1) * TILE].astype(f32)
                for i in blocks
                if i >= delta
            ]
            diag[hh, delta] = functools.reduce(jnp.add, parts)
    high = {key: x.astype(bf16) for key, x in diag.items()}
    low = {key: (x - high[key].astype(f32)).astype(bf16) for key, x in diag.items()}
    turned = {key: dot(flip, high[key]) + dot(flip, low[key]) for key in diag}
    sums = {}
    for key, x in turned.items():
        wide = jnp.concatenate([x, jnp.zeros_like(x)], axis=1)
        wide = pltpu.roll(wide, 0, 1, stride=1, stride_axis=0)
        sums[key] = jnp.sum(wide, axis=0, keepdims=True)
    for hh in heads:
        for delta in blocks:
            here = sums[hh, delta][:, :TILE]
            if delta + 1 in blocks:
                here = here + sums[hh, delta + 1][:, TILE:]
            sum_ref[0, hh : hh + 1, rows[delta]] = here


def attn_bwd(packed, ga, att, probs, seq, into):
    heads, slot = probs.shape[:2]
    steps = heads // 2
    return pl.pallas_call(
        attn_bwd_kernel,
        grid=(steps,),
        in_specs=[
            pl.BlockSpec((slot, 3 * PAIR), lambda p: (seq, p)),
            pl.BlockSpec((slot, PAIR), lambda p: (0, p)),
            pl.BlockSpec((slot, PAIR), lambda p: (0, p)),
            pl.BlockSpec((2, slot, slot), lambda p: (p, 0, 0)),
        ]
        + ([] if into is None else [pl.BlockSpec(memory_space=pl.ANY)]),
        out_specs=[
            pl.BlockSpec((slot, 3 * PAIR), lambda p: (seq, p)),
            pl.BlockSpec((1, 2, slot), lambda p: (p, 0, 0)),
        ],
        out_shape=[
            jax.ShapeDtypeStruct(packed.shape, bf16),
            jax.ShapeDtypeStruct((steps, 2, slot), f32),
        ],
        scratch_shapes=[pltpu.VMEM((2, slot, slot), bf16)],
        input_output_aliases={} if into is None else {4: 0},
        compiler_params=pltpu.CompilerParams(vmem_limit_bytes=VMEM_LIMIT),
        cost_estimate=cost(5, 0.2),
        name="attn_bwd",
    )(packed, ga, att, probs, *(() if into is None else (into,)))


def ln1_last_kernel(tok_ref, xhat_ref, gmid_ref, small_ref, p0_ref, p1_ref, p2_ref, p3_ref, out_ref):
    _, factor = normalized(tok_ref[...].astype(f32))
    xhat = xhat_ref[...]
    low = pl.program_id(0) == 0
    e = p0_ref[...] + p1_ref[...].astype(f32) + jnp.where(low, p2_ref[...], p3_ref[...]).astype(f32)
    e = e * small_ref[0:1]
    out_ref[...] = gmid_ref[...] + factor * (
        e - jnp.mean(e, axis=-1, keepdims=True) - xhat * jnp.mean(e * xhat, axis=-1, keepdims=True)
    )


def ln1_last(tokens, xhat, grad_middle, small, p0, p1, p2, p3):
    slot, model = tokens.shape
    row = pl.BlockSpec((slot // 2, model), lambda i: (i, 0))
    part = pl.BlockSpec((slot // 2, model), lambda i: (0, 0))
    return pl.pallas_call(
        ln1_last_kernel,
        grid=(2,),
        in_specs=[row] * 3 + [block_of(small), row, row, part, part],
        out_specs=row,
        out_shape=jax.ShapeDtypeStruct((slot, model), f32),
        compiler_params=pltpu.CompilerParams(vmem_limit_bytes=VMEM_LIMIT),
        cost_estimate=cost(5, 0.05),
        name="ln1_last",
    )(tokens, xhat, grad_middle, small, p0, p1, p2, p3)


def quarters(n, r, size):
    return pl.ds(pl.multiple_of(lax.bitwise_xor(n, r) * size, size), size)


def out_ln2_kernel(part, n_ref, len_ref, tok_ref, small_ref, *refs):
    atts, wouts = refs[:4], refs[4:8]
    mid_ref, all_ref, norm_ref = refs[-3:]
    n = n_ref[0]
    rows, model = tok_ref.shape
    size = model // 4
    for r in range(4):
        all_ref[:, quarters(n, r, size)] = atts[r][...]
    valid = part * rows + lax.broadcasted_iota(jnp.int32, (rows, 1), 0) < len_ref[0]
    for r in range(4):
        cols = quarters(n, r, size)
        out = dot(all_ref[...], wouts[r][...])
        mid_ref[:, cols] = tok_ref[:, cols].astype(f32) + jnp.where(valid, out, 0.0)
    xhat, _ = normalized(mid_ref[...])
    norm_ref[...] = (xhat * small_ref[2:3] + small_ref[3:4]).astype(bf16)


def out_ln2(n, length, tokens, small, atts, wouts, part, into):
    slot, model = tokens.shape
    smem = pl.BlockSpec(memory_space=pltpu.SMEM)
    whole = lambda x: pl.BlockSpec(x.shape, lambda i: (0, 0))
    rows = lambda cols: pl.BlockSpec((slot // 2, cols), lambda i: (part, 0))
    return pl.pallas_call(
        functools.partial(out_ln2_kernel, part),
        grid=(1,),
        in_specs=[smem, smem, rows(model), whole(small)]
        + [rows(model // 4)] * 4
        + [whole(w) for w in wouts]
        + [pl.BlockSpec(memory_space=pl.ANY)] * len(into),
        out_specs=[rows(model), rows(model), pl.BlockSpec((slot // 2, model), lambda i: (0, 0))],
        out_shape=[
            jax.ShapeDtypeStruct((slot, model), f32),
            jax.ShapeDtypeStruct((slot, model), bf16),
            jax.ShapeDtypeStruct((slot // 2, model), bf16),
        ],
        input_output_aliases={12 + i: i for i in range(len(into))},
        compiler_params=pltpu.CompilerParams(vmem_limit_bytes=VMEM_LIMIT),
        cost_estimate=cost(4, 1 / 64),
        name="out_ln2",
    )(n, length, tokens, small, *atts, *wouts, *into)


def ln2_back_kernel(part, n_ref, len_ref, mid_ref, cot_ref, small_ref, p0_ref, p2_ref, *refs):
    near, wouts = refs[:2], refs[2:6]
    gmid_ref, keep_ref, send_ref = refs[-9:-6]
    gatts = refs[-6:-2]
    vec_ref, branch_ref = refs[-2:]
    n = n_ref[0]
    rows, model = mid_ref.shape
    size = model // 4
    xhat, factor = normalized(mid_ref[...])
    grad = p0_ref[...] + p2_ref[...].astype(f32)
    grad = grad + jnp.concatenate([x[...] for x in near], axis=0).astype(f32)
    vec_ref[0:1] = jnp.sum(grad * xhat, axis=0, keepdims=True)
    vec_ref[1:2] = jnp.sum(grad, axis=0, keepdims=True)
    e = grad * small_ref[2:3]
    back = factor * (
        e - jnp.mean(e, axis=-1, keepdims=True) - xhat * jnp.mean(e * xhat, axis=-1, keepdims=True)
    )
    gmid = cot_ref[...].astype(f32) + back
    gmid_ref[...] = gmid
    valid = part * rows + lax.broadcasted_iota(jnp.int32, (rows, 1), 0) < len_ref[0]
    branch_ref[...] = jnp.where(valid, gmid, 0.0).astype(bf16)
    cuts = [branch_ref[:, quarters(n, r, size)] for r in range(4)]
    keep_ref[:, :size] = cuts[0]
    keep_ref[:, size:] = cuts[2]
    send_ref[:, :size] = cuts[1]
    send_ref[:, size:] = cuts[3]
    for r in range(4):
        feats = quarters(n, r, size)
        total = dot(cuts[0], wouts[0][feats, :], NT)
        for k in range(1, 4):
            total = total + dot(cuts[k], wouts[k][feats, :], NT)
        gatts[r][...] = total.astype(bf16)


def ln2_back(n, length, middle, cot, small, p0, near, p2, wouts, part, into):
    slot, model = middle.shape
    smem = pl.BlockSpec(memory_space=pltpu.SMEM)
    whole = lambda x: pl.BlockSpec(x.shape, lambda i: (0, 0))
    rows = lambda cols: pl.BlockSpec((slot // 2, cols), lambda i: (part, 0))
    return pl.pallas_call(
        functools.partial(ln2_back_kernel, part),
        grid=(1,),
        in_specs=[smem, smem, rows(model), rows(model), whole(small), rows(model), whole(p2)]
        + [whole(w) for w in (*near, *wouts)]
        + [pl.BlockSpec(memory_space=pl.ANY)] * len(into),
        out_specs=[rows(model), rows(model // 2), rows(model // 2)]
        + [rows(model // 4)] * 4
        + [pl.BlockSpec((2, model), lambda i: (0, 0))],
        out_shape=[
            jax.ShapeDtypeStruct((slot, model), f32),
            jax.ShapeDtypeStruct((slot, model // 2), bf16),
            jax.ShapeDtypeStruct((slot, model // 2), bf16),
        ]
        + [jax.ShapeDtypeStruct((slot, model // 4), bf16)] * 4
        + [jax.ShapeDtypeStruct((2, model), f32)],
        scratch_shapes=[pltpu.VMEM((slot // 2, model), bf16)],
        input_output_aliases={13 + i: i for i in range(len(into))},
        compiler_params=pltpu.CompilerParams(vmem_limit_bytes=VMEM_LIMIT),
        cost_estimate=cost(5),
        name="ln2_back",
    )(n, length, middle, cot, small, p0, p2, *near, *wouts, *into)


def gelu_both(u):
    c0 = 0.7978845608028654
    c1 = 0.044715
    sq = u * u
    t = jnp.tanh(u * (c0 + (c0 * c1) * sq))
    half = 0.5 + 0.5 * t
    slope = half + (1.0 - t * t) * (u * (0.5 * c0 + (1.5 * c0 * c1) * sq))
    return u * half, slope


def ffn_kernel(count, places, start, cuts, w_any, *refs):
    norms, grads = refs[:count], refs[count : count + len(places)]
    n4_any, g4_any, hid4_any, gua4_any = refs[-13:-9]
    sums = refs[-16 - cuts : -13]
    o0_ref, gn0_ref = sums[:2]
    n_ref, g_ref, wu_ref, wd_ref, hid_ref, gua_ref, sems, w_sems, out_sems = refs[-9:]
    step = pl.program_id(0)
    steps = pl.num_programs(0) // 2
    rows = n_ref.shape[0]
    block = o0_ref.shape[1]
    mine = pl.ds(start, rows)
    outs = [
        pltpu.make_async_copy(src, dst.at[mine], out_sems.at[i])
        for i, (src, dst) in enumerate(
            ((n_ref, n4_any), (g_ref, g4_any), (hid_ref, hid4_any), (gua_ref, gua4_any))
        )
    ]
    shards, _, size, _ = w_any.shape
    weights = [
        [
            pltpu.make_async_copy(
                w_any.at[d, i], whole.at[pl.ds(d * size, size)], w_sems.at[d, i]
            )
            for d in range(shards)
        ]
        for i, whole in enumerate((wu_ref, wd_ref))
    ]
    acts = []
    grads = [g.at[pl.ds(first, size)] for g, (first, size) in zip(grads, places)]
    for j, (pieces, whole) in enumerate(((norms, n_ref), (grads, g_ref))):
        acts.append([])
        at = 0
        for i, piece in enumerate(pieces):
            here = piece.shape[0]
            acts[j].append(
                pltpu.make_async_copy(piece, whole.at[pl.ds(at, here)], sems.at[j, i])
            )
            at += here

    @pl.when(step == 0)
    def _():
        for copy in acts[0] + weights[0] + acts[1] + weights[1]:
            copy.start()
        for copy in acts[0] + weights[0]:
            copy.wait()

    @pl.when(step < steps)
    def _():
        cols = pl.ds(pl.multiple_of(step * block, block), block)
        u = dot(n_ref[...], wu_ref[:, cols])
        hid, slope = gelu_both(u)

        @pl.when(step == 0)
        def _():
            for copy in acts[1] + weights[1]:
                copy.wait()

        gh = dot(g_ref[...], wd_ref[cols, :], NT)
        hid_ref[:, cols] = hid.astype(bf16)
        gua_ref[:, cols] = (slope * gh).astype(bf16)

    @pl.when(step == steps)
    def _():
        for copy in outs:
            copy.start()

    @pl.when(step >= steps)
    def _():
        cols = pl.ds(pl.multiple_of((step - steps) * block, block), block)
        half = rows // 2
        gn = dot(gua_ref[...], wu_ref[cols, :], NT)
        o = dot(hid_ref[...], wd_ref[:, cols])
        for first, pieces, total in ((o0_ref, sums[2:3], o), (gn0_ref, sums[3:], gn)):
            first[...] = total[:half]
            size = half // len(pieces)
            for i, piece in enumerate(pieces):
                piece[...] = total[half + i * size : half + (i + 1) * size].astype(bf16)

    @pl.when(step == 2 * steps - 1)
    def _():
        for copy in outs:
            copy.wait()


def ffn(norms, grads, places, weights, start, into, cuts):
    width = norms[0].shape[1]
    rows = sum(x.shape[0] for x in norms)
    total = into[0].shape[0] if into else 2 * rows
    units = weights.shape[0] * weights.shape[2]
    block = min(512, units)
    steps = units // block
    half = rows // 2
    anywhere = pl.BlockSpec(memory_space=pl.ANY)
    late = lambda size: pl.BlockSpec((size, block), lambda i: (0, jnp.maximum(i - steps, 0)))
    acts = pltpu.VMEM((rows, width), bf16)
    hidden = pltpu.VMEM((rows, units), bf16)
    ins = 1 + len(norms) + len(grads)
    outs = 3 + cuts
    got = pl.pallas_call(
        functools.partial(ffn_kernel, len(norms), places, start, cuts),
        grid=(2 * steps,),
        in_specs=[anywhere] * (ins + len(into)),
        out_specs=[late(half)] * 2 + [late(half)] + [late(half // cuts)] * cuts + [anywhere] * 4,
        out_shape=[jax.ShapeDtypeStruct((half, width), f32)] * 2
        + [jax.ShapeDtypeStruct((half, width), bf16)]
        + [jax.ShapeDtypeStruct((half // cuts, width), bf16)] * cuts
        + [jax.ShapeDtypeStruct((total, width), bf16)] * 2
        + [jax.ShapeDtypeStruct((total, units), bf16)] * 2,
        scratch_shapes=[
            acts,
            acts,
            pltpu.VMEM((width, units), bf16),
            pltpu.VMEM((units, width), bf16),
            hidden,
            hidden,
            pltpu.SemaphoreType.DMA((2, max(len(norms), len(grads)))),
            pltpu.SemaphoreType.DMA((weights.shape[0], 2)),
            pltpu.SemaphoreType.DMA((4,)),
        ],
        input_output_aliases={ins + i: outs + i for i in range(len(into))},
        compiler_params=pltpu.CompilerParams(vmem_limit_bytes=VMEM_LIMIT),
        cost_estimate=cost(8 if into else 12, 1 / 64),
        name="ffn",
    )(weights, *norms, *grads, *into)
    return got[0], got[2], got[1], got[3:outs], got[outs:]


def pack_small_kernel(heads, n_ref, y_ref, one_ref, also_ref, two_ref, more_ref, buckets_ref, *refs):
    dists, (keep_ref, send_ref) = refs[:-2], refs[-2:]
    n = n_ref[0]
    odd = y_ref[0] == 1
    slot = buckets_ref.shape[1]
    total = dists[0][...]
    for ref in dists[1:]:
        total = total + ref[...]
    lanes = heads * BUCKETS
    bucket = lax.broadcasted_iota(jnp.int32, (lanes, slot), 0) % BUCKETS
    onehot = (buckets_ref[...] == bucket).astype(f32).astype(bf16)
    lane = lax.broadcasted_iota(jnp.int32, (1, lanes), 1)
    table = jnp.zeros((1, lanes), f32)
    for h in range(heads):
        row = jnp.broadcast_to(total[h // 2, h % 2 : h % 2 + 1], (8, slot))
        parts = []
        for _ in range(3):
            low = row.astype(bf16)
            parts.append(dot(low, onehot, NT))
            row = row - low.astype(f32)
        got = (parts[0] + parts[1] + parts[2])[0:1]
        table = jnp.where(lane // BUCKETS == h, got, table)
    zeros = jnp.zeros((1, TILE), f32)
    half = lanes // 2
    low = jnp.where(lane < half, table, 0.0)
    high = jnp.where(lane < half, pltpu.roll(table, half, 1), 0.0)
    for z in range(keep_ref.shape[0]):
        both = []
        for b, share in ((0, low), (1, high)):
            d = 2 * z + b
            cols = slice(d * TILE, (d + 1) * TILE)
            rel = jnp.where(d == 2 * n + b, share, zeros)
            both.append(
                jnp.concatenate(
                    [
                        one_ref[:, cols] + also_ref[:, cols],
                        two_ref[:, cols] + more_ref[:, cols],
                        rel,
                        zeros,
                        zeros,
                        zeros,
                    ],
                    axis=0,
                )
            )
        keep_ref[z] = jnp.where(odd, both[1], both[0])
        send_ref[z] = jnp.where(odd, both[0], both[1])


def pack_small(n, y, grad_one, grad_two, buckets, dists, heads):
    slot = buckets.shape[0]
    model = grad_one[0].shape[1]
    smem = pl.BlockSpec(memory_space=pltpu.SMEM)
    operands = [*grad_one, *grad_two, buckets.reshape(1, slot), *dists]
    shape = jax.ShapeDtypeStruct((model // TILE // 2, 8, TILE), f32)
    return pl.pallas_call(
        functools.partial(pack_small_kernel, heads),
        grid=(1,),
        in_specs=[smem, smem] + [block_of(x) for x in operands],
        out_specs=[pl.BlockSpec(shape.shape, lambda i: (0, 0, 0))] * 2,
        out_shape=[shape, shape],
        cost_estimate=cost(3),
        name="pack_small",
    )(n, y, *operands)


def join_ffn_kernel(quarter, n_ref, *refs):
    ins, (up_ref, down_ref) = refs[:4], refs[4:]
    model = down_ref.shape[1]
    rows = up_ref.shape[0]
    for r in range(4):
        j = lax.bitwise_xor(n_ref[0], r)
        for d in range(model // quarter):
            start = pl.multiple_of((d * 4 + j) * quarter, quarter)
            up_ref[:, pl.ds(start, quarter)] = ins[r][:, d * quarter : (d + 1) * quarter].astype(f32)
        down_ref[pl.ds(pl.multiple_of(j * quarter, quarter), quarter), :] = ins[r][:, model:].astype(f32)


def join_ffn(n, parts, quarter):
    rows, both = parts[0].shape
    model = both // 2
    shapes = [(rows, 4 * model), (4 * quarter, model)]
    if quarter % TILE:
        wide = model // quarter
        rel = jnp.stack(parts)
        rel = jnp.stack(
            [lax.dynamic_index_in_dim(rel, n[0] ^ j, 0, keepdims=False) for j in range(4)]
        ).astype(f32)
        up = rel[:, :, :model].reshape(4, rows, wide, quarter).transpose(1, 2, 0, 3)
        return up.reshape(shapes[0]), rel[:, :, model:].reshape(shapes[1])
    return pl.pallas_call(
        functools.partial(join_ffn_kernel, quarter),
        grid=(1,),
        in_specs=[pl.BlockSpec(memory_space=pltpu.SMEM)] + [block_of(x) for x in parts],
        out_specs=[pl.BlockSpec(x, lambda i: (0, 0)) for x in shapes],
        out_shape=[jax.ShapeDtypeStruct(x, f32) for x in shapes],
        compiler_params=pltpu.CompilerParams(vmem_limit_bytes=VMEM_LIMIT),
        cost_estimate=cost(4, 0.05),
        name="join_ffn",
    )(n, *parts)


def join_attn_kernel(n_ref, *refs):
    ins, (qkv_ref, out_ref) = refs[:4], refs[4:]
    model = out_ref.shape[1]
    mine = model // 4
    for r in range(4):
        j = lax.bitwise_xor(n_ref[0], r)
        at = 0
        for p in range(mine // PAIR):
            for part in range(3):
                start = pl.multiple_of(part * model + j * mine + p * PAIR, PAIR)
                qkv_ref[:, pl.ds(start, PAIR)] = ins[r][:, at : at + PAIR].astype(f32)
                at += PAIR
        out_ref[:, pl.ds(pl.multiple_of(j * mine, mine), mine)] = ins[r][
            :, at : at + mine
        ].astype(f32) + ins[r ^ 2][:, at + mine :].astype(f32)


def join_attn(n, parts, model):
    rows = parts[0].shape[0]
    shapes = [(rows, 3 * model), (rows, model)]
    return pl.pallas_call(
        join_attn_kernel,
        grid=(1,),
        in_specs=[pl.BlockSpec(memory_space=pltpu.SMEM)] + [block_of(x) for x in parts],
        out_specs=[pl.BlockSpec(x, lambda i: (0, 0)) for x in shapes],
        out_shape=[jax.ShapeDtypeStruct(x, f32) for x in shapes],
        cost_estimate=cost(3),
        name="join_attn",
    )(n, *parts)


def ring_order(size):
    return list(range(0, size, 2)) + list(range(size - 1, 0, -2))


def ring_member(pos, size):
    pos = lax.rem(pos + 2 * size, size)
    return jnp.where(pos < size // 2, 2 * pos, 2 * (size - 1 - pos) + 1)


def ring_pairs(narrow, size):
    order = ring_order(size)
    pairs = []
    for n in range(narrow):
        turn = 1 if n % 2 == 0 else -1
        for p in range(size):
            pairs.append((n * size + order[p], n * size + order[(p + turn) % size]))
    return pairs


class Places:
    def __init__(self):
        self.narrow = lax.axis_size("narrow")
        self.wide = lax.axis_size("wide")
        self.n = lax.axis_index("narrow")
        self.w = lax.axis_index("wide")
        self.core = lax.rem(self.n, 2)
        self.turn = 1 - 2 * self.core
        self.y = lax.rem(self.w, 2)
        self.z = self.w // 2
        self.pos = jnp.where(self.y == 0, self.z, self.wide - 1 - self.z)
        self.pairs = ring_pairs(self.narrow, self.wide)
        self.rings = self.wide <= 16

    def ring(self, x, way):
        pairs = self.pairs if way == 0 else [(b, a) for a, b in self.pairs]
        return lax.ppermute(x, ("narrow", "wide"), pairs)

    def member(self, steps):
        return ring_member(self.pos + self.turn * steps, self.wide)

    def swap(self, x, bit):
        return lax.ppermute(x, "narrow", [(i, i ^ bit) for i in range(self.narrow)])

    def all_narrow(self, x):
        far = self.swap(x, 2)
        return [x, self.swap(x, 1), far, self.swap(far, 1)]

    def swap_y(self, x):
        return lax.ppermute(x, "wide", [(i, i ^ 1) for i in range(self.wide)])

    def along_z(self, x, steps):
        return lax.ppermute(
            x, "wide", [(i, (i + 2 * steps) % self.wide) for i in range(self.wide)]
        )


def row_major(x):
    return with_layout_constraint(x, Layout(major_to_minor=tuple(range(x.ndim))))


def after(x, *deps):
    return lax.optimization_barrier((x, *deps))[0]


def add_low(*terms):
    return sum(t.astype(f32) for t in terms).astype(bf16)


def gather_ring(at, piece, holds):
    pieces, steps = [piece], [0]
    ahead = behind = piece
    far = at.wide // 2
    for k in range(1, far + 1):
        ahead = at.ring(ahead, 0)
        came = [ahead]
        if k < far:
            behind = at.ring(behind, 1)
            came.append(behind)
        held = holds[k](*came) if k in holds else ()
        came = lax.optimization_barrier((*came, *held))
        ahead = came[0]
        if k < far:
            behind = came[1]
            pieces.append(behind)
            steps.append(k)
        pieces.append(ahead)
        steps.append(-k)
    return pieces, steps


def reduce_ring(at, parts):
    size = at.wide

    def chunk(k):
        member = at.member(k)
        cut = [lax.dynamic_index_in_dim(p, member, 0, keepdims=False) for p in parts]
        return row_major(jnp.concatenate(cut, axis=1) if len(cut) > 1 else cut[0])

    far = size // 2
    ahead, behind = chunk(far), chunk(1 - far)
    yield ahead, behind
    for k in range(far - 1, 0, -1):
        ahead, behind = at.ring(ahead, 0), at.ring(behind, 1)
        held = yield ahead, behind
        ahead, behind, *_ = lax.optimization_barrier((ahead, behind, *(held or ())))
        ahead = row_major(add_low(ahead, chunk(k)))
        if k > 1:
            behind = row_major(add_low(behind, chunk(1 - k)))
        yield ahead, behind
    ahead = at.ring(ahead, 0)
    held = yield (ahead,)
    ahead, *_ = lax.optimization_barrier((ahead, *(held or ())))
    yield row_major(add_low(chunk(0), ahead, behind))


def scatter(at, parts):
    return jnp.concatenate(
        [lax.psum_scatter(p, "wide", scatter_dimension=0, tiled=True)[0] for p in parts], axis=1
    )


def local(
    tokens,
    lengths,
    buckets,
    ln1_gain,
    ln1_bias,
    w_qkv,
    rel_table,
    w_out,
    ln2_gain,
    ln2_bias,
    w_up,
    w_down,
    cotangent,
):
    at = Places()
    wide = at.wide
    slot, model = tokens.shape
    backwards = buckets.reshape(-1, TILE)[:, ::-1].reshape(slot)
    rows = w_qkv.shape[0]
    ff = w_up.shape[1]
    ff_rows = w_down.shape[0]
    quarter = ff_rows // 4
    heads = HEADS // 4
    width = 3 * model // 4
    rel_rows = rel_table.shape[0]
    n = at.n.reshape(1)
    far = wide // 2

    cut = slot // 16 * 7
    tokens_far = [at.swap(tokens[:cut], 2), at.swap(tokens[cut:], 2)]
    tokens_all = [[tokens], [at.swap(tokens, 1)], tokens_far, [at.swap(t, 1) for t in tokens_far]]

    lengths_far = at.swap(after(lengths, tokens_far[0]), 2)
    lengths_all = [lengths, at.swap(lengths, 1), lengths_far, at.swap(lengths_far, 1)]

    vectors = [ln1_gain, ln1_bias, ln2_gain, ln2_bias, rel_table]
    vectors = jnp.stack([jnp.pad(s, (0, TILE - s.shape[0])) for s in vectors])
    vectors = jnp.pad(vectors, ((0, 16 - vectors.shape[0]), (0, 0)))
    if at.rings:
        attn_piece = cut_attn(n, w_qkv, w_out, vectors)
        ffn_piece = cut_ffn(n, after(w_up, attn_piece), w_down)
        came, xhats = [], []

        def hold(x, *deps):
            xhats.append(xhat_of([after(t, *deps) for t in x]))
            return xhats[-1]

        pieces, steps = gather_ring(
            at,
            attn_piece,
            {
                1: lambda *x: [ffn_piece, tokens_far[0]],
                2: lambda *x: [
                    lengths_far,
                    tokens_far[1],
                    hold(tokens_all[0], *x),
                    hold(tokens_all[1], *x),
                ],
                3: lambda *x: came.extend(x) or lengths_all[1::2],
            },
        )
        hold(tokens_all[2], *came)
        hold(tokens_all[3], *came)
        ffn_piece = after(ffn_piece, *came)
        where = jnp.stack([at.member(k) for k in steps])
        small = small_rows(where, pieces, model)
    else:
        pick = lambda x, axis: lax.dynamic_index_in_dim(x, at.n, axis, keepdims=False)
        cut = pick(w_qkv.reshape(rows, 3, 4, heads // 2, PAIR), 2)
        cut = cut.transpose(0, 2, 1, 3).reshape(rows, width)
        cut = [cut, pick(w_out.reshape(rows, 4, model // 4), 1), jnp.zeros((rows, TILE), bf16)]
        attn_piece = jnp.concatenate(cut, axis=1)
        ffn_piece = jnp.stack(
            [
                pick(w_up.reshape(rows, wide, 4, quarter), 2).reshape(rows, wide * quarter),
                pick(w_down.reshape(4, quarter, model), 0),
            ]
        )
        pieces = [lax.all_gather(attn_piece, "wide", axis=0, tiled=True)]
        where = jnp.zeros((1,), jnp.int32)
        small = lax.all_gather(vectors, "wide", axis=0).astype(f32)
        small = [small[:, i, :rows].reshape(1, model) for i in range(4)] + [
            jnp.pad(small[:, 4, :rel_rows].reshape(1, -1), ((0, 0), (0, model - HEADS * BUCKETS)))
        ]
        small = jnp.pad(jnp.concatenate(small, axis=0), ((0, 3), (0, 0)))
    w_ffn = lax.all_gather(ffn_piece, "wide", axis=0)

    if not at.rings:
        xhats = [xhat_of(t) for t in tokens_all]
    valid = (jnp.arange(slot, dtype=jnp.int32) < lengths[0]).astype(f32)[:, None]
    cotan = cotangent.astype(f32)
    grad_ffn = at.all_narrow(after((valid * cotan).astype(bf16), *tokens_far))
    half = slot // 2
    norm_one, packed, wqkv, wout = qkv_of(where, small, xhats, pieces, width)
    wout_far = at.swap(wout, 2)
    tiles = bias_tiles(n, small, buckets, heads)
    atts, probs = [None] * 4, [None] * 4
    for r in (3, 2, 1, 0):
        length = {2: [grad_ffn[2]], 0: grad_ffn[1:]}.get(r, [])
        length = after(lengths_all[r], *length) if length else lengths_all[r]
        atts[r], probs[r] = attn_fwd(length, packed, tiles, r)
    wouts = [wout, at.swap(wout, 1), wout_far, at.swap(after(wout_far, atts[1]), 1)]
    attended = [atts[0]] + [at.swap(atts[r], r) for r in (1, 2, 3)]
    whole, norm_two, norm_far = [], [], []
    for i in range(2):
        *whole, norm = out_ln2(n, lengths, tokens, small, attended, wouts, i, whole)
        norm_two.append(norm)
        norm_far.append(at.swap(norm, 2))
    middle, attended = whole

    norm_near = norm_two + [at.swap(x, 1) for x in norm_two]
    o0, o1, gn0, gn1, rows_all = ffn(
        norm_near, grad_ffn[:2], [(0, slot)] * 2, w_ffn, 0, [], 4
    )
    gn_near = [at.swap(x, 1) for x in gn1]

    def chip_sum(p2, p3):
        return add_low(p2, jnp.concatenate([at.swap(x, 1) for x in p3], axis=0))

    cuts = 4
    gn_far, o_far, gn_back = [], [], []
    for i in range(2):
        norms = after(norm_far[i], gn2 if i else gn0)
        cut = half // cuts
        norms = [norms] + [at.swap(norms[j : j + cut], 1) for j in range(0, half, cut)]
        norms[0] = after(norms[0], *gn_far)
        o2, o3, gn2, gn3, rows_all = ffn(
            norms, grad_ffn[2:], [(i * half, half)] * 2, w_ffn, 2 * slot + i * slot, rows_all, cuts
        )
        gn_far.append(chip_sum(gn2, gn3))
        o_far.append((o2, o3))
        gn_back.append(at.swap(gn_far[i], 2))
    norms, grads, hid, gua = rows_all
    gu = dot(norms, after(gua, gn_back[0], *gn_far), TN).astype(bf16)
    gd = dot(hid, after(grads, gn_back[0], *gn_far), TN).astype(bf16)
    shape = (wide, rows, model)
    if at.rings:
        turns = reduce_ring(at, [gu.reshape(shape), gd.reshape(shape)])
        next(turns)

    whole, grad_two = [], []
    for i in range(2):
        near = gn_near[2 * i : 2 * i + 2]
        *whole, vec = ln2_back(
            n, lengths, middle, cotangent, small, gn0, near, gn_back[i], wouts, i, whole
        )
        grad_two.append(vec)
    grad_middle, branch_keep, branch_send, *grad_att = whole
    if at.rings:
        next(turns)
        grad_att[0] = after(grad_att[0], *next(turns))
    grad_att = [grad_att[0]] + [at.swap(grad_att[r], r) for r in (1, 2, 3)]
    grad_packed, dists = None, []

    def backward(r, *deps):
        ga = after(grad_att[r], *deps) if deps else grad_att[r]
        return attn_bwd(packed, ga, atts[r], probs[r], r, grad_packed)

    def turned():
        return list(next(turns)) if at.rings else []

    def turn_after(*deps):
        if at.rings:
            turns.send(list(deps))

    grad_packed, dist = backward(0)
    dists.append(dist)
    attended = after(attended, dist, *grad_att[2:])
    out_send = dot(attended, branch_send, TN).astype(bf16)
    out_keep = dot(attended, branch_keep, TN).astype(bf16)
    o_far = [chip_sum(after(x, dist), [after(y, dist)]) for x, y in o_far]
    out_back = [at.swap(o_far[0], 2)]
    grad_packed, dist = backward(2, out_send, out_keep, *turned())
    turn_after(grad_att[2])
    dists.append(dist)
    out_sum = add_low(out_keep, at.swap(out_send, 1))
    grad_packed, dist = backward(3, out_sum)
    dists.append(dist)
    p2, p3, more_one = ln1_back(after(grad_packed, out_back[0], *turned()), wqkv, xhats[2:], 2)
    turn_after(p3)
    p_far = chip_sum(p2, [p3])
    p_back = [at.swap(p_far[:half], 2)]
    grad_packed, dist = backward(1, p_far)
    dists.append(dist)
    grad_qkv = dot(norm_one, grad_packed, TN).astype(bf16)
    parts = [grad_qkv.reshape(wide, rows, width), out_sum.reshape(wide, rows, model // 2)]
    if at.rings:
        next(turns)
        ffn_own = turns.send([dist])
        turns = reduce_ring(at, parts)
        grad_packed = after(grad_packed, p_back[0], *next(turns))
    else:
        ffn_own = scatter(at, [gu.reshape(shape), gd.reshape(shape)])
        attn_own = scatter(at, parts)
    ffn_all = at.all_narrow(after(ffn_own, p_back[0]))
    p_back.append(at.swap(after(p_far[half:], ffn_all[2]), 2))
    out_back.append(at.swap(after(o_far[1], p_back[1]), 2))

    p0, p1, grad_one = ln1_back(grad_packed, wqkv, xhats[:2], 0)
    grad_one = [grad_one, more_one]
    p_near = at.swap(p1, 1)
    if at.rings:
        keep, send = pack_small(n, at.y.reshape(1), grad_one, grad_two, backwards, dists, heads)
        next(turns)
        sent = turns.send([p1, keep, ffn_all[2]])
        smalls = keep + at.swap_y(after(send, *sent))
        next(turns)
        sent = turns.send([p_back[1], smalls])
        p0 = after(p0, *sent)
        up_full, down_full = join_ffn(n, ffn_all, quarter)
    grad_tokens = ln1_last(tokens, xhats[0], grad_middle, small, p0, p_near, *p_back)

    outs = [o0, at.swap(o1, 1), jnp.concatenate(out_back, axis=0)]
    if at.rings:
        next(turns)
        sent = turns.send([grad_tokens, up_full])
        smalls, outs[0] = after(smalls, *sent), after(o0, *sent)
        pick = lambda i: lax.dynamic_index_in_dim(smalls, i, 0, keepdims=False)
        z_parts = [pick(at.z)] + [
            at.along_z(pick(lax.rem(at.z + k, far)), k) for k in range(1, far)
        ]
    output = (middle + valid * sum(p.astype(f32) for p in outs)).astype(bf16)
    if at.rings:
        next(turns)
        attn_own = turns.send([output, *z_parts[1:]])
        smalls = after(z_parts[0], attn_own) + sum(z_parts[1:])

    if not at.rings:
        onehot = (backwards[:, None] == jnp.arange(BUCKETS, dtype=jnp.int32)[None, :]).astype(f32)
        table = jnp.dot(sum(dists).reshape(heads, slot), onehot, precision=lax.Precision.HIGHEST)
        table = lax.dynamic_update_slice(
            jnp.zeros((4, heads * BUCKETS), f32), table.reshape(1, -1), (at.n, 0)
        )
        two = grad_two[0] + grad_two[1]
        one = grad_one[0] + grad_one[1]
        smalls = [one[0], one[1], two[0], two[1], table]
        smalls = [g.reshape(wide, 1, -1) for g in smalls]
        smalls = [jnp.pad(g, ((0, 0), (0, 0), (0, TILE - g.shape[2]))) for g in smalls]
        smalls = jnp.concatenate(smalls + [jnp.zeros((wide, 3, TILE), f32)], axis=1)
        smalls = lax.psum_scatter(smalls, "wide", scatter_dimension=0, tiled=True)[0]
    smalls = smalls + at.swap(smalls, 2)
    smalls = smalls + at.swap(smalls, 1)

    if not at.rings:
        up_full, down_full = join_ffn(n, ffn_all, quarter)
    qkv_full, out_full = join_attn(n, at.all_narrow(attn_own), model)

    return (
        output,
        grad_tokens,
        smalls[0, :rows],
        smalls[1, :rows],
        qkv_full,
        smalls[4, :rel_rows],
        out_full,
        smalls[2, :rows],
        smalls[3, :rows],
        up_full,
        down_full,
    )


def solution(mesh):
    return jax.shard_map(
        local,
        mesh=mesh,
        in_specs=(
            P(("narrow", "wide"), None),
            P(("narrow", "wide")),
            P(),
            P("wide"),
            P("wide"),
            P("wide", None),
            P("wide"),
            P("wide", None),
            P("wide"),
            P("wide"),
            P("wide", None),
            P("wide", None),
            P(("narrow", "wide"), None),
        ),
        out_specs=(
            P(("narrow", "wide"), None),
            P(("narrow", "wide"), None),
            P("wide"),
            P("wide"),
            P("wide", None),
            P("wide"),
            P("wide", None),
            P("wide"),
            P("wide"),
            P("wide", None),
            P("wide", None),
        ),
        check_vma=False,
    )
```

```python
import functools

import jax
import jax.numpy as jnp
from jax import lax
from jax.experimental import pallas as pl
from jax.experimental.layout import Layout, with_layout_constraint
from jax.experimental.pallas import tpu as pltpu
from jax.sharding import PartitionSpec as P

HEADS = 16
HEAD_DIM = 64
BUCKETS = 32
TILE = 128
PAIR = 2 * HEAD_DIM

norm_eps = 1e-05
neg_large = -1e30
f32 = jnp.float32
bf16 = jnp.bfloat16
VMEM_LIMIT = 56 * 1024 * 1024


PEAK = 1.15e15


def cost(us, share=1.0):
    return pl.CostEstimate(flops=int(us * share * 1e-6 * PEAK), bytes_accessed=0, transcendentals=0)


def dot(a, b, dims=((1,), (0,))):
    return lax.dot_general(a, b, (dims, ((), ())), preferred_element_type=f32)


NT = ((1,), (1,))
TN = ((0,), (0,))


def block_of(x):
    zeros = (0,) * x.ndim
    return pl.BlockSpec(x.shape, lambda i: zeros)


def cut_attn_kernel(n_ref, qkv_ref, out_ref, small_ref, o_ref):
    n = n_ref[0]
    model = out_ref.shape[1]
    mine = model // 4
    at = 0
    for p in range(mine // PAIR):
        for part in range(3):
            start = pl.multiple_of(part * model + n * mine + p * PAIR, PAIR)
            o_ref[:, at : at + PAIR] = qkv_ref[:, pl.ds(start, PAIR)]
            at += PAIR
    o_ref[:, at : at + mine] = out_ref[:, pl.ds(pl.multiple_of(n * mine, mine), mine)]
    at += mine
    o_ref[:, at:] = jnp.zeros((o_ref.shape[0], TILE), bf16)
    o_ref[:16, at:] = small_ref[...]


def cut_attn(n, w_qkv, w_out, small):
    rows, model = w_out.shape
    return pl.pallas_call(
        cut_attn_kernel,
        grid=(1,),
        in_specs=[pl.BlockSpec(memory_space=pltpu.SMEM)]
        + [block_of(x) for x in (w_qkv, w_out, small)],
        out_specs=pl.BlockSpec((rows, model + TILE), lambda i: (0, 0)),
        out_shape=jax.ShapeDtypeStruct((rows, model + TILE), bf16),
        cost_estimate=cost(2),
        name="cut_attn",
    )(n, w_qkv, w_out, small)


def cut_ffn_kernel(n_ref, up_ref, down_ref, o_ref):
    n = n_ref[0]
    size = down_ref.shape[0]
    model = down_ref.shape[1]
    for d in range(model // size):
        start = pl.multiple_of(d * 4 * size + n * size, size)
        o_ref[0, :, d * size : (d + 1) * size] = up_ref[:, pl.ds(start, size)]
    o_ref[1] = down_ref[...]


def cut_ffn(n, w_up, w_down):
    rows = w_up.shape[0]
    quarter, model = w_down.shape[0] // 4, w_down.shape[1]
    return pl.pallas_call(
        cut_ffn_kernel,
        grid_spec=pltpu.PrefetchScalarGridSpec(
            num_scalar_prefetch=1,
            grid=(1,),
            in_specs=[
                pl.BlockSpec(w_up.shape, lambda i, n: (0, 0)),
                pl.BlockSpec((quarter, model), lambda i, n: (n[0], 0)),
            ],
            out_specs=pl.BlockSpec((2, rows, model), lambda i, n: (0, 0, 0)),
        ),
        out_shape=jax.ShapeDtypeStruct((2, rows, model), bf16),
        cost_estimate=cost(2, 0.05),
        name="cut_ffn",
    )(n, w_up, w_down)


def small_kernel(where_ref, *refs):
    out_ref = refs[-1]
    out_ref[...] = jnp.zeros_like(out_ref)
    lane = lax.broadcasted_iota(jnp.int32, (1, TILE), 1)
    for i, ref in enumerate(refs[:-1]):
        d = where_ref[i]
        got = ref[...].astype(f32)
        start = pl.multiple_of(d * TILE, TILE)
        for v in range(4):
            out_ref[v : v + 1, pl.ds(start, TILE)] = got[v : v + 1]
        rel = got[4:5]
        odd = lax.rem(d, 2) == 1
        rel = jnp.where(odd, pltpu.roll(rel, TILE // 2, 1), rel)
        rel = jnp.where((lane >= TILE // 2) == odd, rel, 0.0)
        start = pl.multiple_of((d // 2) * TILE, TILE)
        out_ref[4:5, pl.ds(start, TILE)] += rel


def small_rows(where, pieces, at):
    model = len(pieces) * TILE
    return pl.pallas_call(
        small_kernel,
        grid=(1,),
        in_specs=[pl.BlockSpec(memory_space=pltpu.SMEM)]
        + [pl.BlockSpec((16, TILE), lambda i: (0, at // TILE))] * len(pieces),
        out_specs=pl.BlockSpec((8, model), lambda i: (0, 0)),
        out_shape=jax.ShapeDtypeStruct((8, model), f32),
        cost_estimate=cost(2),
        name="small_rows",
    )(where, *pieces)


def tiles_kernel(n_ref, small_ref, buckets_ref, out_ref):
    heads, count = out_ref.shape[:2]
    lanes = heads * BUCKETS
    slot = buckets_ref.shape[1]
    rel = small_ref[4:5, pl.ds(pl.multiple_of(n_ref[0] * lanes, lanes), lanes)]
    head = lax.broadcasted_iota(jnp.int32, (8, lanes), 0)
    lane = lax.broadcasted_iota(jnp.int32, (8, lanes), 1)
    table = jnp.where(lane // BUCKETS == head, rel, 0.0).astype(bf16)
    bucket = lax.broadcasted_iota(jnp.int32, (lanes, slot), 0) % BUCKETS
    onehot = (buckets_ref[...] == bucket).astype(f32).astype(bf16)
    by_distance = dot(table, onehot)
    row = lax.broadcasted_iota(jnp.int32, (TILE, TILE), 0)
    col = lax.broadcasted_iota(jnp.int32, (TILE, TILE), 1)
    for h in range(heads):
        for delta in range(count):
            here = by_distance[h : h + 1, delta * TILE : (delta + 1) * TILE]
            below = by_distance[h : h + 1, max(delta - 1, 0) * TILE : max(delta, 1) * TILE]
            wide = jnp.broadcast_to(jnp.concatenate([here, below], axis=1), (TILE, 2 * TILE))
            tile = pltpu.roll(wide, 0, 1, stride=1, stride_axis=0)[:, :TILE].T
            if delta == 0:
                tile = jnp.where(col <= row, tile, neg_large)
            out_ref[h, delta] = tile


def bias_tiles(n, small, buckets, heads):
    slot = buckets.shape[0]
    buckets = buckets.reshape(1, slot)
    shape = (heads, slot // TILE, TILE, TILE)
    return pl.pallas_call(
        tiles_kernel,
        grid=(1,),
        in_specs=[pl.BlockSpec(memory_space=pltpu.SMEM), block_of(small), block_of(buckets)],
        out_specs=pl.BlockSpec(shape, lambda i: (0, 0, 0, 0)),
        out_shape=jax.ShapeDtypeStruct(shape, f32),
        cost_estimate=cost(4),
        name="bias_tiles",
    )(n, small, buckets)


def normalized(v):
    center = v - jnp.mean(v, axis=-1, keepdims=True)
    factor = lax.rsqrt(jnp.mean(center * center, axis=-1, keepdims=True) + norm_eps)
    return center * factor, factor


def xhat_kernel(*refs):
    out_ref = refs[-1]
    at = 0
    for ref in refs[:-1]:
        rows = ref.shape[0]
        out_ref[at : at + rows] = normalized(ref[...].astype(f32))[0]
        at += rows


def xhat_of(pieces):
    slot, model = sum(p.shape[0] for p in pieces), pieces[0].shape[1]
    return pl.pallas_call(
        xhat_kernel,
        grid=(1,),
        in_specs=[block_of(p) for p in pieces],
        out_specs=pl.BlockSpec((slot, model), lambda i: (0, 0)),
        out_shape=jax.ShapeDtypeStruct((slot, model), f32),
        compiler_params=pltpu.CompilerParams(vmem_limit_bytes=VMEM_LIMIT),
        cost_estimate=cost(2.5, 0.05),
        name="xhat",
    )(*pieces)


def qkv_kernel(count, where_ref, small_ref, *refs):
    xhats, pieces = refs[:4], refs[4 : 4 + count]
    norm_ref, packed_ref, wq_ref, wo_ref, w_ref, x_ref, sems, x_sems = refs[4 + count :]
    step = pl.program_id(0)
    width = wq_ref.shape[1]

    def fetch(r):
        return pltpu.make_async_copy(xhats[r], x_ref.at[r % 2], x_sems.at[r % 2])

    @pl.when(step == 0)
    def _():
        fetch(0).start()
        copies = []
        for i, piece in enumerate(pieces):
            size = piece.shape[0]
            start = pl.multiple_of(where_ref[i] * size, size)
            copies.append(pltpu.make_async_copy(piece, w_ref.at[pl.ds(start, size)], sems.at[i]))
            copies[-1].start()
        for copy in copies:
            copy.wait()
        wq_ref[...] = w_ref[:, :width]
        wo_ref[...] = w_ref[:, width : width + wo_ref.shape[1]]

    for r in range(4):

        @pl.when(step == r)
        def _(r=r):
            if r < 3:
                fetch(r + 1).start()
            fetch(r).wait()

    norm = (x_ref[lax.rem(step, 2)] * small_ref[0:1] + small_ref[1:2]).astype(bf16)
    norm_ref[...] = norm
    packed_ref[...] = dot(norm, wq_ref[...]).astype(bf16)


def qkv_of(where, small, xhats, pieces, width):
    slot, model = xhats[0].shape
    total = pieces[0].shape[1]
    out = model // 4
    whole = lambda shape: pl.BlockSpec(shape, lambda i: (0, 0))
    rows = lambda cols: pl.BlockSpec((slot, cols), lambda i: (i, 0))
    return pl.pallas_call(
        functools.partial(qkv_kernel, len(pieces)),
        grid=(4,),
        in_specs=[pl.BlockSpec(memory_space=pltpu.SMEM), whole(small.shape)]
        + [pl.BlockSpec(memory_space=pl.ANY)] * (4 + len(pieces)),
        out_specs=[rows(model), rows(width), whole((model, width)), whole((model, out))],
        out_shape=[
            jax.ShapeDtypeStruct((4 * slot, model), bf16),
            jax.ShapeDtypeStruct((4 * slot, width), bf16),
            jax.ShapeDtypeStruct((model, width), bf16),
            jax.ShapeDtypeStruct((model, out), bf16),
        ],
        scratch_shapes=[
            pltpu.VMEM((model, total), bf16),
            pltpu.VMEM((2, slot, model), f32),
            pltpu.SemaphoreType.DMA((len(pieces),)),
            pltpu.SemaphoreType.DMA((2,)),
        ],
        compiler_params=pltpu.CompilerParams(vmem_limit_bytes=VMEM_LIMIT),
        cost_estimate=cost(7, 0.05),
        name="qkv",
    )(where, small, *xhats, *pieces)


def ln1_back_kernel(gp_ref, wq_ref, x0_ref, x1_ref, p0_ref, p1_ref, vec_ref):
    step = pl.program_id(0)
    grad = dot(gp_ref[...], wq_ref[...], NT)

    @pl.when(step == 0)
    def _():
        vec_ref[0:1] = jnp.sum(grad * x0_ref[...], axis=0, keepdims=True)
        vec_ref[1:2] = jnp.sum(grad, axis=0, keepdims=True)
        p0_ref[...] = grad.astype(p0_ref.dtype)

    @pl.when(step == 1)
    def _():
        vec_ref[0:1] += jnp.sum(grad * x1_ref[...], axis=0, keepdims=True)
        vec_ref[1:2] += jnp.sum(grad, axis=0, keepdims=True)
        p1_ref[...] = grad.astype(p1_ref.dtype)


def ln1_back(grad_packed, wqkv, xhats, first):
    slot, model = xhats[0].shape
    width = wqkv.shape[1]
    whole = lambda shape: pl.BlockSpec(shape, lambda i: (0, 0))
    return pl.pallas_call(
        ln1_back_kernel,
        grid=(2,),
        in_specs=[
            pl.BlockSpec((slot, width), lambda i: (first + i, 0)),
            whole((model, width)),
            whole((slot, model)),
            whole((slot, model)),
        ],
        out_specs=[whole((slot, model)), whole((slot, model)), whole((2, model))],
        out_shape=[
            jax.ShapeDtypeStruct((slot, model), bf16 if first else f32),
            jax.ShapeDtypeStruct((slot, model), bf16),
            jax.ShapeDtypeStruct((2, model), f32),
        ],
        compiler_params=pltpu.CompilerParams(vmem_limit_bytes=VMEM_LIMIT),
        cost_estimate=cost(5, 0.1 if first else 1.0),
        name="ln1_back",
    )(grad_packed, wqkv, *xhats)


def attn_fwd_kernel(len_ref, qkv_ref, tiles_ref, att_ref, p_ref):
    slot = qkv_ref.shape[0]
    blocks = range(slot // TILE)
    heads = range(2)
    length = len_ref[0]
    lane = lax.broadcasted_iota(jnp.int32, (1, PAIR), 1)
    col = lax.broadcasted_iota(jnp.int32, (1, slot), 1)
    hidden = jnp.where(col < length, 0.0, neg_large)
    q = qkv_ref[:, :PAIR] * HEAD_DIM ** (-0.5)
    k = qkv_ref[:, PAIR : 2 * PAIR]
    v = qkv_ref[:, 2 * PAIR :]
    own = [(lane // HEAD_DIM) == hh for hh in heads]
    qm = [jnp.where(own[hh], q, jnp.zeros_like(q)) for hh in heads]
    span = [(i + 1) * TILE for i in blocks]
    items = [(hh, i) for hh in heads for i in blocks]
    s = [dot(qm[hh][i * TILE : span[i]], k[: span[i]], NT) for hh, i in items]
    s = [
        x + jnp.concatenate([tiles_ref[hh, i - j] for j in range(i + 1)], axis=1) + hidden[:, : span[i]]
        for x, (hh, i) in zip(s, items)
    ]
    top = [jnp.max(x, axis=1, keepdims=True) for x in s]
    e = [jnp.exp(x - m) for x, m in zip(s, top)]
    scale = [1.0 / jnp.sum(x, axis=1, keepdims=True) for x in e]
    probs = [(x * r).astype(bf16) for x, r in zip(e, scale)]
    for x, (hh, i) in zip(probs, items):
        p_ref[hh, i * TILE : span[i], : span[i]] = x
    o = {item: dot(x, v[: span[item[1]]]) for x, item in zip(probs, items)}
    for i in blocks:
        att_ref[i * TILE : span[i], :] = jnp.where(own[0], o[0, i], o[1, i]).astype(bf16)


def attn_fwd(lengths, packed, tiles, seq):
    heads, count = tiles.shape[:2]
    slot = count * TILE
    return pl.pallas_call(
        attn_fwd_kernel,
        grid=(heads // 2,),
        in_specs=[
            pl.BlockSpec(memory_space=pltpu.SMEM),
            pl.BlockSpec((slot, 3 * PAIR), lambda p: (seq, p)),
            pl.BlockSpec((2, count, TILE, TILE), lambda p: (p, 0, 0, 0)),
        ],
        out_specs=[
            pl.BlockSpec((slot, PAIR), lambda p: (0, p)),
            pl.BlockSpec((2, slot, slot), lambda p: (p, 0, 0)),
        ],
        out_shape=[
            jax.ShapeDtypeStruct((slot, heads * HEAD_DIM), bf16),
            jax.ShapeDtypeStruct((heads, slot, slot), bf16),
        ],
        compiler_params=pltpu.CompilerParams(vmem_limit_bytes=VMEM_LIMIT),
        cost_estimate=cost(4.5, 0.1),
        name="attn_fwd",
    )(lengths, packed, tiles)


def attn_bwd_kernel(qkv_ref, ga_ref, att_ref, p_ref, *refs):
    g_ref, sum_ref, ds_ref = refs[-3:]
    slot = qkv_ref.shape[0]
    blocks = range(slot // TILE)
    heads = range(2)
    lane = lax.broadcasted_iota(jnp.int32, (1, PAIR), 1)
    scale = HEAD_DIM ** (-0.5)
    q = qkv_ref[:, :PAIR] * scale
    k = qkv_ref[:, PAIR : 2 * PAIR]
    v = qkv_ref[:, 2 * PAIR :]
    ga = ga_ref[...]
    prod = ga.astype(f32) * att_ref[...].astype(f32)
    own = [(lane // HEAD_DIM) == hh for hh in heads]
    gam = [jnp.where(own[hh], ga, jnp.zeros_like(ga)) for hh in heads]
    inner = [jnp.sum(jnp.where(own[hh], prod, 0.0), axis=1, keepdims=True) for hh in heads]
    span = [(i + 1) * TILE for i in blocks]
    rows = [slice(i * TILE, span[i]) for i in blocks]
    items = [(hh, i) for hh in heads for i in blocks]
    dp = [dot(gam[hh][rows[i]], v[: span[i]], NT) for hh, i in items]
    ds = {
        (hh, i): (p_ref[hh, rows[i], : span[i]].astype(f32) * (x - inner[hh][rows[i]])).astype(bf16)
        for x, (hh, i) in zip(dp, items)
    }
    for hh, i in items:
        ds_ref[hh, rows[i], : span[i]] = ds[hh, i]
    dq = {(hh, i): dot(ds[hh, i], k[: span[i]]) for hh, i in items}
    dv = {(hh, j): dot(p_ref[hh, j * TILE :, rows[j]], ga[j * TILE :], TN) for hh, j in items}
    dk = {(hh, j): dot(ds_ref[hh, j * TILE :, rows[j]], q[j * TILE :], TN) for hh, j in items}
    for i in blocks:
        for at, got, factor in ((0, dq, scale), (PAIR, dk, 1.0), (2 * PAIR, dv, 1.0)):
            both = jnp.where(own[0], got[0, i], got[1, i]) * factor
            g_ref[rows[i], at : at + PAIR] = both.astype(bf16)
    row = lax.broadcasted_iota(jnp.int32, (TILE, TILE), 0)
    col = lax.broadcasted_iota(jnp.int32, (TILE, TILE), 1)
    flip = jnp.where(row + col == TILE - 1, 1.0, 0.0).astype(bf16)
    diag = {}
    for hh in heads:
        for delta in blocks:
            parts = [
                ds[hh, i][:, (i - delta) * TILE : (i - delta + 1) * TILE].astype(f32)
                for i in blocks
                if i >= delta
            ]
            diag[hh, delta] = functools.reduce(jnp.add, parts)
    high = {key: x.astype(bf16) for key, x in diag.items()}
    low = {key: (x - high[key].astype(f32)).astype(bf16) for key, x in diag.items()}
    turned = {key: dot(flip, high[key]) + dot(flip, low[key]) for key in diag}
    sums = {}
    for key, x in turned.items():
        wide = jnp.concatenate([x, jnp.zeros_like(x)], axis=1)
        wide = pltpu.roll(wide, 0, 1, stride=1, stride_axis=0)
        sums[key] = jnp.sum(wide, axis=0, keepdims=True)
    for hh in heads:
        for delta in blocks:
            here = sums[hh, delta][:, :TILE]
            if delta + 1 in blocks:
                here = here + sums[hh, delta + 1][:, TILE:]
            sum_ref[0, hh : hh + 1, rows[delta]] = here


def attn_bwd(packed, ga, att, probs, seq, into):
    heads, slot = probs.shape[:2]
    steps = heads // 2
    return pl.pallas_call(
        attn_bwd_kernel,
        grid=(steps,),
        in_specs=[
            pl.BlockSpec((slot, 3 * PAIR), lambda p: (seq, p)),
            pl.BlockSpec((slot, PAIR), lambda p: (0, p)),
            pl.BlockSpec((slot, PAIR), lambda p: (0, p)),
            pl.BlockSpec((2, slot, slot), lambda p: (p, 0, 0)),
        ]
        + ([] if into is None else [pl.BlockSpec(memory_space=pl.ANY)]),
        out_specs=[
            pl.BlockSpec((slot, 3 * PAIR), lambda p: (seq, p)),
            pl.BlockSpec((1, 2, slot), lambda p: (p, 0, 0)),
        ],
        out_shape=[
            jax.ShapeDtypeStruct(packed.shape, bf16),
            jax.ShapeDtypeStruct((steps, 2, slot), f32),
        ],
        scratch_shapes=[pltpu.VMEM((2, slot, slot), bf16)],
        input_output_aliases={} if into is None else {4: 0},
        compiler_params=pltpu.CompilerParams(vmem_limit_bytes=VMEM_LIMIT),
        cost_estimate=cost(5, 0.2),
        name="attn_bwd",
    )(packed, ga, att, probs, *(() if into is None else (into,)))


def ln1_last_kernel(tok_ref, xhat_ref, gmid_ref, small_ref, p0_ref, p1_ref, p2_ref, p3_ref, out_ref):
    _, factor = normalized(tok_ref[...].astype(f32))
    xhat = xhat_ref[...]
    low = pl.program_id(0) == 0
    e = p0_ref[...] + p1_ref[...].astype(f32) + jnp.where(low, p2_ref[...], p3_ref[...]).astype(f32)
    e = e * small_ref[0:1]
    out_ref[...] = gmid_ref[...] + factor * (
        e - jnp.mean(e, axis=-1, keepdims=True) - xhat * jnp.mean(e * xhat, axis=-1, keepdims=True)
    )


def ln1_last(tokens, xhat, grad_middle, small, p0, p1, p2, p3):
    slot, model = tokens.shape
    row = pl.BlockSpec((slot // 2, model), lambda i: (i, 0))
    part = pl.BlockSpec((slot // 2, model), lambda i: (0, 0))
    return pl.pallas_call(
        ln1_last_kernel,
        grid=(2,),
        in_specs=[row] * 3 + [block_of(small), row, row, part, part],
        out_specs=row,
        out_shape=jax.ShapeDtypeStruct((slot, model), f32),
        compiler_params=pltpu.CompilerParams(vmem_limit_bytes=VMEM_LIMIT),
        cost_estimate=cost(5, 0.05),
        name="ln1_last",
    )(tokens, xhat, grad_middle, small, p0, p1, p2, p3)


def quarters(n, r, size):
    return pl.ds(pl.multiple_of(lax.bitwise_xor(n, r) * size, size), size)


def out_ln2_kernel(part, n_ref, len_ref, tok_ref, small_ref, *refs):
    atts, wouts = refs[:4], refs[4:8]
    mid_ref, all_ref, norm_ref = refs[-3:]
    n = n_ref[0]
    rows, model = tok_ref.shape
    size = model // 4
    for r in range(4):
        all_ref[:, quarters(n, r, size)] = atts[r][...]
    valid = part * rows + lax.broadcasted_iota(jnp.int32, (rows, 1), 0) < len_ref[0]
    for r in range(4):
        cols = quarters(n, r, size)
        out = dot(all_ref[...], wouts[r][...])
        mid_ref[:, cols] = tok_ref[:, cols].astype(f32) + jnp.where(valid, out, 0.0)
    xhat, _ = normalized(mid_ref[...])
    norm_ref[...] = (xhat * small_ref[2:3] + small_ref[3:4]).astype(bf16)


def out_ln2(n, length, tokens, small, atts, wouts, part, into):
    slot, model = tokens.shape
    smem = pl.BlockSpec(memory_space=pltpu.SMEM)
    whole = lambda x: pl.BlockSpec(x.shape, lambda i: (0, 0))
    rows = lambda cols: pl.BlockSpec((slot // 2, cols), lambda i: (part, 0))
    return pl.pallas_call(
        functools.partial(out_ln2_kernel, part),
        grid=(1,),
        in_specs=[smem, smem, rows(model), whole(small)]
        + [rows(model // 4)] * 4
        + [whole(w) for w in wouts]
        + [pl.BlockSpec(memory_space=pl.ANY)] * len(into),
        out_specs=[rows(model), rows(model), pl.BlockSpec((slot // 2, model), lambda i: (0, 0))],
        out_shape=[
            jax.ShapeDtypeStruct((slot, model), f32),
            jax.ShapeDtypeStruct((slot, model), bf16),
            jax.ShapeDtypeStruct((slot // 2, model), bf16),
        ],
        input_output_aliases={12 + i: i for i in range(len(into))},
        compiler_params=pltpu.CompilerParams(vmem_limit_bytes=VMEM_LIMIT),
        cost_estimate=cost(4, 1 / 64),
        name="out_ln2",
    )(n, length, tokens, small, *atts, *wouts, *into)


def ln2_back_kernel(part, n_ref, len_ref, mid_ref, cot_ref, small_ref, p0_ref, p2_ref, *refs):
    near, wouts = refs[:2], refs[2:6]
    gmid_ref, keep_ref, send_ref = refs[-9:-6]
    gatts = refs[-6:-2]
    vec_ref, branch_ref = refs[-2:]
    n = n_ref[0]
    rows, model = mid_ref.shape
    size = model // 4
    xhat, factor = normalized(mid_ref[...])
    grad = p0_ref[...] + p2_ref[...].astype(f32)
    grad = grad + jnp.concatenate([x[...] for x in near], axis=0).astype(f32)
    vec_ref[0:1] = jnp.sum(grad * xhat, axis=0, keepdims=True)
    vec_ref[1:2] = jnp.sum(grad, axis=0, keepdims=True)
    e = grad * small_ref[2:3]
    back = factor * (
        e - jnp.mean(e, axis=-1, keepdims=True) - xhat * jnp.mean(e * xhat, axis=-1, keepdims=True)
    )
    gmid = cot_ref[...].astype(f32) + back
    gmid_ref[...] = gmid
    valid = part * rows + lax.broadcasted_iota(jnp.int32, (rows, 1), 0) < len_ref[0]
    branch_ref[...] = jnp.where(valid, gmid, 0.0).astype(bf16)
    cuts = [branch_ref[:, quarters(n, r, size)] for r in range(4)]
    keep_ref[:, :size] = cuts[0]
    keep_ref[:, size:] = cuts[2]
    send_ref[:, :size] = cuts[1]
    send_ref[:, size:] = cuts[3]
    for r in range(4):
        feats = quarters(n, r, size)
        total = dot(cuts[0], wouts[0][feats, :], NT)
        for k in range(1, 4):
            total = total + dot(cuts[k], wouts[k][feats, :], NT)
        gatts[r][...] = total.astype(bf16)


def ln2_back(n, length, middle, cot, small, p0, near, p2, wouts, part, into):
    slot, model = middle.shape
    smem = pl.BlockSpec(memory_space=pltpu.SMEM)
    whole = lambda x: pl.BlockSpec(x.shape, lambda i: (0, 0))
    rows = lambda cols: pl.BlockSpec((slot // 2, cols), lambda i: (part, 0))
    return pl.pallas_call(
        functools.partial(ln2_back_kernel, part),
        grid=(1,),
        in_specs=[smem, smem, rows(model), rows(model), whole(small), rows(model), whole(p2)]
        + [whole(w) for w in (*near, *wouts)]
        + [pl.BlockSpec(memory_space=pl.ANY)] * len(into),
        out_specs=[rows(model), rows(model // 2), rows(model // 2)]
        + [rows(model // 4)] * 4
        + [pl.BlockSpec((2, model), lambda i: (0, 0))],
        out_shape=[
            jax.ShapeDtypeStruct((slot, model), f32),
            jax.ShapeDtypeStruct((slot, model // 2), bf16),
            jax.ShapeDtypeStruct((slot, model // 2), bf16),
        ]
        + [jax.ShapeDtypeStruct((slot, model // 4), bf16)] * 4
        + [jax.ShapeDtypeStruct((2, model), f32)],
        scratch_shapes=[pltpu.VMEM((slot // 2, model), bf16)],
        input_output_aliases={13 + i: i for i in range(len(into))},
        compiler_params=pltpu.CompilerParams(vmem_limit_bytes=VMEM_LIMIT),
        cost_estimate=cost(5),
        name="ln2_back",
    )(n, length, middle, cot, small, p0, p2, *near, *wouts, *into)


def gelu_both(u):
    c0 = 0.7978845608028654
    c1 = 0.044715
    sq = u * u
    t = jnp.tanh(u * (c0 + (c0 * c1) * sq))
    half = 0.5 + 0.5 * t
    slope = half + (1.0 - t * t) * (u * (0.5 * c0 + (1.5 * c0 * c1) * sq))
    return u * half, slope


def ffn_kernel(count, places, start, cuts, w_any, *refs):
    norms, grads = refs[:count], refs[count : count + len(places)]
    n4_any, g4_any, hid4_any, gua4_any = refs[-13:-9]
    sums = refs[-16 - cuts : -13]
    o0_ref, gn0_ref = sums[:2]
    n_ref, g_ref, wu_ref, wd_ref, hid_ref, gua_ref, sems, w_sems, out_sems = refs[-9:]
    step = pl.program_id(0)
    steps = pl.num_programs(0) // 2
    rows = n_ref.shape[0]
    block = o0_ref.shape[1]
    mine = pl.ds(start, rows)
    outs = [
        pltpu.make_async_copy(src, dst.at[mine], out_sems.at[i])
        for i, (src, dst) in enumerate(
            ((n_ref, n4_any), (g_ref, g4_any), (hid_ref, hid4_any), (gua_ref, gua4_any))
        )
    ]
    shards, _, size, _ = w_any.shape
    weights = [
        [
            pltpu.make_async_copy(
                w_any.at[d, i], whole.at[pl.ds(d * size, size)], w_sems.at[d, i]
            )
            for d in range(shards)
        ]
        for i, whole in enumerate((wu_ref, wd_ref))
    ]
    acts = []
    grads = [g.at[pl.ds(first, size)] for g, (first, size) in zip(grads, places)]
    for j, (pieces, whole) in enumerate(((norms, n_ref), (grads, g_ref))):
        acts.append([])
        at = 0
        for i, piece in enumerate(pieces):
            here = piece.shape[0]
            acts[j].append(
                pltpu.make_async_copy(piece, whole.at[pl.ds(at, here)], sems.at[j, i])
            )
            at += here

    @pl.when(step == 0)
    def _():
        for copy in acts[0] + weights[0] + acts[1] + weights[1]:
            copy.start()
        for copy in acts[0] + weights[0]:
            copy.wait()

    @pl.when(step < steps)
    def _():
        cols = pl.ds(pl.multiple_of(step * block, block), block)
        u = dot(n_ref[...], wu_ref[:, cols])
        hid, slope = gelu_both(u)

        @pl.when(step == 0)
        def _():
            for copy in acts[1] + weights[1]:
                copy.wait()

        gh = dot(g_ref[...], wd_ref[cols, :], NT)
        hid_ref[:, cols] = hid.astype(bf16)
        gua_ref[:, cols] = (slope * gh).astype(bf16)

    @pl.when(step == steps)
    def _():
        for copy in outs:
            copy.start()

    @pl.when(step >= steps)
    def _():
        cols = pl.ds(pl.multiple_of((step - steps) * block, block), block)
        half = rows // 2
        gn = dot(gua_ref[...], wu_ref[cols, :], NT)
        o = dot(hid_ref[...], wd_ref[:, cols])
        for first, pieces, total in ((o0_ref, sums[2:3], o), (gn0_ref, sums[3:], gn)):
            first[...] = total[:half]
            size = half // len(pieces)
            for i, piece in enumerate(pieces):
                piece[...] = total[half + i * size : half + (i + 1) * size].astype(bf16)

    @pl.when(step == 2 * steps - 1)
    def _():
        for copy in outs:
            copy.wait()


def ffn(norms, grads, places, weights, start, into, cuts):
    width = norms[0].shape[1]
    rows = sum(x.shape[0] for x in norms)
    total = into[0].shape[0] if into else 2 * rows
    units = weights.shape[0] * weights.shape[2]
    block = min(512, units)
    steps = units // block
    half = rows // 2
    anywhere = pl.BlockSpec(memory_space=pl.ANY)
    late = lambda size: pl.BlockSpec((size, block), lambda i: (0, jnp.maximum(i - steps, 0)))
    acts = pltpu.VMEM((rows, width), bf16)
    hidden = pltpu.VMEM((rows, units), bf16)
    ins = 1 + len(norms) + len(grads)
    outs = 3 + cuts
    got = pl.pallas_call(
        functools.partial(ffn_kernel, len(norms), places, start, cuts),
        grid=(2 * steps,),
        in_specs=[anywhere] * (ins + len(into)),
        out_specs=[late(half)] * 2 + [late(half)] + [late(half // cuts)] * cuts + [anywhere] * 4,
        out_shape=[jax.ShapeDtypeStruct((half, width), f32)] * 2
        + [jax.ShapeDtypeStruct((half, width), bf16)]
        + [jax.ShapeDtypeStruct((half // cuts, width), bf16)] * cuts
        + [jax.ShapeDtypeStruct((total, width), bf16)] * 2
        + [jax.ShapeDtypeStruct((total, units), bf16)] * 2,
        scratch_shapes=[
            acts,
            acts,
            pltpu.VMEM((width, units), bf16),
            pltpu.VMEM((units, width), bf16),
            hidden,
            hidden,
            pltpu.SemaphoreType.DMA((2, max(len(norms), len(grads)))),
            pltpu.SemaphoreType.DMA((weights.shape[0], 2)),
            pltpu.SemaphoreType.DMA((4,)),
        ],
        input_output_aliases={ins + i: outs + i for i in range(len(into))},
        compiler_params=pltpu.CompilerParams(vmem_limit_bytes=VMEM_LIMIT),
        cost_estimate=cost(8 if into else 12, 1 / 64),
        name="ffn",
    )(weights, *norms, *grads, *into)
    return got[0], got[2], got[1], got[3:outs], got[outs:]


def pack_small_kernel(heads, n_ref, y_ref, one_ref, also_ref, two_ref, more_ref, buckets_ref, *refs):
    dists, (keep_ref, send_ref) = refs[:-2], refs[-2:]
    n = n_ref[0]
    odd = y_ref[0] == 1
    slot = buckets_ref.shape[1]
    total = dists[0][...]
    for ref in dists[1:]:
        total = total + ref[...]
    lanes = heads * BUCKETS
    bucket = lax.broadcasted_iota(jnp.int32, (lanes, slot), 0) % BUCKETS
    onehot = (buckets_ref[...] == bucket).astype(f32).astype(bf16)
    lane = lax.broadcasted_iota(jnp.int32, (1, lanes), 1)
    table = jnp.zeros((1, lanes), f32)
    for h in range(heads):
        row = jnp.broadcast_to(total[h // 2, h % 2 : h % 2 + 1], (8, slot))
        parts = []
        for _ in range(3):
            low = row.astype(bf16)
            parts.append(dot(low, onehot, NT))
            row = row - low.astype(f32)
        got = (parts[0] + parts[1] + parts[2])[0:1]
        table = jnp.where(lane // BUCKETS == h, got, table)
    zeros = jnp.zeros((1, TILE), f32)
    half = lanes // 2
    low = jnp.where(lane < half, table, 0.0)
    high = jnp.where(lane < half, pltpu.roll(table, half, 1), 0.0)
    for z in range(keep_ref.shape[0]):
        both = []
        for b, share in ((0, low), (1, high)):
            d = 2 * z + b
            cols = slice(d * TILE, (d + 1) * TILE)
            rel = jnp.where(d == 2 * n + b, share, zeros)
            both.append(
                jnp.concatenate(
                    [
                        one_ref[:, cols] + also_ref[:, cols],
                        two_ref[:, cols] + more_ref[:, cols],
                        rel,
                        zeros,
                        zeros,
                        zeros,
                    ],
                    axis=0,
                )
            )
        keep_ref[z] = jnp.where(odd, both[1], both[0])
        send_ref[z] = jnp.where(odd, both[0], both[1])


def pack_small(n, y, grad_one, grad_two, buckets, dists, heads):
    slot = buckets.shape[0]
    model = grad_one[0].shape[1]
    smem = pl.BlockSpec(memory_space=pltpu.SMEM)
    operands = [*grad_one, *grad_two, buckets.reshape(1, slot), *dists]
    shape = jax.ShapeDtypeStruct((model // TILE // 2, 8, TILE), f32)
    return pl.pallas_call(
        functools.partial(pack_small_kernel, heads),
        grid=(1,),
        in_specs=[smem, smem] + [block_of(x) for x in operands],
        out_specs=[pl.BlockSpec(shape.shape, lambda i: (0, 0, 0))] * 2,
        out_shape=[shape, shape],
        cost_estimate=cost(3),
        name="pack_small",
    )(n, y, *operands)


def join_ffn_kernel(quarter, n_ref, *refs):
    ins, (up_ref, down_ref) = refs[:4], refs[4:]
    model = down_ref.shape[1]
    rows = up_ref.shape[0]
    for r in range(4):
        j = lax.bitwise_xor(n_ref[0], r)
        for d in range(model // quarter):
            start = pl.multiple_of((d * 4 + j) * quarter, quarter)
            up_ref[:, pl.ds(start, quarter)] = ins[r][:, d * quarter : (d + 1) * quarter].astype(f32)
        down_ref[pl.ds(pl.multiple_of(j * quarter, quarter), quarter), :] = ins[r][:, model:].astype(f32)


def join_ffn(n, parts, quarter):
    rows, both = parts[0].shape
    model = both // 2
    shapes = [(rows, 4 * model), (4 * quarter, model)]
    if quarter % TILE:
        wide = model // quarter
        rel = jnp.stack(parts)
        rel = jnp.stack(
            [lax.dynamic_index_in_dim(rel, n[0] ^ j, 0, keepdims=False) for j in range(4)]
        ).astype(f32)
        up = rel[:, :, :model].reshape(4, rows, wide, quarter).transpose(1, 2, 0, 3)
        return up.reshape(shapes[0]), rel[:, :, model:].reshape(shapes[1])
    return pl.pallas_call(
        functools.partial(join_ffn_kernel, quarter),
        grid=(1,),
        in_specs=[pl.BlockSpec(memory_space=pltpu.SMEM)] + [block_of(x) for x in parts],
        out_specs=[pl.BlockSpec(x, lambda i: (0, 0)) for x in shapes],
        out_shape=[jax.ShapeDtypeStruct(x, f32) for x in shapes],
        compiler_params=pltpu.CompilerParams(vmem_limit_bytes=VMEM_LIMIT),
        cost_estimate=cost(4, 0.05),
        name="join_ffn",
    )(n, *parts)


def join_attn_kernel(n_ref, *refs):
    ins, (qkv_ref, out_ref) = refs[:4], refs[4:]
    model = out_ref.shape[1]
    mine = model // 4
    for r in range(4):
        j = lax.bitwise_xor(n_ref[0], r)
        at = 0
        for p in range(mine // PAIR):
            for part in range(3):
                start = pl.multiple_of(part * model + j * mine + p * PAIR, PAIR)
                qkv_ref[:, pl.ds(start, PAIR)] = ins[r][:, at : at + PAIR].astype(f32)
                at += PAIR
        out_ref[:, pl.ds(pl.multiple_of(j * mine, mine), mine)] = ins[r][
            :, at : at + mine
        ].astype(f32) + ins[r ^ 2][:, at + mine :].astype(f32)


def join_attn(n, parts, model):
    rows = parts[0].shape[0]
    shapes = [(rows, 3 * model), (rows, model)]
    return pl.pallas_call(
        join_attn_kernel,
        grid=(1,),
        in_specs=[pl.BlockSpec(memory_space=pltpu.SMEM)] + [block_of(x) for x in parts],
        out_specs=[pl.BlockSpec(x, lambda i: (0, 0)) for x in shapes],
        out_shape=[jax.ShapeDtypeStruct(x, f32) for x in shapes],
        cost_estimate=cost(3),
        name="join_attn",
    )(n, *parts)


def ring_order(size):
    return list(range(0, size, 2)) + list(range(size - 1, 0, -2))


def ring_member(pos, size):
    pos = lax.rem(pos + 2 * size, size)
    return jnp.where(pos < size // 2, 2 * pos, 2 * (size - 1 - pos) + 1)


def ring_pairs(narrow, size):
    order = ring_order(size)
    pairs = []
    for n in range(narrow):
        turn = 1 if n % 2 == 0 else -1
        for p in range(size):
            pairs.append((n * size + order[p], n * size + order[(p + turn) % size]))
    return pairs


class Places:
    def __init__(self):
        self.narrow = lax.axis_size("narrow")
        self.wide = lax.axis_size("wide")
        self.n = lax.axis_index("narrow")
        self.w = lax.axis_index("wide")
        self.core = lax.rem(self.n, 2)
        self.turn = 1 - 2 * self.core
        self.y = lax.rem(self.w, 2)
        self.z = self.w // 2
        self.pos = jnp.where(self.y == 0, self.z, self.wide - 1 - self.z)
        self.pairs = ring_pairs(self.narrow, self.wide)
        self.rings = self.wide <= 16

    def ring(self, x, way):
        pairs = self.pairs if way == 0 else [(b, a) for a, b in self.pairs]
        return lax.ppermute(x, ("narrow", "wide"), pairs)

    def member(self, steps):
        return ring_member(self.pos + self.turn * steps, self.wide)

    def swap(self, x, bit):
        return lax.ppermute(x, "narrow", [(i, i ^ bit) for i in range(self.narrow)])

    def all_narrow(self, x):
        far = self.swap(x, 2)
        return [x, self.swap(x, 1), far, self.swap(far, 1)]

    def swap_y(self, x):
        return lax.ppermute(x, "wide", [(i, i ^ 1) for i in range(self.wide)])

    def along_z(self, x, steps):
        return lax.ppermute(
            x, "wide", [(i, (i + 2 * steps) % self.wide) for i in range(self.wide)]
        )


def row_major(x):
    return with_layout_constraint(x, Layout(major_to_minor=tuple(range(x.ndim))))


def after(x, *deps):
    return lax.optimization_barrier((x, *deps))[0]


def add_low(*terms):
    return sum(t.astype(f32) for t in terms).astype(bf16)


def gather_ring(at, piece, holds):
    pieces, steps = [piece], [0]
    ahead = behind = piece
    far = at.wide // 2
    for k in range(1, far + 1):
        ahead = at.ring(ahead, 0)
        came = [ahead]
        if k < far:
            behind = at.ring(behind, 1)
            came.append(behind)
        held = holds[k](*came) if k in holds else ()
        came = lax.optimization_barrier((*came, *held))
        ahead = came[0]
        if k < far:
            behind = came[1]
            pieces.append(behind)
            steps.append(k)
        pieces.append(ahead)
        steps.append(-k)
    return pieces, steps


def reduce_ring(at, parts):
    size = at.wide

    def chunk(k):
        member = at.member(k)
        cut = [lax.dynamic_index_in_dim(p, member, 0, keepdims=False) for p in parts]
        return row_major(jnp.concatenate(cut, axis=1) if len(cut) > 1 else cut[0])

    far = size // 2
    ahead, behind = chunk(far), chunk(1 - far)
    yield ahead, behind
    for k in range(far - 1, 0, -1):
        ahead, behind = at.ring(ahead, 0), at.ring(behind, 1)
        held = yield ahead, behind
        ahead, behind, *_ = lax.optimization_barrier((ahead, behind, *(held or ())))
        ahead = row_major(add_low(ahead, chunk(k)))
        if k > 1:
            behind = row_major(add_low(behind, chunk(1 - k)))
        yield ahead, behind
    ahead = at.ring(ahead, 0)
    held = yield (ahead,)
    ahead, *_ = lax.optimization_barrier((ahead, *(held or ())))
    yield row_major(add_low(chunk(0), ahead, behind))


def scatter(at, parts):
    return jnp.concatenate(
        [lax.psum_scatter(p, "wide", scatter_dimension=0, tiled=True)[0] for p in parts], axis=1
    )


def local(
    tokens,
    lengths,
    buckets,
    ln1_gain,
    ln1_bias,
    w_qkv,
    rel_table,
    w_out,
    ln2_gain,
    ln2_bias,
    w_up,
    w_down,
    cotangent,
):
    at = Places()
    wide = at.wide
    slot, model = tokens.shape
    backwards = buckets.reshape(-1, TILE)[:, ::-1].reshape(slot)
    rows = w_qkv.shape[0]
    ff = w_up.shape[1]
    ff_rows = w_down.shape[0]
    quarter = ff_rows // 4
    heads = HEADS // 4
    width = 3 * model // 4
    rel_rows = rel_table.shape[0]
    n = at.n.reshape(1)
    far = wide // 2

    cut = slot // 16 * 7
    tokens_far = [at.swap(tokens[:cut], 2), at.swap(tokens[cut:], 2)]
    tokens_all = [[tokens], [at.swap(tokens, 1)], tokens_far, [at.swap(t, 1) for t in tokens_far]]

    lengths_far = at.swap(after(lengths, tokens_far[0]), 2)
    lengths_all = [lengths, at.swap(lengths, 1), lengths_far, at.swap(lengths_far, 1)]

    vectors = [ln1_gain, ln1_bias, ln2_gain, ln2_bias, rel_table]
    vectors = jnp.stack([jnp.pad(s, (0, TILE - s.shape[0])) for s in vectors])
    vectors = jnp.pad(vectors, ((0, 16 - vectors.shape[0]), (0, 0)))
    if at.rings:
        attn_piece = cut_attn(n, w_qkv, w_out, vectors)
        ffn_piece = cut_ffn(n, after(w_up, attn_piece), w_down)
        came, xhats = [], []

        def hold(x, *deps):
            xhats.append(xhat_of([after(t, *deps) for t in x]))
            return xhats[-1]

        pieces, steps = gather_ring(
            at,
            attn_piece,
            {
                1: lambda *x: [ffn_piece, tokens_far[0]],
                2: lambda *x: [
                    lengths_far,
                    tokens_far[1],
                    hold(tokens_all[0], *x),
                    hold(tokens_all[1], *x),
                ],
                3: lambda *x: came.extend(x) or lengths_all[1::2],
            },
        )
        hold(tokens_all[2], *came)
        hold(tokens_all[3], *came)
        ffn_piece = after(ffn_piece, *came)
        where = jnp.stack([at.member(k) for k in steps])
        small = small_rows(where, pieces, model)
    else:
        pick = lambda x, axis: lax.dynamic_index_in_dim(x, at.n, axis, keepdims=False)
        cut = pick(w_qkv.reshape(rows, 3, 4, heads // 2, PAIR), 2)
        cut = cut.transpose(0, 2, 1, 3).reshape(rows, width)
        cut = [cut, pick(w_out.reshape(rows, 4, model // 4), 1), jnp.zeros((rows, TILE), bf16)]
        attn_piece = jnp.concatenate(cut, axis=1)
        ffn_piece = jnp.stack(
            [
                pick(w_up.reshape(rows, wide, 4, quarter), 2).reshape(rows, wide * quarter),
                pick(w_down.reshape(4, quarter, model), 0),
            ]
        )
        pieces = [lax.all_gather(attn_piece, "wide", axis=0, tiled=True)]
        where = jnp.zeros((1,), jnp.int32)
        small = lax.all_gather(vectors, "wide", axis=0).astype(f32)
        small = [small[:, i, :rows].reshape(1, model) for i in range(4)] + [
            jnp.pad(small[:, 4, :rel_rows].reshape(1, -1), ((0, 0), (0, model - HEADS * BUCKETS)))
        ]
        small = jnp.pad(jnp.concatenate(small, axis=0), ((0, 3), (0, 0)))
    w_ffn = lax.all_gather(ffn_piece, "wide", axis=0)

    if not at.rings:
        xhats = [xhat_of(t) for t in tokens_all]
    valid = (jnp.arange(slot, dtype=jnp.int32) < lengths[0]).astype(f32)[:, None]
    cotan = cotangent.astype(f32)
    grad_ffn = at.all_narrow(after((valid * cotan).astype(bf16), *tokens_far))
    half = slot // 2
    norm_one, packed, wqkv, wout = qkv_of(where, small, xhats, pieces, width)
    wout_far = at.swap(wout, 2)
    tiles = bias_tiles(n, small, buckets, heads)
    atts, probs = [None] * 4, [None] * 4
    for r in (3, 2, 1, 0):
        length = {2: [grad_ffn[2]], 0: [grad_ffn[1]]}.get(r, [])
        length = after(lengths_all[r], *length) if length else lengths_all[r]
        atts[r], probs[r] = attn_fwd(length, packed, tiles, r)
    wouts = [wout, at.swap(wout, 1), wout_far, at.swap(after(wout_far, atts[1]), 1)]
    attended = [atts[0]] + [at.swap(atts[r], r) for r in (1, 2, 3)]
    whole, norm_two, norm_far = [], [], []
    for i in range(2):
        *whole, norm = out_ln2(n, lengths, tokens, small, attended, wouts, i, whole)
        norm_two.append(norm)
        norm_far.append(at.swap(norm, 2))
    middle, attended = whole

    norm_near = norm_two + [at.swap(x, 1) for x in norm_two]
    o0, o1, gn0, gn1, rows_all = ffn(
        norm_near, grad_ffn[:2], [(0, slot)] * 2, w_ffn, 0, [], 4
    )
    gn_near = [at.swap(x, 1) for x in gn1]

    def chip_sum(p2, p3):
        return add_low(p2, jnp.concatenate([at.swap(x, 1) for x in p3], axis=0))

    cuts = 4
    gn_far, o_far, gn_back = [], [], []
    for i in range(2):
        norms = after(norm_far[i], gn2 if i else gn0)
        cut = half // cuts
        norms = [norms] + [at.swap(norms[j : j + cut], 1) for j in range(0, half, cut)]
        norms[0] = after(norms[0], *gn_far)
        o2, o3, gn2, gn3, rows_all = ffn(
            norms, grad_ffn[2:], [(i * half, half)] * 2, w_ffn, 2 * slot + i * slot, rows_all, cuts
        )
        gn_far.append(chip_sum(gn2, gn3))
        o_far.append((o2, o3))
        gn_back.append(at.swap(gn_far[i], 2))
    norms, grads, hid, gua = rows_all
    gu = dot(norms, after(gua, gn_back[0], *gn_far), TN).astype(bf16)
    gd = dot(hid, after(grads, gn_back[0], *gn_far), TN).astype(bf16)
    shape = (wide, rows, model)
    if at.rings:
        turns = reduce_ring(at, [gu.reshape(shape), gd.reshape(shape)])
        next(turns)

    whole, grad_two = [], []
    for i in range(2):
        near = gn_near[2 * i : 2 * i + 2]
        *whole, vec = ln2_back(
            n, lengths, middle, cotangent, small, gn0, near, gn_back[i], wouts, i, whole
        )
        grad_two.append(vec)
    grad_middle, branch_keep, branch_send, *grad_att = whole
    if at.rings:
        next(turns)
        grad_att[0] = after(grad_att[0], *next(turns))
    grad_att = [grad_att[0]] + [at.swap(grad_att[r], r) for r in (1, 2, 3)]
    grad_packed, dists = None, []

    def backward(r, *deps):
        ga = after(grad_att[r], *deps) if deps else grad_att[r]
        return attn_bwd(packed, ga, atts[r], probs[r], r, grad_packed)

    def turned():
        return list(next(turns)) if at.rings else []

    def turn_after(*deps):
        if at.rings:
            turns.send(list(deps))

    grad_packed, dist = backward(0)
    dists.append(dist)
    attended = after(attended, dist, *grad_att[2:])
    out_send = dot(attended, branch_send, TN).astype(bf16)
    out_keep = dot(attended, branch_keep, TN).astype(bf16)
    o_far = [chip_sum(after(x, dist), [after(y, dist)]) for x, y in o_far]
    out_back = [at.swap(o_far[0], 2)]
    grad_packed, dist = backward(2, out_send, out_keep, *turned())
    turn_after(grad_att[2])
    dists.append(dist)
    out_sum = add_low(out_keep, at.swap(out_send, 1))
    grad_packed, dist = backward(3, out_sum)
    dists.append(dist)
    p2, p3, more_one = ln1_back(after(grad_packed, out_back[0], *turned()), wqkv, xhats[2:], 2)
    turn_after(p3)
    p_far = chip_sum(p2, [p3])
    p_back = [at.swap(p_far[:half], 2)]
    grad_packed, dist = backward(1, p_far)
    dists.append(dist)
    grad_qkv = dot(norm_one, grad_packed, TN).astype(bf16)
    parts = [grad_qkv.reshape(wide, rows, width), out_sum.reshape(wide, rows, model // 2)]
    if at.rings:
        next(turns)
        ffn_own = turns.send([dist])
        turns = reduce_ring(at, parts)
        grad_packed = after(grad_packed, p_back[0], *next(turns))
    else:
        ffn_own = scatter(at, [gu.reshape(shape), gd.reshape(shape)])
        attn_own = scatter(at, parts)
    ffn_all = at.all_narrow(after(ffn_own, p_back[0]))
    p_back.append(at.swap(after(p_far[half:], ffn_all[2]), 2))
    out_back.append(at.swap(after(o_far[1], p_back[1]), 2))

    p0, p1, grad_one = ln1_back(grad_packed, wqkv, xhats[:2], 0)
    grad_one = [grad_one, more_one]
    p_near = at.swap(p1, 1)
    if at.rings:
        keep, send = pack_small(n, at.y.reshape(1), grad_one, grad_two, backwards, dists, heads)
        next(turns)
        sent = turns.send([p1, keep, ffn_all[2]])
        smalls = keep + at.swap_y(after(send, *sent))
        next(turns)
        sent = turns.send([p_back[1], smalls])
        p0 = after(p0, *sent)
    grad_tokens = ln1_last(tokens, xhats[0], grad_middle, small, p0, p_near, *p_back)

    outs = [o0, at.swap(o1, 1), jnp.concatenate(out_back, axis=0)]
    if at.rings:
        next(turns)
        sent = turns.send([grad_tokens])
        smalls, outs[0] = after(smalls, *sent), after(o0, *sent)
        pick = lambda i: lax.dynamic_index_in_dim(smalls, i, 0, keepdims=False)
        z_parts = [pick(at.z)] + [
            at.along_z(pick(lax.rem(at.z + k, far)), k) for k in range(1, far)
        ]
    output = (middle + valid * sum(p.astype(f32) for p in outs)).astype(bf16)
    if at.rings:
        next(turns)
        attn_own = turns.send([output, *z_parts[1:]])
        smalls = after(z_parts[0], attn_own) + sum(z_parts[1:])

    if not at.rings:
        onehot = (backwards[:, None] == jnp.arange(BUCKETS, dtype=jnp.int32)[None, :]).astype(f32)
        table = jnp.dot(sum(dists).reshape(heads, slot), onehot, precision=lax.Precision.HIGHEST)
        table = lax.dynamic_update_slice(
            jnp.zeros((4, heads * BUCKETS), f32), table.reshape(1, -1), (at.n, 0)
        )
        two = grad_two[0] + grad_two[1]
        one = grad_one[0] + grad_one[1]
        smalls = [one[0], one[1], two[0], two[1], table]
        smalls = [g.reshape(wide, 1, -1) for g in smalls]
        smalls = [jnp.pad(g, ((0, 0), (0, 0), (0, TILE - g.shape[2]))) for g in smalls]
        smalls = jnp.concatenate(smalls + [jnp.zeros((wide, 3, TILE), f32)], axis=1)
        smalls = lax.psum_scatter(smalls, "wide", scatter_dimension=0, tiled=True)[0]
    ffn_all[0] = after(ffn_all[0], attn_own)
    up_full, down_full = join_ffn(n, ffn_all, quarter)
    smalls = smalls + after(at.swap(smalls, 2), up_full)
    smalls = smalls + at.swap(smalls, 1)

    qkv_full, out_full = join_attn(n, at.all_narrow(attn_own), model)

    return (
        output,
        grad_tokens,
        smalls[0, :rows],
        smalls[1, :rows],
        qkv_full,
        smalls[4, :rel_rows],
        out_full,
        smalls[2, :rows],
        smalls[3, :rows],
        up_full,
        down_full,
    )


def solution(mesh):
    return jax.shard_map(
        local,
        mesh=mesh,
        in_specs=(
            P(("narrow", "wide"), None),
            P(("narrow", "wide")),
            P(),
            P("wide"),
            P("wide"),
            P("wide", None),
            P("wide"),
            P("wide", None),
            P("wide"),
            P("wide"),
            P("wide", None),
            P("wide", None),
            P(("narrow", "wide"), None),
        ),
        out_specs=(
            P(("narrow", "wide"), None),
            P(("narrow", "wide"), None),
            P("wide"),
            P("wide"),
            P("wide", None),
            P("wide"),
            P("wide", None),
            P("wide"),
            P("wide"),
            P("wide", None),
            P("wide", None),
        ),
        check_vma=False,
    )
```

```python
import functools

import jax
import jax.numpy as jnp
from jax import lax
from jax.experimental import pallas as pl
from jax.experimental.layout import Layout, with_layout_constraint
from jax.experimental.pallas import tpu as pltpu
from jax.sharding import PartitionSpec as P

HEADS = 16
HEAD_DIM = 64
BUCKETS = 32
TILE = 128
PAIR = 2 * HEAD_DIM

norm_eps = 1e-05
neg_large = -1e30
f32 = jnp.float32
bf16 = jnp.bfloat16
VMEM_LIMIT = 56 * 1024 * 1024


PEAK = 1.15e15


def cost(us, share=1.0):
    return pl.CostEstimate(flops=int(us * share * 1e-6 * PEAK), bytes_accessed=0, transcendentals=0)


def dot(a, b, dims=((1,), (0,))):
    return lax.dot_general(a, b, (dims, ((), ())), preferred_element_type=f32)


NT = ((1,), (1,))
TN = ((0,), (0,))


def block_of(x):
    zeros = (0,) * x.ndim
    return pl.BlockSpec(x.shape, lambda i: zeros)


def cut_attn_kernel(n_ref, qkv_ref, out_ref, small_ref, o_ref):
    n = n_ref[0]
    model = out_ref.shape[1]
    mine = model // 4
    at = 0
    for p in range(mine // PAIR):
        for part in range(3):
            start = pl.multiple_of(part * model + n * mine + p * PAIR, PAIR)
            o_ref[:, at : at + PAIR] = qkv_ref[:, pl.ds(start, PAIR)]
            at += PAIR
    o_ref[:, at : at + mine] = out_ref[:, pl.ds(pl.multiple_of(n * mine, mine), mine)]
    at += mine
    o_ref[:, at:] = jnp.zeros((o_ref.shape[0], TILE), bf16)
    o_ref[:16, at:] = small_ref[...]


def cut_attn(n, w_qkv, w_out, small):
    rows, model = w_out.shape
    return pl.pallas_call(
        cut_attn_kernel,
        grid=(1,),
        in_specs=[pl.BlockSpec(memory_space=pltpu.SMEM)]
        + [block_of(x) for x in (w_qkv, w_out, small)],
        out_specs=pl.BlockSpec((rows, model + TILE), lambda i: (0, 0)),
        out_shape=jax.ShapeDtypeStruct((rows, model + TILE), bf16),
        cost_estimate=cost(2),
        name="cut_attn",
    )(n, w_qkv, w_out, small)


def cut_ffn_kernel(n_ref, up_ref, down_ref, o_ref):
    n = n_ref[0]
    size = down_ref.shape[0]
    model = down_ref.shape[1]
    for d in range(model // size):
        start = pl.multiple_of(d * 4 * size + n * size, size)
        o_ref[0, :, d * size : (d + 1) * size] = up_ref[:, pl.ds(start, size)]
    o_ref[1] = down_ref[...]


def cut_ffn(n, w_up, w_down):
    rows = w_up.shape[0]
    quarter, model = w_down.shape[0] // 4, w_down.shape[1]
    return pl.pallas_call(
        cut_ffn_kernel,
        grid_spec=pltpu.PrefetchScalarGridSpec(
            num_scalar_prefetch=1,
            grid=(1,),
            in_specs=[
                pl.BlockSpec(w_up.shape, lambda i, n: (0, 0)),
                pl.BlockSpec((quarter, model), lambda i, n: (n[0], 0)),
            ],
            out_specs=pl.BlockSpec((2, rows, model), lambda i, n: (0, 0, 0)),
        ),
        out_shape=jax.ShapeDtypeStruct((2, rows, model), bf16),
        cost_estimate=cost(2, 0.05),
        name="cut_ffn",
    )(n, w_up, w_down)


def small_kernel(where_ref, *refs):
    out_ref = refs[-1]
    out_ref[...] = jnp.zeros_like(out_ref)
    lane = lax.broadcasted_iota(jnp.int32, (1, TILE), 1)
    for i, ref in enumerate(refs[:-1]):
        d = where_ref[i]
        got = ref[...].astype(f32)
        start = pl.multiple_of(d * TILE, TILE)
        for v in range(4):
            out_ref[v : v + 1, pl.ds(start, TILE)] = got[v : v + 1]
        rel = got[4:5]
        odd = lax.rem(d, 2) == 1
        rel = jnp.where(odd, pltpu.roll(rel, TILE // 2, 1), rel)
        rel = jnp.where((lane >= TILE // 2) == odd, rel, 0.0)
        start = pl.multiple_of((d // 2) * TILE, TILE)
        out_ref[4:5, pl.ds(start, TILE)] += rel


def small_rows(where, pieces, at):
    model = len(pieces) * TILE
    return pl.pallas_call(
        small_kernel,
        grid=(1,),
        in_specs=[pl.BlockSpec(memory_space=pltpu.SMEM)]
        + [pl.BlockSpec((16, TILE), lambda i: (0, at // TILE))] * len(pieces),
        out_specs=pl.BlockSpec((8, model), lambda i: (0, 0)),
        out_shape=jax.ShapeDtypeStruct((8, model), f32),
        cost_estimate=cost(2),
        name="small_rows",
    )(where, *pieces)


def tiles_kernel(n_ref, small_ref, buckets_ref, out_ref):
    heads, count = out_ref.shape[:2]
    lanes = heads * BUCKETS
    slot = buckets_ref.shape[1]
    rel = small_ref[4:5, pl.ds(pl.multiple_of(n_ref[0] * lanes, lanes), lanes)]
    head = lax.broadcasted_iota(jnp.int32, (8, lanes), 0)
    lane = lax.broadcasted_iota(jnp.int32, (8, lanes), 1)
    table = jnp.where(lane // BUCKETS == head, rel, 0.0).astype(bf16)
    bucket = lax.broadcasted_iota(jnp.int32, (lanes, slot), 0) % BUCKETS
    onehot = (buckets_ref[...] == bucket).astype(f32).astype(bf16)
    by_distance = dot(table, onehot)
    row = lax.broadcasted_iota(jnp.int32, (TILE, TILE), 0)
    col = lax.broadcasted_iota(jnp.int32, (TILE, TILE), 1)
    for h in range(heads):
        for delta in range(count):
            here = by_distance[h : h + 1, delta * TILE : (delta + 1) * TILE]
            below = by_distance[h : h + 1, max(delta - 1, 0) * TILE : max(delta, 1) * TILE]
            wide = jnp.broadcast_to(jnp.concatenate([here, below], axis=1), (TILE, 2 * TILE))
            tile = pltpu.roll(wide, 0, 1, stride=1, stride_axis=0)[:, :TILE].T
            if delta == 0:
                tile = jnp.where(col <= row, tile, neg_large)
            out_ref[h, delta] = tile


def bias_tiles(n, small, buckets, heads):
    slot = buckets.shape[0]
    buckets = buckets.reshape(1, slot)
    shape = (heads, slot // TILE, TILE, TILE)
    return pl.pallas_call(
        tiles_kernel,
        grid=(1,),
        in_specs=[pl.BlockSpec(memory_space=pltpu.SMEM), block_of(small), block_of(buckets)],
        out_specs=pl.BlockSpec(shape, lambda i: (0, 0, 0, 0)),
        out_shape=jax.ShapeDtypeStruct(shape, f32),
        cost_estimate=cost(4),
        name="bias_tiles",
    )(n, small, buckets)


def normalized(v):
    center = v - jnp.mean(v, axis=-1, keepdims=True)
    factor = lax.rsqrt(jnp.mean(center * center, axis=-1, keepdims=True) + norm_eps)
    return center * factor, factor


def xhat_kernel(*refs):
    out_ref = refs[-1]
    at = 0
    for ref in refs[:-1]:
        rows = ref.shape[0]
        out_ref[at : at + rows] = normalized(ref[...].astype(f32))[0]
        at += rows


def xhat_of(pieces):
    slot, model = sum(p.shape[0] for p in pieces), pieces[0].shape[1]
    return pl.pallas_call(
        xhat_kernel,
        grid=(1,),
        in_specs=[block_of(p) for p in pieces],
        out_specs=pl.BlockSpec((slot, model), lambda i: (0, 0)),
        out_shape=jax.ShapeDtypeStruct((slot, model), f32),
        compiler_params=pltpu.CompilerParams(vmem_limit_bytes=VMEM_LIMIT),
        cost_estimate=cost(2.5, 0.05),
        name="xhat",
    )(*pieces)


def qkv_kernel(count, where_ref, small_ref, *refs):
    xhats, pieces = refs[:4], refs[4 : 4 + count]
    norm_ref, packed_ref, wq_ref, wo_ref, w_ref, x_ref, sems, x_sems = refs[4 + count :]
    step = pl.program_id(0)
    width = wq_ref.shape[1]

    def fetch(r):
        return pltpu.make_async_copy(xhats[r], x_ref.at[r % 2], x_sems.at[r % 2])

    @pl.when(step == 0)
    def _():
        fetch(0).start()
        copies = []
        for i, piece in enumerate(pieces):
            size = piece.shape[0]
            start = pl.multiple_of(where_ref[i] * size, size)
            copies.append(pltpu.make_async_copy(piece, w_ref.at[pl.ds(start, size)], sems.at[i]))
            copies[-1].start()
        for copy in copies:
            copy.wait()
        wq_ref[...] = w_ref[:, :width]
        wo_ref[...] = w_ref[:, width : width + wo_ref.shape[1]]

    for r in range(4):

        @pl.when(step == r)
        def _(r=r):
            if r < 3:
                fetch(r + 1).start()
            fetch(r).wait()

    norm = (x_ref[lax.rem(step, 2)] * small_ref[0:1] + small_ref[1:2]).astype(bf16)
    norm_ref[...] = norm
    packed_ref[...] = dot(norm, wq_ref[...]).astype(bf16)


def qkv_of(where, small, xhats, pieces, width):
    slot, model = xhats[0].shape
    total = pieces[0].shape[1]
    out = model // 4
    whole = lambda shape: pl.BlockSpec(shape, lambda i: (0, 0))
    rows = lambda cols: pl.BlockSpec((slot, cols), lambda i: (i, 0))
    return pl.pallas_call(
        functools.partial(qkv_kernel, len(pieces)),
        grid=(4,),
        in_specs=[pl.BlockSpec(memory_space=pltpu.SMEM), whole(small.shape)]
        + [pl.BlockSpec(memory_space=pl.ANY)] * (4 + len(pieces)),
        out_specs=[rows(model), rows(width), whole((model, width)), whole((model, out))],
        out_shape=[
            jax.ShapeDtypeStruct((4 * slot, model), bf16),
            jax.ShapeDtypeStruct((4 * slot, width), bf16),
            jax.ShapeDtypeStruct((model, width), bf16),
            jax.ShapeDtypeStruct((model, out), bf16),
        ],
        scratch_shapes=[
            pltpu.VMEM((model, total), bf16),
            pltpu.VMEM((2, slot, model), f32),
            pltpu.SemaphoreType.DMA((len(pieces),)),
            pltpu.SemaphoreType.DMA((2,)),
        ],
        compiler_params=pltpu.CompilerParams(vmem_limit_bytes=VMEM_LIMIT),
        cost_estimate=cost(7, 0.05),
        name="qkv",
    )(where, small, *xhats, *pieces)


def ln1_back_kernel(gp_ref, wq_ref, x0_ref, x1_ref, p0_ref, p1_ref, vec_ref):
    step = pl.program_id(0)
    grad = dot(gp_ref[...], wq_ref[...], NT)

    @pl.when(step == 0)
    def _():
        vec_ref[0:1] = jnp.sum(grad * x0_ref[...], axis=0, keepdims=True)
        vec_ref[1:2] = jnp.sum(grad, axis=0, keepdims=True)
        p0_ref[...] = grad.astype(p0_ref.dtype)

    @pl.when(step == 1)
    def _():
        vec_ref[0:1] += jnp.sum(grad * x1_ref[...], axis=0, keepdims=True)
        vec_ref[1:2] += jnp.sum(grad, axis=0, keepdims=True)
        p1_ref[...] = grad.astype(p1_ref.dtype)


def ln1_back(grad_packed, wqkv, xhats, first):
    slot, model = xhats[0].shape
    width = wqkv.shape[1]
    whole = lambda shape: pl.BlockSpec(shape, lambda i: (0, 0))
    return pl.pallas_call(
        ln1_back_kernel,
        grid=(2,),
        in_specs=[
            pl.BlockSpec((slot, width), lambda i: (first + i, 0)),
            whole((model, width)),
            whole((slot, model)),
            whole((slot, model)),
        ],
        out_specs=[whole((slot, model)), whole((slot, model)), whole((2, model))],
        out_shape=[
            jax.ShapeDtypeStruct((slot, model), bf16 if first else f32),
            jax.ShapeDtypeStruct((slot, model), bf16),
            jax.ShapeDtypeStruct((2, model), f32),
        ],
        compiler_params=pltpu.CompilerParams(vmem_limit_bytes=VMEM_LIMIT),
        cost_estimate=cost(5, 0.1 if first else 1.0),
        name="ln1_back",
    )(grad_packed, wqkv, *xhats)


def attn_fwd_kernel(len_ref, qkv_ref, tiles_ref, att_ref, p_ref):
    slot = qkv_ref.shape[0]
    blocks = range(slot // TILE)
    heads = range(2)
    length = len_ref[0]
    lane = lax.broadcasted_iota(jnp.int32, (1, PAIR), 1)
    col = lax.broadcasted_iota(jnp.int32, (1, slot), 1)
    hidden = jnp.where(col < length, 0.0, neg_large)
    q = qkv_ref[:, :PAIR] * HEAD_DIM ** (-0.5)
    k = qkv_ref[:, PAIR : 2 * PAIR]
    v = qkv_ref[:, 2 * PAIR :]
    own = [(lane // HEAD_DIM) == hh for hh in heads]
    qm = [jnp.where(own[hh], q, jnp.zeros_like(q)) for hh in heads]
    span = [(i + 1) * TILE for i in blocks]
    items = [(hh, i) for hh in heads for i in blocks]
    s = [dot(qm[hh][i * TILE : span[i]], k[: span[i]], NT) for hh, i in items]
    s = [
        x + jnp.concatenate([tiles_ref[hh, i - j] for j in range(i + 1)], axis=1) + hidden[:, : span[i]]
        for x, (hh, i) in zip(s, items)
    ]
    top = [jnp.max(x, axis=1, keepdims=True) for x in s]
    e = [jnp.exp(x - m) for x, m in zip(s, top)]
    scale = [1.0 / jnp.sum(x, axis=1, keepdims=True) for x in e]
    probs = [(x * r).astype(bf16) for x, r in zip(e, scale)]
    for x, (hh, i) in zip(probs, items):
        p_ref[hh, i * TILE : span[i], : span[i]] = x
    o = {item: dot(x, v[: span[item[1]]]) for x, item in zip(probs, items)}
    for i in blocks:
        att_ref[i * TILE : span[i], :] = jnp.where(own[0], o[0, i], o[1, i]).astype(bf16)


def attn_fwd(lengths, packed, tiles, seq):
    heads, count = tiles.shape[:2]
    slot = count * TILE
    return pl.pallas_call(
        attn_fwd_kernel,
        grid=(heads // 2,),
        in_specs=[
            pl.BlockSpec(memory_space=pltpu.SMEM),
            pl.BlockSpec((slot, 3 * PAIR), lambda p: (seq, p)),
            pl.BlockSpec((2, count, TILE, TILE), lambda p: (p, 0, 0, 0)),
        ],
        out_specs=[
            pl.BlockSpec((slot, PAIR), lambda p: (0, p)),
            pl.BlockSpec((2, slot, slot), lambda p: (p, 0, 0)),
        ],
        out_shape=[
            jax.ShapeDtypeStruct((slot, heads * HEAD_DIM), bf16),
            jax.ShapeDtypeStruct((heads, slot, slot), bf16),
        ],
        compiler_params=pltpu.CompilerParams(vmem_limit_bytes=VMEM_LIMIT),
        cost_estimate=cost(4.5, 0.1),
        name="attn_fwd",
    )(lengths, packed, tiles)


def attn_bwd_kernel(qkv_ref, ga_ref, att_ref, p_ref, *refs):
    g_ref, sum_ref, ds_ref = refs[-3:]
    slot = qkv_ref.shape[0]
    blocks = range(slot // TILE)
    heads = range(2)
    lane = lax.broadcasted_iota(jnp.int32, (1, PAIR), 1)
    scale = HEAD_DIM ** (-0.5)
    q = qkv_ref[:, :PAIR] * scale
    k = qkv_ref[:, PAIR : 2 * PAIR]
    v = qkv_ref[:, 2 * PAIR :]
    ga = ga_ref[...]
    prod = ga.astype(f32) * att_ref[...].astype(f32)
    own = [(lane // HEAD_DIM) == hh for hh in heads]
    gam = [jnp.where(own[hh], ga, jnp.zeros_like(ga)) for hh in heads]
    inner = [jnp.sum(jnp.where(own[hh], prod, 0.0), axis=1, keepdims=True) for hh in heads]
    span = [(i + 1) * TILE for i in blocks]
    rows = [slice(i * TILE, span[i]) for i in blocks]
    items = [(hh, i) for hh in heads for i in blocks]
    dp = [dot(gam[hh][rows[i]], v[: span[i]], NT) for hh, i in items]
    ds = {
        (hh, i): (p_ref[hh, rows[i], : span[i]].astype(f32) * (x - inner[hh][rows[i]])).astype(bf16)
        for x, (hh, i) in zip(dp, items)
    }
    for hh, i in items:
        ds_ref[hh, rows[i], : span[i]] = ds[hh, i]
    dq = {(hh, i): dot(ds[hh, i], k[: span[i]]) for hh, i in items}
    dv = {(hh, j): dot(p_ref[hh, j * TILE :, rows[j]], ga[j * TILE :], TN) for hh, j in items}
    dk = {(hh, j): dot(ds_ref[hh, j * TILE :, rows[j]], q[j * TILE :], TN) for hh, j in items}
    for i in blocks:
        for at, got, factor in ((0, dq, scale), (PAIR, dk, 1.0), (2 * PAIR, dv, 1.0)):
            both = jnp.where(own[0], got[0, i], got[1, i]) * factor
            g_ref[rows[i], at : at + PAIR] = both.astype(bf16)
    row = lax.broadcasted_iota(jnp.int32, (TILE, TILE), 0)
    col = lax.broadcasted_iota(jnp.int32, (TILE, TILE), 1)
    flip = jnp.where(row + col == TILE - 1, 1.0, 0.0).astype(bf16)
    diag = {}
    for hh in heads:
        for delta in blocks:
            parts = [
                ds[hh, i][:, (i - delta) * TILE : (i - delta + 1) * TILE].astype(f32)
                for i in blocks
                if i >= delta
            ]
            diag[hh, delta] = functools.reduce(jnp.add, parts)
    high = {key: x.astype(bf16) for key, x in diag.items()}
    low = {key: (x - high[key].astype(f32)).astype(bf16) for key, x in diag.items()}
    turned = {key: dot(flip, high[key]) + dot(flip, low[key]) for key in diag}
    sums = {}
    for key, x in turned.items():
        wide = jnp.concatenate([x, jnp.zeros_like(x)], axis=1)
        wide = pltpu.roll(wide, 0, 1, stride=1, stride_axis=0)
        sums[key] = jnp.sum(wide, axis=0, keepdims=True)
    for hh in heads:
        for delta in blocks:
            here = sums[hh, delta][:, :TILE]
            if delta + 1 in blocks:
                here = here + sums[hh, delta + 1][:, TILE:]
            sum_ref[0, hh : hh + 1, rows[delta]] = here


def attn_bwd(packed, ga, att, probs, seq, into):
    heads, slot = probs.shape[:2]
    steps = heads // 2
    return pl.pallas_call(
        attn_bwd_kernel,
        grid=(steps,),
        in_specs=[
            pl.BlockSpec((slot, 3 * PAIR), lambda p: (seq, p)),
            pl.BlockSpec((slot, PAIR), lambda p: (0, p)),
            pl.BlockSpec((slot, PAIR), lambda p: (0, p)),
            pl.BlockSpec((2, slot, slot), lambda p: (p, 0, 0)),
        ]
        + ([] if into is None else [pl.BlockSpec(memory_space=pl.ANY)]),
        out_specs=[
            pl.BlockSpec((slot, 3 * PAIR), lambda p: (seq, p)),
            pl.BlockSpec((1, 2, slot), lambda p: (p, 0, 0)),
        ],
        out_shape=[
            jax.ShapeDtypeStruct(packed.shape, bf16),
            jax.ShapeDtypeStruct((steps, 2, slot), f32),
        ],
        scratch_shapes=[pltpu.VMEM((2, slot, slot), bf16)],
        input_output_aliases={} if into is None else {4: 0},
        compiler_params=pltpu.CompilerParams(vmem_limit_bytes=VMEM_LIMIT),
        cost_estimate=cost(5, 0.2),
        name="attn_bwd",
    )(packed, ga, att, probs, *(() if into is None else (into,)))


def ln1_last_kernel(tok_ref, xhat_ref, gmid_ref, small_ref, p0_ref, p1_ref, p2_ref, p3_ref, out_ref):
    _, factor = normalized(tok_ref[...].astype(f32))
    xhat = xhat_ref[...]
    low = pl.program_id(0) == 0
    e = p0_ref[...] + p1_ref[...].astype(f32) + jnp.where(low, p2_ref[...], p3_ref[...]).astype(f32)
    e = e * small_ref[0:1]
    out_ref[...] = gmid_ref[...] + factor * (
        e - jnp.mean(e, axis=-1, keepdims=True) - xhat * jnp.mean(e * xhat, axis=-1, keepdims=True)
    )


def ln1_last(tokens, xhat, grad_middle, small, p0, p1, p2, p3):
    slot, model = tokens.shape
    row = pl.BlockSpec((slot // 2, model), lambda i: (i, 0))
    part = pl.BlockSpec((slot // 2, model), lambda i: (0, 0))
    return pl.pallas_call(
        ln1_last_kernel,
        grid=(2,),
        in_specs=[row] * 3 + [block_of(small), row, row, part, part],
        out_specs=row,
        out_shape=jax.ShapeDtypeStruct((slot, model), f32),
        compiler_params=pltpu.CompilerParams(vmem_limit_bytes=VMEM_LIMIT),
        cost_estimate=cost(5, 0.05),
        name="ln1_last",
    )(tokens, xhat, grad_middle, small, p0, p1, p2, p3)


def quarters(n, r, size):
    return pl.ds(pl.multiple_of(lax.bitwise_xor(n, r) * size, size), size)


def out_ln2_kernel(part, n_ref, len_ref, tok_ref, small_ref, *refs):
    atts, wouts = refs[:4], refs[4:8]
    mid_ref, all_ref, norm_ref = refs[-3:]
    n = n_ref[0]
    rows, model = tok_ref.shape
    size = model // 4
    for r in range(4):
        all_ref[:, quarters(n, r, size)] = atts[r][...]
    valid = part * rows + lax.broadcasted_iota(jnp.int32, (rows, 1), 0) < len_ref[0]
    for r in range(4):
        cols = quarters(n, r, size)
        out = dot(all_ref[...], wouts[r][...])
        mid_ref[:, cols] = tok_ref[:, cols].astype(f32) + jnp.where(valid, out, 0.0)
    xhat, _ = normalized(mid_ref[...])
    norm_ref[...] = (xhat * small_ref[2:3] + small_ref[3:4]).astype(bf16)


def out_ln2(n, length, tokens, small, atts, wouts, part, into):
    slot, model = tokens.shape
    smem = pl.BlockSpec(memory_space=pltpu.SMEM)
    whole = lambda x: pl.BlockSpec(x.shape, lambda i: (0, 0))
    rows = lambda cols: pl.BlockSpec((slot // 2, cols), lambda i: (part, 0))
    return pl.pallas_call(
        functools.partial(out_ln2_kernel, part),
        grid=(1,),
        in_specs=[smem, smem, rows(model), whole(small)]
        + [rows(model // 4)] * 4
        + [whole(w) for w in wouts]
        + [pl.BlockSpec(memory_space=pl.ANY)] * len(into),
        out_specs=[rows(model), rows(model), pl.BlockSpec((slot // 2, model), lambda i: (0, 0))],
        out_shape=[
            jax.ShapeDtypeStruct((slot, model), f32),
            jax.ShapeDtypeStruct((slot, model), bf16),
            jax.ShapeDtypeStruct((slot // 2, model), bf16),
        ],
        input_output_aliases={12 + i: i for i in range(len(into))},
        compiler_params=pltpu.CompilerParams(vmem_limit_bytes=VMEM_LIMIT),
        cost_estimate=cost(4, 1 / 64),
        name="out_ln2",
    )(n, length, tokens, small, *atts, *wouts, *into)


def ln2_back_kernel(part, n_ref, len_ref, mid_ref, cot_ref, small_ref, p0_ref, p2_ref, *refs):
    near, wouts = refs[:2], refs[2:6]
    gmid_ref, keep_ref, send_ref = refs[-9:-6]
    gatts = refs[-6:-2]
    vec_ref, branch_ref = refs[-2:]
    n = n_ref[0]
    rows, model = mid_ref.shape
    size = model // 4
    xhat, factor = normalized(mid_ref[...])
    grad = p0_ref[...] + p2_ref[...].astype(f32)
    grad = grad + jnp.concatenate([x[...] for x in near], axis=0).astype(f32)
    vec_ref[0:1] = jnp.sum(grad * xhat, axis=0, keepdims=True)
    vec_ref[1:2] = jnp.sum(grad, axis=0, keepdims=True)
    e = grad * small_ref[2:3]
    back = factor * (
        e - jnp.mean(e, axis=-1, keepdims=True) - xhat * jnp.mean(e * xhat, axis=-1, keepdims=True)
    )
    gmid = cot_ref[...].astype(f32) + back
    gmid_ref[...] = gmid
    valid = part * rows + lax.broadcasted_iota(jnp.int32, (rows, 1), 0) < len_ref[0]
    branch_ref[...] = jnp.where(valid, gmid, 0.0).astype(bf16)
    cuts = [branch_ref[:, quarters(n, r, size)] for r in range(4)]
    keep_ref[:, :size] = cuts[0]
    keep_ref[:, size:] = cuts[2]
    send_ref[:, :size] = cuts[1]
    send_ref[:, size:] = cuts[3]
    for r in range(4):
        feats = quarters(n, r, size)
        total = dot(cuts[0], wouts[0][feats, :], NT)
        for k in range(1, 4):
            total = total + dot(cuts[k], wouts[k][feats, :], NT)
        gatts[r][...] = total.astype(bf16)


def ln2_back(n, length, middle, cot, small, p0, near, p2, wouts, part, into):
    slot, model = middle.shape
    smem = pl.BlockSpec(memory_space=pltpu.SMEM)
    whole = lambda x: pl.BlockSpec(x.shape, lambda i: (0, 0))
    rows = lambda cols: pl.BlockSpec((slot // 2, cols), lambda i: (part, 0))
    return pl.pallas_call(
        functools.partial(ln2_back_kernel, part),
        grid=(1,),
        in_specs=[smem, smem, rows(model), rows(model), whole(small), rows(model), whole(p2)]
        + [whole(w) for w in (*near, *wouts)]
        + [pl.BlockSpec(memory_space=pl.ANY)] * len(into),
        out_specs=[rows(model), rows(model // 2), rows(model // 2)]
        + [rows(model // 4)] * 4
        + [pl.BlockSpec((2, model), lambda i: (0, 0))],
        out_shape=[
            jax.ShapeDtypeStruct((slot, model), f32),
            jax.ShapeDtypeStruct((slot, model // 2), bf16),
            jax.ShapeDtypeStruct((slot, model // 2), bf16),
        ]
        + [jax.ShapeDtypeStruct((slot, model // 4), bf16)] * 4
        + [jax.ShapeDtypeStruct((2, model), f32)],
        scratch_shapes=[pltpu.VMEM((slot // 2, model), bf16)],
        input_output_aliases={13 + i: i for i in range(len(into))},
        compiler_params=pltpu.CompilerParams(vmem_limit_bytes=VMEM_LIMIT),
        cost_estimate=cost(5),
        name="ln2_back",
    )(n, length, middle, cot, small, p0, p2, *near, *wouts, *into)


def gelu_both(u):
    c0 = 0.7978845608028654
    c1 = 0.044715
    sq = u * u
    t = jnp.tanh(u * (c0 + (c0 * c1) * sq))
    half = 0.5 + 0.5 * t
    slope = half + (1.0 - t * t) * (u * (0.5 * c0 + (1.5 * c0 * c1) * sq))
    return u * half, slope


def ffn_kernel(count, places, start, cuts, w_any, *refs):
    norms, grads = refs[:count], refs[count : count + len(places)]
    n4_any, g4_any, hid4_any, gua4_any = refs[-13:-9]
    sums = refs[-16 - cuts : -13]
    o0_ref, gn0_ref = sums[:2]
    n_ref, g_ref, wu_ref, wd_ref, hid_ref, gua_ref, sems, w_sems, out_sems = refs[-9:]
    step = pl.program_id(0)
    steps = pl.num_programs(0) // 2
    rows = n_ref.shape[0]
    block = o0_ref.shape[1]
    mine = pl.ds(start, rows)
    outs = [
        pltpu.make_async_copy(src, dst.at[mine], out_sems.at[i])
        for i, (src, dst) in enumerate(
            ((n_ref, n4_any), (g_ref, g4_any), (hid_ref, hid4_any), (gua_ref, gua4_any))
        )
    ]
    shards, _, size, _ = w_any.shape
    weights = [
        [
            pltpu.make_async_copy(
                w_any.at[d, i], whole.at[pl.ds(d * size, size)], w_sems.at[d, i]
            )
            for d in range(shards)
        ]
        for i, whole in enumerate((wu_ref, wd_ref))
    ]
    acts = []
    grads = [g.at[pl.ds(first, size)] for g, (first, size) in zip(grads, places)]
    for j, (pieces, whole) in enumerate(((norms, n_ref), (grads, g_ref))):
        acts.append([])
        at = 0
        for i, piece in enumerate(pieces):
            here = piece.shape[0]
            acts[j].append(
                pltpu.make_async_copy(piece, whole.at[pl.ds(at, here)], sems.at[j, i])
            )
            at += here

    @pl.when(step == 0)
    def _():
        for copy in acts[0] + weights[0] + acts[1] + weights[1]:
            copy.start()
        for copy in acts[0] + weights[0]:
            copy.wait()

    @pl.when(step < steps)
    def _():
        cols = pl.ds(pl.multiple_of(step * block, block), block)
        u = dot(n_ref[...], wu_ref[:, cols])
        hid, slope = gelu_both(u)

        @pl.when(step == 0)
        def _():
            for copy in acts[1] + weights[1]:
                copy.wait()

        gh = dot(g_ref[...], wd_ref[cols, :], NT)
        hid_ref[:, cols] = hid.astype(bf16)
        gua_ref[:, cols] = (slope * gh).astype(bf16)

    @pl.when(step == steps)
    def _():
        for copy in outs:
            copy.start()

    @pl.when(step >= steps)
    def _():
        cols = pl.ds(pl.multiple_of((step - steps) * block, block), block)
        half = rows // 2
        gn = dot(gua_ref[...], wu_ref[cols, :], NT)
        o = dot(hid_ref[...], wd_ref[:, cols])
        for first, pieces, total in ((o0_ref, sums[2:3], o), (gn0_ref, sums[3:], gn)):
            first[...] = total[:half]
            size = half // len(pieces)
            for i, piece in enumerate(pieces):
                piece[...] = total[half + i * size : half + (i + 1) * size].astype(bf16)

    @pl.when(step == 2 * steps - 1)
    def _():
        for copy in outs:
            copy.wait()


def ffn(norms, grads, places, weights, start, into, cuts):
    width = norms[0].shape[1]
    rows = sum(x.shape[0] for x in norms)
    total = into[0].shape[0] if into else 2 * rows
    units = weights.shape[0] * weights.shape[2]
    block = min(512, units)
    steps = units // block
    half = rows // 2
    anywhere = pl.BlockSpec(memory_space=pl.ANY)
    late = lambda size: pl.BlockSpec((size, block), lambda i: (0, jnp.maximum(i - steps, 0)))
    acts = pltpu.VMEM((rows, width), bf16)
    hidden = pltpu.VMEM((rows, units), bf16)
    ins = 1 + len(norms) + len(grads)
    outs = 3 + cuts
    got = pl.pallas_call(
        functools.partial(ffn_kernel, len(norms), places, start, cuts),
        grid=(2 * steps,),
        in_specs=[anywhere] * (ins + len(into)),
        out_specs=[late(half)] * 2 + [late(half)] + [late(half // cuts)] * cuts + [anywhere] * 4,
        out_shape=[jax.ShapeDtypeStruct((half, width), f32)] * 2
        + [jax.ShapeDtypeStruct((half, width), bf16)]
        + [jax.ShapeDtypeStruct((half // cuts, width), bf16)] * cuts
        + [jax.ShapeDtypeStruct((total, width), bf16)] * 2
        + [jax.ShapeDtypeStruct((total, units), bf16)] * 2,
        scratch_shapes=[
            acts,
            acts,
            pltpu.VMEM((width, units), bf16),
            pltpu.VMEM((units, width), bf16),
            hidden,
            hidden,
            pltpu.SemaphoreType.DMA((2, max(len(norms), len(grads)))),
            pltpu.SemaphoreType.DMA((weights.shape[0], 2)),
            pltpu.SemaphoreType.DMA((4,)),
        ],
        input_output_aliases={ins + i: outs + i for i in range(len(into))},
        compiler_params=pltpu.CompilerParams(vmem_limit_bytes=VMEM_LIMIT),
        cost_estimate=cost(8 if into else 12, 1 / 64),
        name="ffn",
    )(weights, *norms, *grads, *into)
    return got[0], got[2], got[1], got[3:outs], got[outs:]


def pack_small_kernel(heads, n_ref, y_ref, one_ref, also_ref, two_ref, more_ref, buckets_ref, *refs):
    dists, (keep_ref, send_ref) = refs[:-2], refs[-2:]
    n = n_ref[0]
    odd = y_ref[0] == 1
    slot = buckets_ref.shape[1]
    total = dists[0][...]
    for ref in dists[1:]:
        total = total + ref[...]
    lanes = heads * BUCKETS
    bucket = lax.broadcasted_iota(jnp.int32, (lanes, slot), 0) % BUCKETS
    onehot = (buckets_ref[...] == bucket).astype(f32).astype(bf16)
    lane = lax.broadcasted_iota(jnp.int32, (1, lanes), 1)
    table = jnp.zeros((1, lanes), f32)
    for h in range(heads):
        row = jnp.broadcast_to(total[h // 2, h % 2 : h % 2 + 1], (8, slot))
        parts = []
        for _ in range(3):
            low = row.astype(bf16)
            parts.append(dot(low, onehot, NT))
            row = row - low.astype(f32)
        got = (parts[0] + parts[1] + parts[2])[0:1]
        table = jnp.where(lane // BUCKETS == h, got, table)
    zeros = jnp.zeros((1, TILE), f32)
    half = lanes // 2
    low = jnp.where(lane < half, table, 0.0)
    high = jnp.where(lane < half, pltpu.roll(table, half, 1), 0.0)
    for z in range(keep_ref.shape[0]):
        both = []
        for b, share in ((0, low), (1, high)):
            d = 2 * z + b
            cols = slice(d * TILE, (d + 1) * TILE)
            rel = jnp.where(d == 2 * n + b, share, zeros)
            both.append(
                jnp.concatenate(
                    [
                        one_ref[:, cols] + also_ref[:, cols],
                        two_ref[:, cols] + more_ref[:, cols],
                        rel,
                        zeros,
                        zeros,
                        zeros,
                    ],
                    axis=0,
                )
            )
        keep_ref[z] = jnp.where(odd, both[1], both[0])
        send_ref[z] = jnp.where(odd, both[0], both[1])


def pack_small(n, y, grad_one, grad_two, buckets, dists, heads):
    slot = buckets.shape[0]
    model = grad_one[0].shape[1]
    smem = pl.BlockSpec(memory_space=pltpu.SMEM)
    operands = [*grad_one, *grad_two, buckets.reshape(1, slot), *dists]
    shape = jax.ShapeDtypeStruct((model // TILE // 2, 8, TILE), f32)
    return pl.pallas_call(
        functools.partial(pack_small_kernel, heads),
        grid=(1,),
        in_specs=[smem, smem] + [block_of(x) for x in operands],
        out_specs=[pl.BlockSpec(shape.shape, lambda i: (0, 0, 0))] * 2,
        out_shape=[shape, shape],
        cost_estimate=cost(3),
        name="pack_small",
    )(n, y, *operands)


def join_ffn_kernel(quarter, n_ref, *refs):
    ins, (up_ref, down_ref) = refs[:4], refs[4:]
    model = down_ref.shape[1]
    rows = up_ref.shape[0]
    for r in range(4):
        j = lax.bitwise_xor(n_ref[0], r)
        for d in range(model // quarter):
            start = pl.multiple_of((d * 4 + j) * quarter, quarter)
            up_ref[:, pl.ds(start, quarter)] = ins[r][:, d * quarter : (d + 1) * quarter].astype(f32)
        down_ref[pl.ds(pl.multiple_of(j * quarter, quarter), quarter), :] = ins[r][:, model:].astype(f32)


def join_ffn(n, parts, quarter):
    rows, both = parts[0].shape
    model = both // 2
    shapes = [(rows, 4 * model), (4 * quarter, model)]
    if quarter % TILE:
        wide = model // quarter
        rel = jnp.stack(parts)
        rel = jnp.stack(
            [lax.dynamic_index_in_dim(rel, n[0] ^ j, 0, keepdims=False) for j in range(4)]
        ).astype(f32)
        up = rel[:, :, :model].reshape(4, rows, wide, quarter).transpose(1, 2, 0, 3)
        return up.reshape(shapes[0]), rel[:, :, model:].reshape(shapes[1])
    return pl.pallas_call(
        functools.partial(join_ffn_kernel, quarter),
        grid=(1,),
        in_specs=[pl.BlockSpec(memory_space=pltpu.SMEM)] + [block_of(x) for x in parts],
        out_specs=[pl.BlockSpec(x, lambda i: (0, 0)) for x in shapes],
        out_shape=[jax.ShapeDtypeStruct(x, f32) for x in shapes],
        compiler_params=pltpu.CompilerParams(vmem_limit_bytes=VMEM_LIMIT),
        cost_estimate=cost(4, 0.05),
        name="join_ffn",
    )(n, *parts)


def join_attn_kernel(n_ref, *refs):
    ins, (qkv_ref, out_ref) = refs[:4], refs[4:]
    model = out_ref.shape[1]
    mine = model // 4
    for r in range(4):
        j = lax.bitwise_xor(n_ref[0], r)
        at = 0
        for p in range(mine // PAIR):
            for part in range(3):
                start = pl.multiple_of(part * model + j * mine + p * PAIR, PAIR)
                qkv_ref[:, pl.ds(start, PAIR)] = ins[r][:, at : at + PAIR].astype(f32)
                at += PAIR
        out_ref[:, pl.ds(pl.multiple_of(j * mine, mine), mine)] = ins[r][
            :, at : at + mine
        ].astype(f32) + ins[r ^ 2][:, at + mine :].astype(f32)


def join_attn(n, parts, model):
    rows = parts[0].shape[0]
    shapes = [(rows, 3 * model), (rows, model)]
    return pl.pallas_call(
        join_attn_kernel,
        grid=(1,),
        in_specs=[pl.BlockSpec(memory_space=pltpu.SMEM)] + [block_of(x) for x in parts],
        out_specs=[pl.BlockSpec(x, lambda i: (0, 0)) for x in shapes],
        out_shape=[jax.ShapeDtypeStruct(x, f32) for x in shapes],
        cost_estimate=cost(3),
        name="join_attn",
    )(n, *parts)


def ring_order(size):
    return list(range(0, size, 2)) + list(range(size - 1, 0, -2))


def ring_member(pos, size):
    pos = lax.rem(pos + 2 * size, size)
    return jnp.where(pos < size // 2, 2 * pos, 2 * (size - 1 - pos) + 1)


def ring_pairs(narrow, size):
    order = ring_order(size)
    pairs = []
    for n in range(narrow):
        turn = 1 if n % 2 == 0 else -1
        for p in range(size):
            pairs.append((n * size + order[p], n * size + order[(p + turn) % size]))
    return pairs


class Places:
    def __init__(self):
        self.narrow = lax.axis_size("narrow")
        self.wide = lax.axis_size("wide")
        self.n = lax.axis_index("narrow")
        self.w = lax.axis_index("wide")
        self.core = lax.rem(self.n, 2)
        self.turn = 1 - 2 * self.core
        self.y = lax.rem(self.w, 2)
        self.z = self.w // 2
        self.pos = jnp.where(self.y == 0, self.z, self.wide - 1 - self.z)
        self.pairs = ring_pairs(self.narrow, self.wide)
        self.rings = self.wide <= 16

    def ring(self, x, way):
        pairs = self.pairs if way == 0 else [(b, a) for a, b in self.pairs]
        return lax.ppermute(x, ("narrow", "wide"), pairs)

    def member(self, steps):
        return ring_member(self.pos + self.turn * steps, self.wide)

    def swap(self, x, bit):
        return lax.ppermute(x, "narrow", [(i, i ^ bit) for i in range(self.narrow)])

    def all_narrow(self, x):
        far = self.swap(x, 2)
        return [x, self.swap(x, 1), far, self.swap(far, 1)]

    def swap_y(self, x):
        return lax.ppermute(x, "wide", [(i, i ^ 1) for i in range(self.wide)])

    def along_z(self, x, steps):
        return lax.ppermute(
            x, "wide", [(i, (i + 2 * steps) % self.wide) for i in range(self.wide)]
        )


def row_major(x):
    return with_layout_constraint(x, Layout(major_to_minor=tuple(range(x.ndim))))


def after(x, *deps):
    return lax.optimization_barrier((x, *deps))[0]


def add_low(*terms):
    return sum(t.astype(f32) for t in terms).astype(bf16)


def gather_ring(at, piece, holds):
    pieces, steps = [piece], [0]
    ahead = behind = piece
    far = at.wide // 2
    for k in range(1, far + 1):
        ahead = at.ring(ahead, 0)
        came = [ahead]
        if k < far:
            behind = at.ring(behind, 1)
            came.append(behind)
        held = holds[k](*came) if k in holds else ()
        came = lax.optimization_barrier((*came, *held))
        ahead = came[0]
        if k < far:
            behind = came[1]
            pieces.append(behind)
            steps.append(k)
        pieces.append(ahead)
        steps.append(-k)
    return pieces, steps


def reduce_ring(at, parts):
    size = at.wide

    def chunk(k):
        member = at.member(k)
        cut = [lax.dynamic_index_in_dim(p, member, 0, keepdims=False) for p in parts]
        return row_major(jnp.concatenate(cut, axis=1) if len(cut) > 1 else cut[0])

    far = size // 2
    ahead, behind = chunk(far), chunk(1 - far)
    yield ahead, behind
    for k in range(far - 1, 0, -1):
        ahead, behind = at.ring(ahead, 0), at.ring(behind, 1)
        held = yield ahead, behind
        ahead, behind, *_ = lax.optimization_barrier((ahead, behind, *(held or ())))
        ahead = row_major(add_low(ahead, chunk(k)))
        if k > 1:
            behind = row_major(add_low(behind, chunk(1 - k)))
        yield ahead, behind
    ahead = at.ring(ahead, 0)
    held = yield (ahead,)
    ahead, *_ = lax.optimization_barrier((ahead, *(held or ())))
    yield row_major(add_low(chunk(0), ahead, behind))


def scatter(at, parts):
    return jnp.concatenate(
        [lax.psum_scatter(p, "wide", scatter_dimension=0, tiled=True)[0] for p in parts], axis=1
    )


def local(
    tokens,
    lengths,
    buckets,
    ln1_gain,
    ln1_bias,
    w_qkv,
    rel_table,
    w_out,
    ln2_gain,
    ln2_bias,
    w_up,
    w_down,
    cotangent,
):
    at = Places()
    wide = at.wide
    slot, model = tokens.shape
    backwards = buckets.reshape(-1, TILE)[:, ::-1].reshape(slot)
    rows = w_qkv.shape[0]
    ff = w_up.shape[1]
    ff_rows = w_down.shape[0]
    quarter = ff_rows // 4
    heads = HEADS // 4
    width = 3 * model // 4
    rel_rows = rel_table.shape[0]
    n = at.n.reshape(1)
    far = wide // 2

    cut = slot // 16 * 7
    tokens_far = [at.swap(tokens[:cut], 2), at.swap(tokens[cut:], 2)]
    tokens_all = [[tokens], [at.swap(tokens, 1)], tokens_far, [at.swap(t, 1) for t in tokens_far]]

    lengths_far = at.swap(after(lengths, tokens_far[0]), 2)
    lengths_all = [lengths, at.swap(lengths, 1), lengths_far, at.swap(lengths_far, 1)]

    vectors = [ln1_gain, ln1_bias, ln2_gain, ln2_bias, rel_table]
    vectors = jnp.stack([jnp.pad(s, (0, TILE - s.shape[0])) for s in vectors])
    vectors = jnp.pad(vectors, ((0, 16 - vectors.shape[0]), (0, 0)))
    if at.rings:
        attn_piece = cut_attn(n, w_qkv, w_out, vectors)
        ffn_piece = cut_ffn(n, after(w_up, attn_piece), w_down)
        came, xhats = [], []

        def hold(x, *deps):
            xhats.append(xhat_of([after(t, *deps) for t in x]))
            return xhats[-1]

        pieces, steps = gather_ring(
            at,
            attn_piece,
            {
                1: lambda *x: [ffn_piece, tokens_far[0]],
                2: lambda *x: [
                    lengths_far,
                    tokens_far[1],
                    hold(tokens_all[0], *x),
                    hold(tokens_all[1], *x),
                ],
                3: lambda *x: came.extend(x) or lengths_all[1::2],
            },
        )
        hold(tokens_all[2], *came)
        hold(tokens_all[3], *came)
        ffn_piece = after(ffn_piece, *came)
        where = jnp.stack([at.member(k) for k in steps])
        small = small_rows(where, pieces, model)
    else:
        pick = lambda x, axis: lax.dynamic_index_in_dim(x, at.n, axis, keepdims=False)
        cut = pick(w_qkv.reshape(rows, 3, 4, heads // 2, PAIR), 2)
        cut = cut.transpose(0, 2, 1, 3).reshape(rows, width)
        cut = [cut, pick(w_out.reshape(rows, 4, model // 4), 1), jnp.zeros((rows, TILE), bf16)]
        attn_piece = jnp.concatenate(cut, axis=1)
        ffn_piece = jnp.stack(
            [
                pick(w_up.reshape(rows, wide, 4, quarter), 2).reshape(rows, wide * quarter),
                pick(w_down.reshape(4, quarter, model), 0),
            ]
        )
        pieces = [lax.all_gather(attn_piece, "wide", axis=0, tiled=True)]
        where = jnp.zeros((1,), jnp.int32)
        small = lax.all_gather(vectors, "wide", axis=0).astype(f32)
        small = [small[:, i, :rows].reshape(1, model) for i in range(4)] + [
            jnp.pad(small[:, 4, :rel_rows].reshape(1, -1), ((0, 0), (0, model - HEADS * BUCKETS)))
        ]
        small = jnp.pad(jnp.concatenate(small, axis=0), ((0, 3), (0, 0)))
    w_ffn = lax.all_gather(ffn_piece, "wide", axis=0)

    if not at.rings:
        xhats = [xhat_of(t) for t in tokens_all]
    valid = (jnp.arange(slot, dtype=jnp.int32) < lengths[0]).astype(f32)[:, None]
    cotan = cotangent.astype(f32)
    grad_ffn = at.all_narrow(after((valid * cotan).astype(bf16), *tokens_far))
    half = slot // 2
    norm_one, packed, wqkv, wout = qkv_of(where, small, xhats, pieces, width)
    wout_far = at.swap(wout, 2)
    tiles = bias_tiles(n, small, buckets, heads)
    atts, probs = [None] * 4, [None] * 4
    for r in (3, 2, 1, 0):
        length = {1: [grad_ffn[2]], 0: [grad_ffn[1]]}.get(r, [])
        length = after(lengths_all[r], *length) if length else lengths_all[r]
        atts[r], probs[r] = attn_fwd(length, packed, tiles, r)
    wouts = [wout, at.swap(wout, 1), wout_far, at.swap(after(wout_far, atts[1]), 1)]
    attended = [atts[0]] + [at.swap(atts[r], r) for r in (1, 2, 3)]
    whole, norm_two, norm_far = [], [], []
    for i in range(2):
        *whole, norm = out_ln2(n, lengths, tokens, small, attended, wouts, i, whole)
        norm_two.append(norm)
        norm_far.append(at.swap(norm, 2))
    middle, attended = whole

    norm_near = norm_two + [at.swap(x, 1) for x in norm_two]
    o0, o1, gn0, gn1, rows_all = ffn(
        norm_near, grad_ffn[:2], [(0, slot)] * 2, w_ffn, 0, [], 4
    )
    gn_near = [at.swap(x, 1) for x in gn1]

    def chip_sum(p2, p3):
        return add_low(p2, jnp.concatenate([at.swap(x, 1) for x in p3], axis=0))

    cuts = 4
    gn_far, o_far, gn_back = [], [], []
    for i in range(2):
        norms = after(norm_far[i], gn2 if i else gn0)
        cut = half // cuts
        norms = [norms] + [at.swap(norms[j : j + cut], 1) for j in range(0, half, cut)]
        norms[0] = after(norms[0], *gn_far)
        o2, o3, gn2, gn3, rows_all = ffn(
            norms, grad_ffn[2:], [(i * half, half)] * 2, w_ffn, 2 * slot + i * slot, rows_all, cuts
        )
        gn_far.append(chip_sum(gn2, gn3))
        o_far.append((o2, o3))
        gn_back.append(at.swap(gn_far[i], 2))
    norms, grads, hid, gua = rows_all
    gu = dot(norms, after(gua, gn_back[0], *gn_far), TN).astype(bf16)
    gd = dot(hid, after(grads, gn_back[0], *gn_far), TN).astype(bf16)
    shape = (wide, rows, model)
    if at.rings:
        turns = reduce_ring(at, [gu.reshape(shape), gd.reshape(shape)])
        next(turns)

    whole, grad_two = [], []
    for i in range(2):
        near = gn_near[2 * i : 2 * i + 2]
        *whole, vec = ln2_back(
            n, lengths, middle, cotangent, small, gn0, near, gn_back[i], wouts, i, whole
        )
        grad_two.append(vec)
    grad_middle, branch_keep, branch_send, *grad_att = whole
    if at.rings:
        next(turns)
        grad_att[0] = after(grad_att[0], *next(turns))
    grad_att = [grad_att[0]] + [at.swap(grad_att[r], r) for r in (1, 2, 3)]
    grad_packed, dists = None, []

    def backward(r, *deps):
        ga = after(grad_att[r], *deps) if deps else grad_att[r]
        return attn_bwd(packed, ga, atts[r], probs[r], r, grad_packed)

    def turned():
        return list(next(turns)) if at.rings else []

    def turn_after(*deps):
        if at.rings:
            turns.send(list(deps))

    grad_packed, dist = backward(0)
    dists.append(dist)
    attended = after(attended, dist, *grad_att[2:])
    out_send = dot(attended, branch_send, TN).astype(bf16)
    out_keep = dot(attended, branch_keep, TN).astype(bf16)
    o_far = [chip_sum(after(x, dist), [after(y, dist)]) for x, y in o_far]
    out_back = [at.swap(o_far[0], 2)]
    grad_packed, dist = backward(2, out_send, out_keep, *turned())
    turn_after(grad_att[2])
    dists.append(dist)
    out_sum = add_low(out_keep, at.swap(out_send, 1))
    grad_packed, dist = backward(3, out_sum)
    dists.append(dist)
    p2, p3, more_one = ln1_back(after(grad_packed, out_back[0], *turned()), wqkv, xhats[2:], 2)
    turn_after(p3)
    p_far = chip_sum(p2, [p3])
    p_back = [at.swap(p_far[:half], 2)]
    grad_packed, dist = backward(1, p_far)
    dists.append(dist)
    grad_qkv = dot(norm_one, grad_packed, TN).astype(bf16)
    parts = [grad_qkv.reshape(wide, rows, width), out_sum.reshape(wide, rows, model // 2)]
    if at.rings:
        next(turns)
        ffn_own = turns.send([dist])
        turns = reduce_ring(at, parts)
        grad_packed = after(grad_packed, p_back[0], *next(turns))
    else:
        ffn_own = scatter(at, [gu.reshape(shape), gd.reshape(shape)])
        attn_own = scatter(at, parts)
    ffn_all = at.all_narrow(after(ffn_own, p_back[0]))
    p_back.append(at.swap(after(p_far[half:], ffn_all[2]), 2))
    out_back.append(at.swap(after(o_far[1], p_back[1]), 2))

    p0, p1, grad_one = ln1_back(grad_packed, wqkv, xhats[:2], 0)
    grad_one = [grad_one, more_one]
    p_near = at.swap(p1, 1)
    if at.rings:
        keep, send = pack_small(n, at.y.reshape(1), grad_one, grad_two, backwards, dists, heads)
        next(turns)
        sent = turns.send([p1, keep, ffn_all[2]])
        smalls = keep + at.swap_y(after(send, *sent))
        next(turns)
        sent = turns.send([p_back[1], smalls])
        p0 = after(p0, *sent)
    grad_tokens = ln1_last(tokens, xhats[0], grad_middle, small, p0, p_near, *p_back)

    outs = [o0, at.swap(o1, 1), jnp.concatenate(out_back, axis=0)]
    if at.rings:
        next(turns)
        sent = turns.send([grad_tokens])
        smalls, outs[0] = after(smalls, *sent), after(o0, *sent)
        pick = lambda i: lax.dynamic_index_in_dim(smalls, i, 0, keepdims=False)
        z_parts = [pick(at.z)] + [
            at.along_z(pick(lax.rem(at.z + k, far)), k) for k in range(1, far)
        ]
    output = (middle + valid * sum(p.astype(f32) for p in outs)).astype(bf16)
    if at.rings:
        next(turns)
        attn_own = turns.send([output, *z_parts[1:]])
        smalls = after(z_parts[0], attn_own) + sum(z_parts[1:])

    if not at.rings:
        onehot = (backwards[:, None] == jnp.arange(BUCKETS, dtype=jnp.int32)[None, :]).astype(f32)
        table = jnp.dot(sum(dists).reshape(heads, slot), onehot, precision=lax.Precision.HIGHEST)
        table = lax.dynamic_update_slice(
            jnp.zeros((4, heads * BUCKETS), f32), table.reshape(1, -1), (at.n, 0)
        )
        two = grad_two[0] + grad_two[1]
        one = grad_one[0] + grad_one[1]
        smalls = [one[0], one[1], two[0], two[1], table]
        smalls = [g.reshape(wide, 1, -1) for g in smalls]
        smalls = [jnp.pad(g, ((0, 0), (0, 0), (0, TILE - g.shape[2]))) for g in smalls]
        smalls = jnp.concatenate(smalls + [jnp.zeros((wide, 3, TILE), f32)], axis=1)
        smalls = lax.psum_scatter(smalls, "wide", scatter_dimension=0, tiled=True)[0]
    ffn_all[0] = after(ffn_all[0], attn_own)
    up_full, down_full = join_ffn(n, ffn_all, quarter)
    smalls = smalls + after(at.swap(smalls, 2), up_full)
    smalls = smalls + at.swap(smalls, 1)

    qkv_full, out_full = join_attn(n, at.all_narrow(attn_own), model)

    return (
        output,
        grad_tokens,
        smalls[0, :rows],
        smalls[1, :rows],
        qkv_full,
        smalls[4, :rel_rows],
        out_full,
        smalls[2, :rows],
        smalls[3, :rows],
        up_full,
        down_full,
    )


def solution(mesh):
    return jax.shard_map(
        local,
        mesh=mesh,
        in_specs=(
            P(("narrow", "wide"), None),
            P(("narrow", "wide")),
            P(),
            P("wide"),
            P("wide"),
            P("wide", None),
            P("wide"),
            P("wide", None),
            P("wide"),
            P("wide"),
            P("wide", None),
            P("wide", None),
            P(("narrow", "wide"), None),
        ),
        out_specs=(
            P(("narrow", "wide"), None),
            P(("narrow", "wide"), None),
            P("wide"),
            P("wide"),
            P("wide", None),
            P("wide"),
            P("wide", None),
            P("wide"),
            P("wide"),
            P("wide", None),
            P("wide", None),
        ),
        check_vma=False,
    )
```
